32 devices in a mesh: chan: 4 (over x, core), space: 8 (over z, y).
Axes of the slice: x: 2, y: 2, z: 4, core: 2. Of those that a mesh axis runs over, the one named last changes fastest.
Arguments:
- velocity: float32 [2, 4, 256, 256], P(None, None, 'space'), may hold values from -6 to 6
- w_first: bfloat16 [3, 3, 2, 64], P(None, None, None, 'chan'), may hold values from -2 to 2
- b_first: bfloat16 [64], P('chan'), may hold values from -3 to 3
- w_mid: bfloat16 [5, 3, 3, 64, 64], P(None, None, None, None, 'chan'), may hold values from -0.375 to 0.375
- b_mid: bfloat16 [5, 64], P(None, 'chan'), may hold values from -3 to 3
- w_last: bfloat16 [3, 3, 64, 32], P(None, None, None, 'chan'), may hold values from -0.1875 to 0.1875
- b_last: bfloat16 [32], P('chan'), may hold values from -3 to 3
- offsets: int32 [2, 16], replicated, may hold values from 0 to 15, each once within a row
- cotangent: float32 [2, 4, 256, 256], P(None, None, 'space'), may hold values from -6 to 6
Outputs:
- new_velocity: float32 [2, 4, 256, 256], P(None, None, 'space')
- velocity_grad: float32 [2, 4, 256, 256], P(None, 'chan', 'space')
- w_first_grad: float32 [3, 3, 2, 64], P(None, None, None, 'chan')
- b_first_grad: float32 [64], P('chan')
- w_mid_grad: float32 [5, 3, 3, 64, 64], P(None, None, None, None, 'chan')
- b_mid_grad: float32 [5, 64], P(None, 'chan')
- w_last_grad: float32 [3, 3, 64, 32], P(None, None, None, 'chan')
- b_last_grad: float32 [32], P('chan')
- rms_stats: float32 [4], replicated
The draws below stay inside these ranges and needn't reach their ends.
Inputs may be any that keep to these rules, and one draw needn't show every extreme that they name: `offsets`: each row names every stencil point 0 to 15 once.
All inputs are finite; a program needn't handle non-finite values.
Results may differ from the reference program's by a relative error of at most 0.015.
The reference program's roundings to bfloat16 on the way count: a program that leaves them out, or rounds other values in their place, can miss the bound.
Values may be sent and summed in bfloat16 or wider, within the bound.
No kernel may reach another device: no remote copies, remote signals or barrier semaphores. Data moves between devices by JAX's collectives and lax.ppermute only.
A program may use at most 704 MiB of HBM per device.

```python
import jax
import jax.numpy as jnp
from jax import lax

C = 64
S = 16
MIDDLE = 5
NX = 256
NY = 256
TRAJ = 4


def draw_velocity(key, part):
    key = jax.random.fold_in(key, 11)
    extent_all = (2, TRAJ, NY, NX)
    row_index = jnp.arange(NY, dtype=jnp.float32)[None, None, :, None]
    rising = 1.0 + 2.0 * row_index / (NY - 1)
    random_part = jnp.clip(jax.random.normal(key, extent_all, jnp.float32), -3.5, 3.5) * 0.5
    return (random_part * rising).astype(jnp.float32)


def block_scale(own_key, dims, cuts, low, high):
    def one(dim, shards_of):
        heights = jax.random.uniform(jax.random.fold_in(jax.random.fold_in(own_key, 6), dim), (shards_of,), jnp.float32, low / len(cuts), high / len(cuts))
        return jnp.repeat(jnp.exp(heights), dims[dim] // shards_of).reshape((-1,) + (1,) * (len(dims) - dim - 1))

    loudness = one(*cuts[0])
    for cut in cuts[1:]:
        loudness = loudness * one(*cut)
    return loudness


def noise(stream_key, extent, spread, reach, cuts=(), held_as=jnp.bfloat16):
    drawn = jax.random.normal(stream_key, extent, jnp.float32) * spread
    if len(cuts) > 0:
        drawn = block_scale(stream_key, extent, cuts, -0.22, 0.18) * drawn
    return jnp.clip(drawn, min=-reach, max=reach).astype(held_as)


def setup_inputs(seed: int = 0) -> dict:
    arg_keys = jax.random.split(jax.random.key(seed), 10)
    velocity = draw_velocity(jax.random.fold_in(arg_keys[9], 71), 0)
    w_first = noise(arg_keys[1], (3, 3, 2, C), 9 ** -0.5, 2.0, ((3, 4),))
    b_first = noise(arg_keys[2], (C,), 0.5, 3.0, ((0, 4),))
    w_mid = noise(arg_keys[3], (MIDDLE, 3, 3, C, C), (4 * C) ** -0.5, 0.375, ((4, 4),))
    b_mid = noise(arg_keys[4], (MIDDLE, C), 0.5, 3.0, ((1, 4),))
    w_last = noise(arg_keys[5], (3, 3, C, 2 * S), (16 * C) ** -0.5, 0.1875, ((3, 4),))
    b_last = noise(arg_keys[6], (2 * S,), 0.5, 3.0, ((0, 4),))
    offsets = jax.vmap(lambda own: jax.random.permutation(own, S))(jax.random.split(arg_keys[7], 2)).reshape((2, S)).astype(jnp.int32)
    cotangent = noise(arg_keys[8], (2, TRAJ, NY, NX), 1.0, 6.0, ((2, 8),), jnp.float32)
    return dict(velocity=velocity, w_first=w_first, b_first=b_first, w_mid=w_mid, b_mid=b_mid, w_last=w_last, b_last=b_last, offsets=offsets, cotangent=cotangent)


@jax.custom_vjp
def low(v):
    return lax.optimization_barrier(v.astype(jnp.bfloat16)).astype(jnp.float32)

@jax.custom_vjp
def low_back(v):
    return v

def low_keep(v):
    return (low(v), None)

def low_pass(kept, grad):
    return (grad,)

def back_keep(v):
    return (v, None)

def back_low(kept, grad):
    return (low(grad),)
low.defvjp(low_keep, low_pass)
low_back.defvjp(back_keep, back_low)
highest = lax.Precision.HIGHEST
time_step = 0.2
viscosity = 0.256

def convolve(activation, weight):
    summed = jnp.zeros((weight.shape[3],) + activation.shape[1:], jnp.float32)
    for row_tap in range(3):
        for col_tap in range(3):
            shifted = jnp.roll(activation, (1 - row_tap, 1 - col_tap), axis=(1, 2))
            summed = summed + jnp.einsum('co,cyx->oyx', weight[row_tap, col_tap], shifted, precision=highest)
    return summed

def stencil_faces(trajectory, stencil, offsets):
    points = offsets.shape[1]
    onehot = (offsets[:, :, None] == jnp.arange(points, dtype=jnp.int32)[None, None, :]).astype(jnp.float32)
    second = jnp.array([[6], [9]], dtype=jnp.int32)
    base_weight = 0.5 * ((offsets == 5).astype(jnp.float32) + (offsets == second).astype(jnp.float32))
    grouped = stencil.reshape((2, points) + stencil.shape[1:])
    stencil_mix = grouped - lax.optimization_barrier(jnp.mean(grouped, axis=1, keepdims=True)) + base_weight[:, :, None, None]
    by_point = jnp.einsum('ckp,ckyx->cpyx', onehot, stencil_mix, precision=highest)
    components = []
    for component in range(2):
        summed = jnp.zeros_like(trajectory[component])
        for stencil_point in range(points):
            row_shift = stencil_point // 4 - 1
            col_shift = stencil_point % 4 - 1
            shifted = jnp.roll(trajectory[component], (-row_shift, -col_shift), axis=(0, 1))
            summed = summed + by_point[component, stencil_point] * shifted
        components.append(summed)
    return jnp.stack(components)

def solver_update(trajectory, face_vals):
    east_col = jnp.roll(trajectory, -1, axis=2)
    west_col = jnp.roll(trajectory, 1, axis=2)
    north_row = jnp.roll(trajectory, -1, axis=1)
    south_row = jnp.roll(trajectory, 1, axis=1)
    laplace = east_col + west_col + north_row + south_row - 4.0 * trajectory
    flux_east = face_vals[0][None] * (trajectory + east_col) * 0.5
    flux_north = face_vals[1][None] * (trajectory + north_row) * 0.5
    advect = flux_east - jnp.roll(flux_east, 1, axis=2) + flux_north - jnp.roll(flux_north, 1, axis=1)
    return trajectory + time_step * (viscosity * laplace - advect)

def projection(field_vals):
    extent_y = field_vals.shape[1]
    extent_x = field_vals.shape[2]
    wave_x = 2.0 * jnp.pi * jnp.fft.fftfreq(extent_x)[None, :]
    wave_y = 2.0 * jnp.pi * jnp.fft.fftfreq(extent_y)[:, None]
    wave_sq = wave_x * wave_x + wave_y * wave_y
    reciprocal = jnp.where(wave_sq > 0, 1.0 / jnp.where(wave_sq > 0, wave_sq, 1.0), 0.0)
    spectra = jnp.fft.fft2(field_vals)
    divergence = (wave_x * spectra[0] + wave_y * spectra[1]) * reciprocal
    projected = jnp.stack([spectra[0] - wave_x * divergence, spectra[1] - wave_y * divergence])
    return jnp.real(jnp.fft.ifft2(projected))

def forward(velocity, w_first, b_first, w_mid, b_mid, w_last, b_last, offsets):

    def single(trajectory):
        activation = low(trajectory)
        preact = low_back(convolve(activation, w_first) + b_first[:, None, None])
        for depth_index in range(w_mid.shape[0]):
            activation = low(jax.nn.gelu(preact))
            preact = low_back(convolve(activation, w_mid[depth_index]) + b_mid[depth_index][:, None, None])
        activation = low(jax.nn.gelu(preact))
        stencil = low_back(convolve(activation, w_last) + b_last[:, None, None])
        face_vals = stencil_faces(trajectory, stencil, offsets)
        provisional = solver_update(trajectory, face_vals)
        change = provisional - trajectory
        return (projection(provisional), jnp.sum(face_vals * face_vals), jnp.sum(change * change))
    results = lax.map(jax.checkpoint(single), jnp.moveaxis(velocity, 1, 0))
    return (jnp.moveaxis(results[0], 0, 1), results[1], results[2])

def reference(velocity, w_first, b_first, w_mid, b_mid, w_last, b_last, offsets, cotangent):

    def wrapped(vel_arg, wf_arg, bf_arg, wm_arg, bm_arg, wl_arg, bl_arg):
        return forward(vel_arg, wf_arg, bf_arg, wm_arg, bm_arg, wl_arg, bl_arg, offsets)
    primal, pull = jax.vjp(wrapped, velocity, w_first.astype(jnp.float32), b_first.astype(jnp.float32), w_mid.astype(jnp.float32), b_mid.astype(jnp.float32), w_last.astype(jnp.float32), b_last.astype(jnp.float32))
    new_velocity, face_sq, update_sq = primal
    grads = pull((cotangent, jnp.zeros_like(face_sq), jnp.zeros_like(update_sq)))
    cell_count = velocity.size
    rms_stats = jnp.sqrt(jnp.stack([jnp.mean(velocity * velocity), jnp.sum(face_sq) / cell_count, jnp.sum(update_sq) / cell_count, jnp.mean(new_velocity * new_velocity)]))
    return (new_velocity, grads[0], grads[1], grads[2], grads[3], grads[4], grads[5], grads[6], rms_stats)
```

```python
import functools

import jax
import jax.numpy as jnp
import numpy as np
from jax import lax
from jax.experimental import pallas as pl
from jax.experimental.pallas import tpu as pltpu
from jax.sharding import PartitionSpec as P

f32 = jnp.float32
bf16 = jnp.bfloat16
highest = lax.Precision.HIGHEST
time_step = 0.2
viscosity = 0.256
HALO = 16
DEEP = 12
GPH = 8
C = 64
NL = 5
KW = 256
MIDROWS = NL * 3 * 16
A0 = 0.7978845608028654
A1 = 0.044715 * A0


def basis(length):
    half = length // 2
    pos = np.arange(length)[:, None]
    table = np.zeros((length, length))
    m = np.arange(half + 1)[None, :]
    table[:, : half + 1] = np.cos(2 * np.pi * ((pos * m) % length) / length) * np.sqrt(2.0 / length)
    table[:, 0] = np.sqrt(1.0 / length)
    table[:, half] = np.cos(np.pi * pos[:, 0]) * np.sqrt(1.0 / length)
    m = np.arange(1, half)[None, :]
    table[:, half + 1 :] = np.sin(2 * np.pi * ((pos * m) % length) / length) * np.sqrt(2.0 / length)
    return table


def multipliers(ny, nx):
    def modes(n):
        half = n // 2
        index = np.arange(n)
        wave = np.where(index <= half, index, index - half) * (2 * np.pi / n)
        return wave, index <= half

    ky, cy = modes(ny)
    kx, cx = modes(nx)
    ky, cy = ky[:, None], cy[:, None]
    kx, cx = kx[None, :], cx[None, :]
    sq = kx * kx + ky * ky
    inv = np.where(sq > 0, 1.0 / np.where(sq > 0, sq, 1.0), 0.0)
    sign = np.where(cx == cy, 1.0, -1.0)
    edge_x = (kx == 0) | (kx >= np.pi - 1e-9)
    edge_y = (ky == 0) | (ky >= np.pi - 1e-9)
    mxy = np.where(edge_x | edge_y, 0.0, sign * kx * ky * inv)
    mxx = 1.0 - kx * kx * inv
    myy = 1.0 - ky * ky * inv
    return mxx, myy, mxy


def split(table):
    high = table.astype(np.float32)
    return jnp.asarray(high)


def project_spectral(u, v, mxx, myy, mxy):
    half_y, half_x = u.shape[0] // 2, u.shape[1] // 2

    def swap(a):
        a = jnp.concatenate([a[:, half_x:], a[:, :half_x]], axis=1)
        return jnp.concatenate([a[half_y:], a[:half_y]], axis=0)

    rows = lax.broadcasted_iota(jnp.int32, u.shape, 0)
    cols = lax.broadcasted_iota(jnp.int32, u.shape, 1)
    corner = jnp.where((rows == half_y) & (cols == half_x), -0.5, 0.0)
    return (
        mxx * u + mxy * swap(v) + corner * v,
        myy * v + mxy * swap(u) + corner * u,
    )


def dot3(a, b):
    return jnp.dot(a, b, preferred_element_type=f32, precision=highest)


def gelu_both(z):
    z2 = z * z
    t = jnp.tanh(z * (A0 + A1 * z2))
    h = 0.5 * t + 0.5
    a = z * h
    return a, h + a * (1.0 - h) * (2.0 * A0 + 6.0 * A1 * z2)


def lroll(x, s):
    return pltpu.roll(x, s % x.shape[1], 1)


def shifts(x):
    return jnp.concatenate([lroll(x, 1), x, lroll(x, -1)], axis=0)


def unshifts(x):
    return jnp.concatenate([lroll(x, -1), x, lroll(x, 1)], axis=0)


def spread(ref, first, values):
    for k in range(ref.shape[0]):
        ref[k, pl.ds(first, values.shape[0], stride=8), :] = values[:, k * 128 : k * 128 + 128]


def collect(ref, first, count):
    planes = [ref[k, pl.ds(first, count, stride=8), :] for k in range(ref.shape[0])]
    return jnp.concatenate(planes, axis=1)


def rows_of(ref, first, count):
    at = pl.ds(first if isinstance(first, int) else pl.multiple_of(first, 8), count)
    return jnp.concatenate([ref[k, at, :] for k in range(ref.shape[0])], axis=1)


def put_rows(ref, first, values):
    at = pl.ds(
        first if isinstance(first, int) else pl.multiple_of(first, 8), values.shape[0]
    )
    for k in range(ref.shape[0]):
        ref[k, at, :] = values[:, k * 128 : k * 128 + 128]


def group4(s):
    i = lax.broadcasted_iota(jnp.int32, s.shape, 0)
    s = s + jnp.where(i % 2 == 0, pltpu.roll(s, 7, 0), pltpu.roll(s, 1, 0))
    return s + jnp.where((i // 2) % 2 == 0, pltpu.roll(s, 6, 0), pltpu.roll(s, 2, 0))


def point_order(offs):
    row = lax.broadcasted_iota(jnp.int32, (32, 16), 0)
    point = (row // 8) * 4 + row % 4
    comp = (row // 4) % 2
    parts = [
        jnp.where((comp == c) & (offs[c : c + 1, :] == point), 1.0, 0.0).astype(f32)
        for c in range(2)
    ]
    return jnp.concatenate(parts, axis=1)


def blocks(n, most=17):
    count = -(-n // most)
    return count, -(-n // count)


def forward_kernel(
    h, me_ref, vel_ref, up_ref, down_ref, w0, w1, w2, w3, offs_ref,
    prov_ref, vp_ref, vs_ref, face_ref, mix_ref, x_out, g_out, wk_ref, w7_ref, wf_ref, perm_ref, sq_ref,
    xb, gb, w7k, f8, xsem, gsem,
):
    rows = h + 2 * HALO
    me = me_ref[0]
    for k, piece in enumerate((w0, w1, w2, w3)):
        slot = jnp.bitwise_xor(me, k)
        at16 = pl.ds(pl.multiple_of(slot * 16, 16), 16)
        at8 = pl.ds(pl.multiple_of(slot * 8, 8), 8)
        for n in range(NL * 3):
            wk_ref[n, at16, :] = piece[n * 16 : n * 16 + 16]
        for j in range(3):
            block = piece[MIDROWS + j * 16 : MIDROWS + j * 16 + 16].astype(f32)
            w7k[j, at8, :] = block[0:8]
        wf_ref[at16, :] = piece[MIDROWS + 48 : MIDROWS + 64]
    perm = point_order(offs_ref[...])
    perm_ref[...] = perm
    perm_low = perm.astype(bf16)
    for i in range(3):
        w7_ref[i] = jnp.dot(perm_low, w7k[i].astype(bf16), preferred_element_type=f32).astype(bf16)

    vp_ref[:, 0:HALO] = up_ref[...]
    vp_ref[:, HALO : HALO + h] = vel_ref[...]
    vp_ref[:, HALO + h :] = down_ref[...]
    for c in range(2):
        plane = vp_ref[c]
        for d in range(4):
            spread(vs_ref, c * 4 + d, lroll(plane, 1 - d))

    def vs_rows(y, n):
        return rows_of(vs_ref, (y + HALO) * 8, 8 * n)

    def copies(l):
        return (
            pltpu.make_async_copy(xb.at[l, pl.ds(DEEP - 1, h + 2)], x_out.at[l], xsem.at[l]),
            pltpu.make_async_copy(
                gb.at[l, pl.ds(DEEP - l - 1, h + 2 * (l + 1))],
                g_out.at[l, pl.ds(0, h + 2 * (l + 1))],
                gsem.at[l],
            ),
        )

    wfirst = wf_ref[:, 0:24]
    bias = jnp.broadcast_to(wf_ref[:, 24:25].astype(f32), (C, KW))
    n = h + 2 * (DEEP - 1)
    count, size = blocks(n)

    def first_block(k, _):
        top = jnp.minimum(k * size, n - size) - (DEEP - 1)
        for r in range(size):
            y = top + r
            x = vs_rows(y - 1, 3).astype(bf16)
            z = jnp.dot(wfirst, x, preferred_element_type=f32)
            a, d = gelu_both(z + bias)
            xb[0, y + DEEP] = a.astype(bf16)
            gb[0, y + DEEP] = d.astype(bf16)
        return 0

    lax.fori_loop(0, count, first_block, 0)
    for copy in copies(0):
        copy.start()

    for l in range(1, NL + 1):
        weight = wk_ref[3 * (l - 1) : 3 * l].reshape(192, KW)
        bias = jnp.broadcast_to(weight[0:C, 192:193].astype(f32), (C, KW))
        weight = weight[:, 0:192]
        n = h + 2 * (DEEP - 1 - l)
        count, size = blocks(n)

        def block(k, _, l=l, weight=weight, bias=bias, n=n, size=size):
            top = jnp.minimum(k * size, n - size) - (DEEP - 1 - l) + DEEP
            p0 = p1 = None
            for r in range(-1, size + 1):
                o = jnp.dot(weight, shifts(xb[l - 1, top + r]), preferred_element_type=f32)
                if r >= 1:
                    a, d = gelu_both(p1 + o[128:192] + bias)
                    xb[l, top + r - 1] = a.astype(bf16)
                    gb[l, top + r - 1] = d.astype(bf16)
                p1 = o[64:128] if p0 is None else p0 + o[64:128]
                p0 = o[0:64]
            return 0

        lax.fori_loop(0, count, block, 0)
        for copy in copies(l):
            copy.start()

    weight = w7_ref[...].reshape(96, KW)
    bias = jnp.broadcast_to(weight[0:32, 192:193].astype(f32), (32, KW))
    weight = weight[:, 0:192]
    row = lax.broadcasted_iota(jnp.int32, (32, KW), 0)
    point = (row // 8) * 4 + row % 4
    second = jnp.where((row // 4) % 2 == 0, 6, 9)
    base = jnp.where((point == 5) | (point == second), 0.5, 0.0).astype(f32)
    n = h + 4
    count, size = blocks(n, 12)

    def last_block(k, _):
        top = jnp.minimum(k * size, n - size) - 2
        p0 = p1 = None
        for r in range(-1, size + 1):
            o = jnp.dot(weight, shifts(xb[NL, top + r + DEEP]), preferred_element_type=f32)
            if r >= 1:
                y = top + r - 1
                s = p1 + o[64:96] + bias
                mean = group4(s[0:8] + s[8:16] + s[16:24] + s[24:32]) * (1.0 / 16.0)
                mix = s - jnp.concatenate([mean] * 4, axis=0) + base
                mix_ref[pl.ds(pl.multiple_of((y + 2) * 32, 32), 32), :] = mix
                m = mix * vs_rows(y - 1, 4)
                m = group4(m[0:8] + m[8:16] + m[16:24] + m[24:32])
                put_rows(f8, (y + 2) * 8, m)
            p1 = o[32:64] if p0 is None else p0 + o[32:64]
            p0 = o[0:32]
        return 0

    lax.fori_loop(0, count, last_block, 0)
    for c in range(2):
        face_ref[c] = collect(f8, c * 4, h + 4)
    ue = face_ref[0, 2 : 2 + h]
    vn = face_ref[1, 2 : 2 + h]
    vn_south = face_ref[1, 1 : 1 + h]
    total = [jnp.sum(ue * ue) + jnp.sum(vn * vn)]
    own = update = 0.0
    for c in range(2):
        q = vp_ref[c, HALO : HALO + h]
        north = vp_ref[c, HALO + 1 : HALO + 1 + h]
        south = vp_ref[c, HALO - 1 : HALO - 1 + h]
        east, west = lroll(q, -1), lroll(q, 1)
        lap = east + west + north + south - 4.0 * q
        fx = ue * (q + east) * 0.5
        adv = fx - lroll(fx, 1) + vn * (q + north) * 0.5 - vn_south * (south + q) * 0.5
        new = q + time_step * (viscosity * lap - adv)
        prov_ref[c] = new
        own = own + jnp.sum(q * q)
        update = update + jnp.sum((new - q) * (new - q))
    lane = lax.broadcasted_iota(jnp.int32, (8, KW), 1)
    sq_ref[...] = jnp.where(
        lane == 0, own, jnp.where(lane == 1, total[0], jnp.where(lane == 2, update, 0.0))
    )
    for l in range(NL + 1):
        for copy in copies(l):
            copy.wait()


def backward_kernel(
    h, me_ref, cot_ref, t_ref, tt_ref, t2_ref, trow_ref, mxx_ref, myy_ref, mxy_ref,
    vp_ref, vs_ref, face_ref, mix_ref, x_in, g_in, wk_ref, w7_ref, wf_ref, perm_ref, sq_ref,
    vel_grad_ref, pack_ref,
    xb, gb, gz7, gz6, gz5, gz4, gz3, gz2, gz1, f8, adv_ref, acc_ref, gp_ref, near8, xsem, gsem,
):
    me_chan = me_ref[0]
    me_space = me_ref[1]

    def copies(l):
        return (
            pltpu.make_async_copy(x_in.at[l], xb.at[l], xsem.at[l]),
            pltpu.make_async_copy(
                g_in.at[l, pl.ds(0, h + 2 * (l + 1))],
                gb.at[l, pl.ds(0, h + 2 * (l + 1))],
                gsem.at[l],
            ),
        )

    for l in range(NL, -1, -1):
        for copy in copies(l):
            copy.start()

    n = h + 2 * GPH
    spectra = dot3(t2_ref[...], dot3(cot_ref[...], t_ref[...]))
    half = spectra.shape[0] // 2
    u, v = project_spectral(spectra[:half], spectra[half:], mxx_ref[...], myy_ref[...], mxy_ref[...])
    trow = trow_ref[me_space]
    gp_ref[0] = dot3(dot3(trow, u), tt_ref[...])
    gp_ref[1] = dot3(dot3(trow, v), tt_ref[...])

    m = n - 1
    fields = []
    gue = gvn = 0.0
    for c in range(2):
        g = -time_step * gp_ref[c, 0:m]
        g_north = -time_step * gp_ref[c, 1 : m + 1]
        q = vp_ref[c, HALO - GPH : HALO - GPH + m]
        q_north = vp_ref[c, HALO - GPH + 1 : HALO - GPH + 1 + m]
        gfx = g - lroll(g, -1)
        gfy = g - g_north
        gue = gue + gfx * (q + lroll(q, -1)) * 0.5
        gvn = gvn + gfy * (q + q_north) * 0.5
        adv_ref[c, 0:m] = gfy
        fields.append(gfx[GPH : GPH + h])
    for d in range(4):
        spread(f8, d, gue)
        spread(f8, 4 + d, gvn)
    ue = face_ref[0, 2 : 2 + h]
    vn = face_ref[1, 2 : 2 + h]
    vn_south = face_ref[1, 1 : 1 + h]
    for c in range(2):
        g = gp_ref[c, GPH : GPH + h]
        lap = (
            lroll(g, -1) + lroll(g, 1) + gp_ref[c, GPH + 1 : GPH + 1 + h]
            + gp_ref[c, GPH - 1 : GPH - 1 + h] - 4.0 * g
        )
        ex = fields[c] * ue
        ny = adv_ref[c, GPH : GPH + h] * vn
        sy = adv_ref[c, GPH - 1 : GPH - 1 + h] * vn_south
        vel_grad_ref[c] = g + time_step * viscosity * lap + 0.5 * (ex + lroll(ex, 1) + ny + sy)

    def f8_row(y):
        return rows_of(f8, (y + GPH) * 8, 8)

    def vs_rows(y, count):
        return rows_of(vs_ref, (y + HALO) * 8, 8 * count)

    def stencil_row(k, _):
        for r in range(2):
            y = 2 * k + r - 7
            face = f8_row(y)
            near = vs_rows(y - 1, 4)
            s = near[0:8] + near[8:16] + near[16:24] + near[24:32]
            mean = group4(s) * (1.0 / 16.0)
            gm = (near - jnp.concatenate([mean] * 4, axis=0)) * jnp.concatenate([face] * 4, axis=0)
            gz7[y + 7] = gm.astype(bf16)
        return 0

    lax.fori_loop(0, (h + 14) // 2, stencil_row, 0, unroll=4 if h >= 16 else 1)

    ones = jnp.ones((16, KW), bf16)

    def wgrad(columns, inputs):
        return lax.dot_general(
            jnp.concatenate(columns, axis=1),
            jnp.concatenate(inputs, axis=1),
            (((1,), (1,)), ((), ())),
            preferred_element_type=f32,
        )

    gzs = {7: gz7, 6: gz6, 5: gz5, 4: gz4, 3: gz3, 2: gz2, 1: gz1}
    for l in range(7, 1, -1):
        for copy in copies(l - 2):
            copy.wait()
        source, target = gzs[l], gzs[l - 1]
        xs, gs = xb.at[l - 2], gb.at[l - 2]
        if l == 7:
            parts = [w7_ref[i][:, 0:192].astype(f32) for i in range(3)]
            width = 32
        else:
            parts = [wk_ref[3 * (l - 2) + i][:, 0:192].astype(f32) for i in range(3)]
            width = C
        weight = jnp.concatenate(
            [
                jnp.concatenate([p[:, j * C : (j + 1) * C].T for j in range(3)], axis=1)
                for p in parts
            ],
            axis=0,
        ).astype(bf16)
        p0 = p1 = None
        acc = None
        for ys in (range(-l, h // 2), range(h // 2, h + l)):
            columns = {y: unshifts(source[y + l]) for y in ys}
            for y in ys:
                o = jnp.dot(weight, columns[y], preferred_element_type=f32)
                if y >= 2 - l:
                    ga = p1 + o[0:64]
                    target[y - 1 + l - 1] = (ga * gs[y - 1 + l - 1].astype(f32)).astype(bf16)
                p1 = o[64:128] if p0 is None else p0 + o[64:128]
                p0 = o[128:192]
            own = [y for y in ys if 0 <= y < h]
            part = wgrad(
                [columns[y] for y in own],
                [
                    jnp.concatenate([xs[y : y + 3].reshape(192, KW), ones], axis=0)
                    for y in own
                ],
            )
            acc = part if acc is None else acc + part
        if l == 7:
            back = perm_ref[...]
            acc = jnp.concatenate(
                [
                    lax.dot_general(
                        back, acc[j * 32 : j * 32 + 32], (((0,), (0,)), ((), ())),
                        preferred_element_type=f32, precision=highest,
                    )
                    for j in range(3)
                ],
                axis=0,
            )
        acc_ref[l - 1, 0 : 3 * width, 0:208] = acc

    wfirst = wf_ref[:, 0:32].astype(f32).T.astype(bf16)
    source = gz1
    outs = {}
    for y in range(-1, h + 1):
        outs[y] = jnp.dot(wfirst[0:24], source[y + 1], preferred_element_type=f32)
    acc_ref[0, 0:64, 0:40] = wgrad(
        [source[y + 1] for y in range(h)],
        [
            jnp.concatenate(
                [vs_rows(y - 1, 3), jnp.ones((16, KW), f32)], axis=0
            ).astype(bf16)
            for y in range(h)
        ],
    )
    for y in range(h):
        total = outs[y + 1][0:8] + outs[y][8:16] + outs[y - 1][16:24]
        for k in range(4):
            at = y + 1 - k
            total = total + f8_row(at) * mix_ref[pl.ds((at + 2) * 32 + k * 8, 8), :]
        put_rows(near8, y * 8, total)
    for c in range(2):
        total = vel_grad_ref[c]
        for d in range(4):
            total = total + lroll(collect(near8, c * 4 + d, h), d - 1)
        vel_grad_ref[c] = total

    for k, other in enumerate((0, 2, 1, 3)):
        slot = jnp.bitwise_xor(me_chan, other)
        for l in range(NL):
            for j in range(3):
                piece = acc_ref[l + 1, pl.ds(pl.multiple_of(j * 64 + slot * 16, 16), 16), :]
                pack_ref[k, (3 * l + j) * 16 : (3 * l + j) * 16 + 16, :] = piece.astype(bf16)
        last = [
            acc_ref[6, pl.ds(pl.multiple_of(j * 32 + slot * 8, 8), 8), :] for j in range(3)
        ]
        pack_ref[k, MIDROWS : MIDROWS + 32, :] = jnp.concatenate(
            last + [sq_ref[...]], axis=0
        ).astype(bf16)
        pack_ref[k, MIDROWS + 32 : MIDROWS + 48, :] = acc_ref[
            0, pl.ds(pl.multiple_of(slot * 16, 16), 16), :
        ].astype(bf16)


def project_kernel(h, me_ref, prov_ref, t_ref, tt_ref, t2_ref, trow_ref, mxx_ref, myy_ref, mxy_ref, out_ref, sq_ref):
    me_space = me_ref[1]
    trow = trow_ref[me_space][GPH : GPH + h]
    total = 0.0
    for t in range(prov_ref.shape[1]):
        field = prov_ref[:, t].reshape(-1, KW)
        spectra = dot3(t2_ref[...], dot3(field, t_ref[...]))
        half = spectra.shape[0] // 2
        u, v = project_spectral(
            spectra[:half], spectra[half:], mxx_ref[...], myy_ref[...], mxy_ref[...]
        )
        total = total + jnp.sum(u * u) + jnp.sum(v * v)
        out_ref[0, t] = dot3(dot3(trow, u), tt_ref[...])
        out_ref[1, t] = dot3(dot3(trow, v), tt_ref[...])
    sq_ref[...] = jnp.full((8, 128), total, f32)


def moved(x, axis, step):
    n = lax.axis_size(axis)
    return lax.ppermute(x, axis, [(i, (i + step) % n) for i in range(n)])


def swapped(x, axis, bit):
    n = lax.axis_size(axis)
    return lax.ppermute(x, axis, [(i, i ^ bit) for i in range(n)])


def halos(own, width):
    height = own.shape[1]
    if height >= width:
        return (
            moved(own[:, height - width :], "space", 1),
            moved(own[:, :width], "space", -1),
        )
    hops = -(-width // height)
    up = jnp.concatenate([moved(own, "space", k) for k in range(hops, 0, -1)], axis=1)
    down = jnp.concatenate([moved(own, "space", -k) for k in range(1, hops + 1)], axis=1)
    return up[:, up.shape[1] - width :], down[:, :width]


def packed_weights(w_first, b_first, w_mid, b_mid, w_last, b_last):
    mid = jnp.transpose(w_mid, (0, 1, 4, 2, 3)).reshape(NL, 3, 16, 192)
    bias = jnp.broadcast_to(b_mid[:, None, :, None], (NL, 3, 16, 64))
    mid = jnp.concatenate([mid, bias], axis=3).reshape(MIDROWS, KW)
    last = jnp.transpose(w_last, (0, 3, 1, 2)).reshape(3, 8, 192)
    last = jnp.concatenate([last, jnp.broadcast_to(b_last[None, :, None], (3, 8, 64))], axis=2)
    last = jnp.pad(last, ((0, 0), (0, 8), (0, 0))).reshape(48, KW)
    first = jnp.pad(jnp.transpose(w_first, (3, 0, 2, 1)), ((0, 0), (0, 0), (0, 0), (0, 1)))
    first = first.reshape(16, 24)
    first = jnp.concatenate([first, jnp.broadcast_to(b_first[:, None], (16, KW - 24))], axis=1)
    return jnp.concatenate([mid, last, first], axis=0)


def vmem(count):
    return [pl.BlockSpec(memory_space=pltpu.VMEM)] * count


def per_device(velocity, w_first, b_first, w_mid, b_mid, w_last, b_last, offsets, cotangent):
    traj, h, nx = velocity.shape[1:]
    space = lax.axis_size("space")
    ny = h * space
    me_chan = lax.axis_index("chan")
    me_space = lax.axis_index("space")
    me = jnp.stack([me_chan, me_space]).astype(jnp.int32)
    rows = h + 2 * HALO
    own = lax.dynamic_index_in_dim(velocity, me_chan, 1, keepdims=False)
    own_cot = lax.dynamic_index_in_dim(cotangent, me_chan, 1, keepdims=False)

    packed = packed_weights(w_first, b_first, w_mid, b_mid, w_last, b_last)
    across = swapped(packed, "chan", 2)
    up, down = halos(own, HALO)
    beside = swapped(packed, "chan", 1)
    diagonal = swapped(across, "chan", 1)
    cot_full = lax.all_to_all(
        jnp.broadcast_to(own_cot[None], (space,) + own_cot.shape), "space", 0, 0, tiled=True
    ).reshape(space * 2 * h, nx)

    any_space = pl.BlockSpec(memory_space=pl.ANY)
    smem = pl.BlockSpec(memory_space=pltpu.SMEM)
    shape = jax.ShapeDtypeStruct
    deep = h + 2 * DEEP
    prov, vp, vs, face, mix, x_all, g_all, wk, w7, wf, perm, squares = pl.pallas_call(
        functools.partial(forward_kernel, h),
        out_shape=[
            shape((2, h, nx), f32),
            shape((2, rows, nx), f32),
            shape((nx // 128, rows * 8, 128), f32),
            shape((2, h + 4, nx), f32),
            shape(((h + 4) * 32, nx), f32),
            shape((NL + 1, h + 2, C, nx), bf16),
            shape((NL + 1, h + 2 * (NL + 1), C, nx), bf16),
            shape((NL * 3, C, KW), bf16),
            shape((3, 32, KW), bf16),
            shape((C, KW), bf16),
            shape((32, 32), f32),
            shape((8, KW), f32),
        ],
        in_specs=[smem] + vmem(8),
        out_specs=vmem(5) + [any_space, any_space] + vmem(5),
        scratch_shapes=[
            pltpu.VMEM((NL + 1, deep, C, nx), bf16),
            pltpu.VMEM((NL + 1, deep, C, nx), bf16),
            pltpu.VMEM((3, 32, KW), f32),
            pltpu.VMEM((nx // 128, (h + 4) * 8, 128), f32),
            pltpu.SemaphoreType.DMA((NL + 1,)),
            pltpu.SemaphoreType.DMA((NL + 1,)),
        ],
        compiler_params=pltpu.CompilerParams(vmem_limit_bytes=56 * 2**20),
        name="forward",
    )(me, own, up, down, packed, beside, across, diagonal, offsets)

    everywhere = lax.all_gather(prov, ("space", "chan"), axis=0, tiled=False)

    ty = basis(ny)
    tx = basis(nx)
    t_full = jnp.asarray(tx.astype(np.float32))
    t_back = jnp.asarray(np.ascontiguousarray(tx.T).astype(np.float32))
    wide = np.zeros((2 * ny, space, 2, h))
    for c in range(2):
        wide[c * ny : (c + 1) * ny, :, c, :] = ty.T.reshape(ny, space, h)
    t_wide = jnp.asarray(wide.reshape(2 * ny, 2 * ny).astype(np.float32))
    ring = (np.arange(space)[:, None] * h + np.arange(h + 2 * GPH)[None, :] - GPH) % ny
    t_rows = jnp.asarray(ty[ring].astype(np.float32))
    spectral = [jnp.asarray(m.astype(np.float32)) for m in multipliers(ny, nx)]

    vel_grad, pack = pl.pallas_call(
        functools.partial(backward_kernel, h),
        out_shape=[shape((2, h, nx), f32), shape((4, MIDROWS + 48, KW), bf16)],
        in_specs=[smem] + vmem(12) + [any_space, any_space] + vmem(5),
        out_specs=vmem(2),
        scratch_shapes=[
            pltpu.VMEM((NL + 1, h + 2, C, nx), bf16),
            pltpu.VMEM((NL + 1, h + 2 * (NL + 1), C, nx), bf16),
            pltpu.VMEM((h + 14, 32, nx), bf16),
        ]
        + [pltpu.VMEM((h + 2 * l, C, nx), bf16) for l in range(6, 0, -1)]
        + [
            pltpu.VMEM((nx // 128, (h + 2 * GPH) * 8, 128), f32),
            pltpu.VMEM((2, h + 2 * GPH, nx), f32),
            pltpu.VMEM((7, 192, KW), f32),
            pltpu.VMEM((2, h + 2 * GPH, nx), f32),
            pltpu.VMEM((nx // 128, h * 8, 128), f32),
            pltpu.SemaphoreType.DMA((NL + 1,)),
            pltpu.SemaphoreType.DMA((NL + 1,)),
        ],
        compiler_params=pltpu.CompilerParams(vmem_limit_bytes=60 * 2**20),
        name="backward",
    )(
        me, cot_full, t_full, t_back, t_wide, t_rows, *spectral,
        vp, vs, face, mix, x_all, g_all, wk, w7, wf, perm, squares,
    )

    pair = (pack[0:2].astype(f32) + swapped(pack[2:4], "chan", 1).astype(f32)).astype(bf16)
    total = pair[0].astype(f32) + swapped(pair[1], "chan", 2).astype(f32)
    bit = 1
    while bit < space:
        low = total.astype(bf16)
        total = low.astype(f32) + swapped(low, "space", bit).astype(f32)
        bit *= 2

    new_velocity, new_sq = pl.pallas_call(
        functools.partial(project_kernel, h),
        out_shape=[shape((2, traj, h, nx), f32), shape((8, 128), f32)],
        in_specs=[smem] + vmem(8),
        out_specs=vmem(2),
        compiler_params=pltpu.CompilerParams(vmem_limit_bytes=56 * 2**20),
        name="project",
    )(
        me, everywhere.reshape(space, traj, 2 * h, nx), t_full, t_back, t_wide, t_rows, *spectral
    )

    mid = total[:MIDROWS].reshape(NL, 3, 16, KW)
    w_mid_grad = jnp.transpose(mid[..., :192].reshape(NL, 3, 16, 3, C), (0, 3, 1, 4, 2))
    b_mid_grad = mid[:, 0, :, 192]
    last = total[MIDROWS : MIDROWS + 24].reshape(3, 8, KW)
    w_last_grad = jnp.transpose(last[..., :192].reshape(3, 8, 3, C), (2, 0, 3, 1))
    b_last_grad = last[0, :, 192]
    first = total[MIDROWS + 32 :]
    w_first_grad = jnp.transpose(first[:, :24].reshape(16, 3, 2, 4)[..., :3], (1, 3, 2, 0))
    b_first_grad = first[:, 24]
    sums = jnp.concatenate([total[MIDROWS + 24, 0:3], new_sq[0, 0:1]])
    rms_stats = jnp.sqrt(sums / (2 * traj * ny * nx))
    return (
        new_velocity,
        vel_grad[:, None],
        w_first_grad,
        b_first_grad,
        w_mid_grad,
        b_mid_grad,
        w_last_grad,
        b_last_grad,
        rms_stats,
    )


def solution(mesh):
    return jax.shard_map(
        per_device,
        mesh=mesh,
        in_specs=(
            P(None, None, "space", None),
            P(None, None, None, "chan"),
            P("chan"),
            P(None, None, None, None, "chan"),
            P(None, "chan"),
            P(None, None, None, "chan"),
            P("chan"),
            P(),
            P(None, None, "space", None),
        ),
        out_specs=(
            P(None, None, "space", None),
            P(None, "chan", "space", None),
            P(None, None, None, "chan"),
            P("chan"),
            P(None, None, None, None, "chan"),
            P(None, "chan"),
            P(None, None, None, "chan"),
            P("chan"),
            P(),
        ),
        check_vma=False,
    )
```

```python
import functools

import jax
import jax.numpy as jnp
import numpy as np
from jax import lax
from jax.experimental import pallas as pl
from jax.experimental.pallas import tpu as pltpu
from jax.sharding import PartitionSpec as P

f32 = jnp.float32
bf16 = jnp.bfloat16
highest = lax.Precision.HIGHEST
time_step = 0.2
viscosity = 0.256
HALO = 16
DEEP = 12
GPH = 8
C = 64
NL = 5
KW = 256
MIDROWS = NL * 3 * 16
A0 = 0.7978845608028654
A1 = 0.044715 * A0


def basis(length):
    half = length // 2
    pos = np.arange(length)[:, None]
    table = np.zeros((length, length))
    m = np.arange(half + 1)[None, :]
    table[:, : half + 1] = np.cos(2 * np.pi * ((pos * m) % length) / length) * np.sqrt(2.0 / length)
    table[:, 0] = np.sqrt(1.0 / length)
    table[:, half] = np.cos(np.pi * pos[:, 0]) * np.sqrt(1.0 / length)
    m = np.arange(1, half)[None, :]
    table[:, half + 1 :] = np.sin(2 * np.pi * ((pos * m) % length) / length) * np.sqrt(2.0 / length)
    return table


def multipliers(ny, nx):
    def modes(n):
        half = n // 2
        index = np.arange(n)
        wave = np.where(index <= half, index, index - half) * (2 * np.pi / n)
        return wave, index <= half

    ky, cy = modes(ny)
    kx, cx = modes(nx)
    ky, cy = ky[:, None], cy[:, None]
    kx, cx = kx[None, :], cx[None, :]
    sq = kx * kx + ky * ky
    inv = np.where(sq > 0, 1.0 / np.where(sq > 0, sq, 1.0), 0.0)
    sign = np.where(cx == cy, 1.0, -1.0)
    edge_x = (kx == 0) | (kx >= np.pi - 1e-9)
    edge_y = (ky == 0) | (ky >= np.pi - 1e-9)
    mxy = np.where(edge_x | edge_y, 0.0, sign * kx * ky * inv)
    mxx = 1.0 - kx * kx * inv
    myy = 1.0 - ky * ky * inv
    return mxx, myy, mxy


def project_spectral(u, v, mxx, myy, mxy):
    half_y, half_x = u.shape[0] // 2, u.shape[1] // 2

    def swap(a):
        a = jnp.concatenate([a[:, half_x:], a[:, :half_x]], axis=1)
        return jnp.concatenate([a[half_y:], a[:half_y]], axis=0)

    rows = lax.broadcasted_iota(jnp.int32, u.shape, 0)
    cols = lax.broadcasted_iota(jnp.int32, u.shape, 1)
    corner = jnp.where((rows == half_y) & (cols == half_x), -0.5, 0.0)
    return (
        mxx * u + mxy * swap(v) + corner * v,
        myy * v + mxy * swap(u) + corner * u,
    )


def halves(x):
    high = x.astype(bf16)
    return high, (x - high.astype(f32)).astype(bf16)


def product(a, b):
    def dot(x, y):
        return jnp.dot(x, y, preferred_element_type=f32)

    return dot(a[0], b[0]) + (dot(a[1], b[0]) + dot(a[0], b[1]))


def both(ref):
    return ref[0], ref[1]


def spectrum(h, field_ref, tx_ref, ty_ref):
    ny = field_ref.shape[0] * h if h % 8 == 0 else field_ref.shape[0] // 2
    if h % 8 == 0:
        fields = [field_ref[:, c].reshape(ny, KW) for c in range(2)]
        field = jnp.concatenate(fields, axis=0)
    else:
        field = field_ref[...]
    along = product(halves(field), both(tx_ref))
    table = both(ty_ref)
    if h % 8 == 0:
        return [product(table, halves(along[c * ny : (c + 1) * ny])) for c in range(2)]
    out = product(table, halves(along))
    return out[:ny], out[ny:]


def project_back(trow, u, back_ref):
    back = both(back_ref)
    return product(halves(product(trow, halves(u))), back)


def gelu_both(z):
    z2 = z * z
    t = jnp.tanh(z * (A0 + A1 * z2))
    h = 0.5 * t + 0.5
    a = z * h
    return a, h + a * (1.0 - h) * (2.0 * A0 + 6.0 * A1 * z2)


def lroll(x, s):
    return pltpu.roll(x, s % x.shape[1], 1)


def shifts(x):
    return jnp.concatenate([lroll(x, 1), x, lroll(x, -1)], axis=0)


def unshifts(x):
    return jnp.concatenate([lroll(x, -1), x, lroll(x, 1)], axis=0)


def spread(ref, first, values):
    for k in range(ref.shape[0]):
        ref[k, pl.ds(first, values.shape[0], stride=8), :] = values[:, k * 128 : k * 128 + 128]


def collect(ref, first, count):
    planes = [ref[k, pl.ds(first, count, stride=8), :] for k in range(ref.shape[0])]
    return jnp.concatenate(planes, axis=1)


def rows_of(ref, first, count):
    at = pl.ds(first if isinstance(first, int) else pl.multiple_of(first, 8), count)
    return jnp.concatenate([ref[k, at, :] for k in range(ref.shape[0])], axis=1)


def put_rows(ref, first, values):
    at = pl.ds(
        first if isinstance(first, int) else pl.multiple_of(first, 8), values.shape[0]
    )
    for k in range(ref.shape[0]):
        ref[k, at, :] = values[:, k * 128 : k * 128 + 128]


def group4(s):
    i = lax.broadcasted_iota(jnp.int32, s.shape, 0)
    s = s + jnp.where(i % 2 == 0, pltpu.roll(s, 7, 0), pltpu.roll(s, 1, 0))
    return s + jnp.where((i // 2) % 2 == 0, pltpu.roll(s, 6, 0), pltpu.roll(s, 2, 0))


def point_order(offs):
    row = lax.broadcasted_iota(jnp.int32, (32, 16), 0)
    point = (row // 8) * 4 + row % 4
    comp = (row // 4) % 2
    parts = [
        jnp.where((comp == c) & (offs[c : c + 1, :] == point), 1.0, 0.0).astype(f32)
        for c in range(2)
    ]
    return jnp.concatenate(parts, axis=1)


def blocks(n, most=27):
    count = -(-n // most)
    return count, -(-n // count)


def forward_kernel(
    h, me_ref, vel_ref, up_ref, down_ref, w0, w1, w2, w3, offs_ref,
    prov_ref, vp_ref, vs_ref, face_ref, mix_ref, x_out, g_out, wk_ref, w7_ref, wf_ref, perm_ref, sq_ref,
    xb, gb, w7k, f8, xsem, gsem,
):
    rows = h + 2 * HALO
    me = me_ref[0]
    for k, piece in enumerate((w0, w1, w2, w3)):
        slot = jnp.bitwise_xor(me, k)
        at16 = pl.ds(pl.multiple_of(slot * 16, 16), 16)
        at8 = pl.ds(pl.multiple_of(slot * 8, 8), 8)
        for n in range(NL * 3):
            wk_ref[n, at16, :] = piece[n * 16 : n * 16 + 16]
        for j in range(3):
            block = piece[MIDROWS + j * 16 : MIDROWS + j * 16 + 16].astype(f32)
            w7k[j, at8, :] = block[0:8]
        wf_ref[at16, :] = piece[MIDROWS + 48 : MIDROWS + 64]
    perm = point_order(offs_ref[...])
    perm_ref[...] = perm
    perm_low = perm.astype(bf16)
    for i in range(3):
        w7_ref[i] = jnp.dot(perm_low, w7k[i].astype(bf16), preferred_element_type=f32).astype(bf16)

    vp_ref[:, 0:HALO] = up_ref[...]
    vp_ref[:, HALO : HALO + h] = vel_ref[...]
    vp_ref[:, HALO + h :] = down_ref[...]
    for c in range(2):
        plane = vp_ref[c]
        for d in range(4):
            spread(vs_ref, c * 4 + d, lroll(plane, 1 - d))

    def vs_rows(y, n):
        return rows_of(vs_ref, (y + HALO) * 8, 8 * n)

    def copies(l):
        return (
            pltpu.make_async_copy(xb.at[l, pl.ds(DEEP - 1, h + 2)], x_out.at[l], xsem.at[l]),
            pltpu.make_async_copy(
                gb.at[l, pl.ds(DEEP - l - 1, h + 2 * (l + 1))],
                g_out.at[l, pl.ds(0, h + 2 * (l + 1))],
                gsem.at[l],
            ),
        )

    wfirst = wf_ref[:, 0:24]
    bias = jnp.broadcast_to(wf_ref[:, 24:25].astype(f32), (C, KW))
    n = h + 2 * (DEEP - 1)
    count, size = blocks(n)

    def first_block(k, _):
        top = jnp.minimum(k * size, n - size) - (DEEP - 1)
        for r in range(size):
            y = top + r
            x = vs_rows(y - 1, 3).astype(bf16)
            z = jnp.dot(wfirst, x, preferred_element_type=f32)
            a, d = gelu_both(z + bias)
            xb[0, y + DEEP] = a.astype(bf16)
            gb[0, y + DEEP] = d.astype(bf16)
        return 0

    lax.fori_loop(0, count, first_block, 0)
    for copy in copies(0):
        copy.start()

    for l in range(1, NL + 1):
        weight = wk_ref[3 * (l - 1) : 3 * l].reshape(192, KW)
        bias = jnp.broadcast_to(weight[0:C, 192:193].astype(f32), (C, KW))
        weight = weight[:, 0:192]
        n = h + 2 * (DEEP - 1 - l)
        count, size = blocks(n)

        def block(k, _, l=l, weight=weight, bias=bias, n=n, size=size):
            top = jnp.minimum(k * size, n - size) - (DEEP - 1 - l) + DEEP
            p0 = p1 = None
            for r in range(-1, size + 1):
                o = jnp.dot(weight, shifts(xb[l - 1, top + r]), preferred_element_type=f32)
                if r >= 1:
                    a, d = gelu_both(p1 + o[128:192] + bias)
                    xb[l, top + r - 1] = a.astype(bf16)
                    gb[l, top + r - 1] = d.astype(bf16)
                p1 = o[64:128] if p0 is None else p0 + o[64:128]
                p0 = o[0:64]
            return 0

        lax.fori_loop(0, count, block, 0)
        for copy in copies(l):
            copy.start()

    weight = w7_ref[...].reshape(96, KW)
    bias = jnp.broadcast_to(weight[0:32, 192:193].astype(f32), (32, KW))
    weight = weight[:, 0:192]
    row = lax.broadcasted_iota(jnp.int32, (32, KW), 0)
    point = (row // 8) * 4 + row % 4
    second = jnp.where((row // 4) % 2 == 0, 6, 9)
    base = jnp.where((point == 5) | (point == second), 0.5, 0.0).astype(f32)
    n = h + 4
    count, size = blocks(n, 12)

    def last_block(k, _):
        top = jnp.minimum(k * size, n - size) - 2
        p0 = p1 = None
        for r in range(-1, size + 1):
            o = jnp.dot(weight, shifts(xb[NL, top + r + DEEP]), preferred_element_type=f32)
            if r >= 1:
                y = top + r - 1
                s = p1 + o[64:96] + bias
                mean = group4(s[0:8] + s[8:16] + s[16:24] + s[24:32]) * (1.0 / 16.0)
                mix = s - jnp.concatenate([mean] * 4, axis=0) + base
                mix_ref[pl.ds(pl.multiple_of((y + 2) * 32, 32), 32), :] = mix
                m = mix * vs_rows(y - 1, 4)
                m = group4(m[0:8] + m[8:16] + m[16:24] + m[24:32])
                put_rows(f8, (y + 2) * 8, m)
            p1 = o[32:64] if p0 is None else p0 + o[32:64]
            p0 = o[0:32]
        return 0

    lax.fori_loop(0, count, last_block, 0)
    for c in range(2):
        face_ref[c] = collect(f8, c * 4, h + 4)
    ue = face_ref[0, 2 : 2 + h]
    vn = face_ref[1, 2 : 2 + h]
    vn_south = face_ref[1, 1 : 1 + h]
    total = [jnp.sum(ue * ue) + jnp.sum(vn * vn)]
    own = update = 0.0
    for c in range(2):
        q = vp_ref[c, HALO : HALO + h]
        north = vp_ref[c, HALO + 1 : HALO + 1 + h]
        south = vp_ref[c, HALO - 1 : HALO - 1 + h]
        east, west = lroll(q, -1), lroll(q, 1)
        lap = east + west + north + south - 4.0 * q
        fx = ue * (q + east) * 0.5
        adv = fx - lroll(fx, 1) + vn * (q + north) * 0.5 - vn_south * (south + q) * 0.5
        new = q + time_step * (viscosity * lap - adv)
        for k in range(prov_ref.shape[0]):
            prov_ref[k, c] = new
        own = own + jnp.sum(q * q)
        update = update + jnp.sum((new - q) * (new - q))
    lane = lax.broadcasted_iota(jnp.int32, (8, KW), 1)
    sq_ref[...] = jnp.where(
        lane == 0, own, jnp.where(lane == 1, total[0], jnp.where(lane == 2, update, 0.0))
    )
    for l in range(NL + 1):
        for copy in copies(l):
            copy.wait()


def backward_kernel(
    h, me_ref, cot_ref, tx_ref, ty_ref, back_ref, trow_ref, mxx_ref, myy_ref, mxy_ref,
    vp_ref, vs_ref, face_ref, mix_ref, x_in, g_in, wk_ref, w7_ref, wf_ref, perm_ref, sq_ref,
    vel_grad_ref, keep_ref, send_ref,
    xb, gb, gz7, gz6, gz5, gz4, gz3, gz2, gz1, f8, adv_ref, acc_ref, gp_ref, near8, xsem, gsem,
):
    me_chan = me_ref[0]
    me_space = me_ref[1]

    def copies(l):
        return (
            pltpu.make_async_copy(x_in.at[l], xb.at[l], xsem.at[l]),
            pltpu.make_async_copy(
                g_in.at[l, pl.ds(0, h + 2 * (l + 1))],
                gb.at[l, pl.ds(0, h + 2 * (l + 1))],
                gsem.at[l],
            ),
        )

    for l in range(NL, -1, -1):
        for copy in copies(l):
            copy.start()

    n = h + 2 * GPH
    u, v = spectrum(h, cot_ref, tx_ref, ty_ref)
    u, v = project_spectral(u, v, mxx_ref[...], myy_ref[...], mxy_ref[...])
    trow = (trow_ref[0, me_space], trow_ref[1, me_space])
    gp_ref[0] = project_back(trow, u, back_ref)
    gp_ref[1] = project_back(trow, v, back_ref)

    m = n - 1
    fields = []
    gue = gvn = 0.0
    for c in range(2):
        g = -time_step * gp_ref[c, 0:m]
        g_north = -time_step * gp_ref[c, 1 : m + 1]
        q = vp_ref[c, HALO - GPH : HALO - GPH + m]
        q_north = vp_ref[c, HALO - GPH + 1 : HALO - GPH + 1 + m]
        gfx = g - lroll(g, -1)
        gfy = g - g_north
        gue = gue + gfx * (q + lroll(q, -1)) * 0.5
        gvn = gvn + gfy * (q + q_north) * 0.5
        adv_ref[c, 0:m] = gfy
        fields.append(gfx[GPH : GPH + h])
    for d in range(4):
        spread(f8, d, gue)
        spread(f8, 4 + d, gvn)
    ue = face_ref[0, 2 : 2 + h]
    vn = face_ref[1, 2 : 2 + h]
    vn_south = face_ref[1, 1 : 1 + h]
    for c in range(2):
        g = gp_ref[c, GPH : GPH + h]
        lap = (
            lroll(g, -1) + lroll(g, 1) + gp_ref[c, GPH + 1 : GPH + 1 + h]
            + gp_ref[c, GPH - 1 : GPH - 1 + h] - 4.0 * g
        )
        ex = fields[c] * ue
        ny = adv_ref[c, GPH : GPH + h] * vn
        sy = adv_ref[c, GPH - 1 : GPH - 1 + h] * vn_south
        vel_grad_ref[c] = g + time_step * viscosity * lap + 0.5 * (ex + lroll(ex, 1) + ny + sy)

    def f8_row(y):
        return rows_of(f8, (y + GPH) * 8, 8)

    def vs_rows(y, count):
        return rows_of(vs_ref, (y + HALO) * 8, 8 * count)

    def stencil_row(k, _):
        for r in range(2):
            y = 2 * k + r - 7
            face = f8_row(y)
            near = vs_rows(y - 1, 4)
            s = near[0:8] + near[8:16] + near[16:24] + near[24:32]
            mean = group4(s) * (1.0 / 16.0)
            gm = (near - jnp.concatenate([mean] * 4, axis=0)) * jnp.concatenate([face] * 4, axis=0)
            gz7[y + 7] = gm.astype(bf16)
        return 0

    lax.fori_loop(0, (h + 14) // 2, stencil_row, 0, unroll=4 if h >= 16 else 1)

    ones = jnp.ones((16, KW), bf16)

    def wgrad(columns, inputs):
        return lax.dot_general(
            jnp.concatenate(columns, axis=1),
            jnp.concatenate(inputs, axis=1),
            (((1,), (1,)), ((), ())),
            preferred_element_type=f32,
        )

    gzs = {7: gz7, 6: gz6, 5: gz5, 4: gz4, 3: gz3, 2: gz2, 1: gz1}
    for l in range(7, 1, -1):
        for copy in copies(l - 2):
            copy.wait()
        source, target = gzs[l], gzs[l - 1]
        xs, gs = xb.at[l - 2], gb.at[l - 2]
        if l == 7:
            parts = [w7_ref[i][:, 0:192].astype(f32) for i in range(3)]
            width = 32
        else:
            parts = [wk_ref[3 * (l - 2) + i][:, 0:192].astype(f32) for i in range(3)]
            width = C
        weight = jnp.concatenate(
            [
                jnp.concatenate([p[:, j * C : (j + 1) * C].T for j in range(3)], axis=1)
                for p in parts
            ],
            axis=0,
        ).astype(bf16)
        p0 = p1 = None
        acc = None
        for ys in (range(-l, h // 2), range(h // 2, h + l)):
            columns = {y: unshifts(source[y + l]) for y in ys}
            for y in ys:
                o = jnp.dot(weight, columns[y], preferred_element_type=f32)
                if y >= 2 - l:
                    ga = p1 + o[0:64]
                    target[y - 1 + l - 1] = (ga * gs[y - 1 + l - 1].astype(f32)).astype(bf16)
                p1 = o[64:128] if p0 is None else p0 + o[64:128]
                p0 = o[128:192]
            own = [y for y in ys if 0 <= y < h]
            part = wgrad(
                [columns[y] for y in own],
                [
                    jnp.concatenate([xs[y : y + 3].reshape(192, KW), ones], axis=0)
                    for y in own
                ],
            )
            acc = part if acc is None else acc + part
        if l == 7:
            back = perm_ref[...]
            acc = jnp.concatenate(
                [
                    lax.dot_general(
                        back, acc[j * 32 : j * 32 + 32], (((0,), (0,)), ((), ())),
                        preferred_element_type=f32, precision=highest,
                    )
                    for j in range(3)
                ],
                axis=0,
            )
        acc_ref[l - 1, 0 : 3 * width, 0:208] = acc

    wfirst = wf_ref[:, 0:32].astype(f32).T.astype(bf16)
    source = gz1
    outs = {}
    for y in range(-1, h + 1):
        outs[y] = jnp.dot(wfirst[0:24], source[y + 1], preferred_element_type=f32)
    acc_ref[0, 0:64, 0:40] = wgrad(
        [source[y + 1] for y in range(h)],
        [
            jnp.concatenate(
                [vs_rows(y - 1, 3), jnp.ones((16, KW), f32)], axis=0
            ).astype(bf16)
            for y in range(h)
        ],
    )
    for y in range(h):
        total = outs[y + 1][0:8] + outs[y][8:16] + outs[y - 1][16:24]
        for k in range(4):
            at = y + 1 - k
            total = total + f8_row(at) * mix_ref[pl.ds((at + 2) * 32 + k * 8, 8), :]
        put_rows(near8, y * 8, total)
    for c in range(2):
        total = vel_grad_ref[c]
        for d in range(4):
            total = total + lroll(collect(near8, c * 4 + d, h), d - 1)
        vel_grad_ref[c] = total

    for k, other in enumerate((0, 2, 1, 3)):
        slot = jnp.bitwise_xor(me_chan, other)
        pack_ref = (keep_ref, send_ref)[k // 2]
        k = k % 2
        for l in range(NL):
            for j in range(3):
                piece = acc_ref[l + 1, pl.ds(pl.multiple_of(j * 64 + slot * 16, 16), 16), :]
                pack_ref[k, (3 * l + j) * 16 : (3 * l + j) * 16 + 16, :] = piece.astype(bf16)
        last = [
            acc_ref[6, pl.ds(pl.multiple_of(j * 32 + slot * 8, 8), 8), :] for j in range(3)
        ]
        pack_ref[k, MIDROWS : MIDROWS + 32, :] = jnp.concatenate(
            last + [sq_ref[...]], axis=0
        ).astype(bf16)
        pack_ref[k, MIDROWS + 32 : MIDROWS + 48, :] = acc_ref[
            0, pl.ds(pl.multiple_of(slot * 16, 16), 16), :
        ].astype(bf16)


def project_kernel(h, me_ref, prov_ref, tx_ref, ty_ref, back_ref, trow_ref, mxx_ref, myy_ref, mxy_ref, out_ref):
    me_space = me_ref[1]
    trow = tuple(trow_ref[k, me_space][GPH : GPH + h] for k in range(2))
    u, v = spectrum(h, prov_ref, tx_ref, ty_ref)
    u, v = project_spectral(u, v, mxx_ref[...], myy_ref[...], mxy_ref[...])
    out_ref[0:h] = project_back(trow, u, back_ref)
    out_ref[h : 2 * h] = project_back(trow, v, back_ref)
    out_ref[2 * h :] = jnp.full((8, KW), jnp.sum(u * u) + jnp.sum(v * v), f32)


def prepare_kernel(h, me_ref, vel_ref, cot_ref, wm_ref, wl_ref, wf_ref, bm_ref, bf_ref, bl_ref, pack_ref, own_ref, top_ref, bottom_ref, cot_all_ref, tall, wide):
    me = me_ref[0]
    own = vel_ref[:, me]
    own_ref[...] = own
    if h >= HALO:
        top_ref[...] = own[:, :HALO]
        bottom_ref[...] = own[:, h - HALO :]
    cot = cot_ref[:, me]
    for k in range(cot_all_ref.shape[0]):
        cot_all_ref[k] = cot
    wide[...] = jnp.zeros_like(wide)
    wide[0:NL, 0:16] = bm_ref[...].astype(f32)
    wide[NL : NL + 1, 0:16] = bf_ref[...].astype(f32)
    wide[NL + 1 : NL + 2, 0:8] = bl_ref[...].astype(f32)
    columns = wide[...].T

    def column(k, count, width):
        return jnp.broadcast_to(columns[0:count, k : k + 1], (count, width))

    for l in range(NL):
        for i in range(3):
            parts = [wm_ref[l, i, j] for j in range(3)] + [column(l, 16, 64).astype(bf16)]
            at = (3 * l + i) * 16
            pack_ref[at : at + 16, :] = jnp.concatenate(parts, axis=1)
    for i in range(3):
        parts = [wl_ref[i, j].astype(f32) for j in range(3)] + [column(NL + 1, 8, 64)]
        block = jnp.concatenate(parts, axis=1)
        at = MIDROWS + i * 16
        pack_ref[at : at + 16, :] = jnp.concatenate([block, jnp.zeros_like(block)], axis=0).astype(bf16)
    tall[...] = jnp.zeros_like(tall)
    for i in range(3):
        for j in range(3):
            taps = wf_ref[i, j].astype(f32)
            for c in range(2):
                at = i * 8 + c * 4 + j
                tall[at : at + 1, 0:16] = taps[c : c + 1]
    tall[24:25, 0:16] = bf_ref[...].astype(f32)
    first = tall[...].T[0:16]
    pack_ref[MIDROWS + 48 :, :] = jnp.concatenate([first, jnp.zeros_like(first)], axis=1).astype(bf16)


def finish_kernel(h, cells, me_ref, low_ref, other_ref, n0, n1, n2, n3, new_ref, wf_ref, bf_ref, wm_ref, bm_ref, wl_ref, bl_ref, rms_ref, parts):
    me = me_ref[0]
    for k, piece in enumerate((n0, n1, n2, n3)):
        slot = jnp.bitwise_xor(me, k)
        new_ref[0, slot] = piece[0:h]
        new_ref[1, slot] = piece[h : 2 * h]
        parts[slot] = piece[2 * h :]

    def total(at, count):
        return low_ref[at : at + count, :].astype(f32) + other_ref[at : at + count, :].astype(f32)

    def turned(block):
        return jnp.concatenate([block, jnp.zeros((128 - block.shape[0], 128), f32)], axis=0).T

    for l in range(NL):
        for j in range(3):
            block = total((3 * l + j) * 16, 16)
            for i in range(3):
                wm_ref[l, i, j] = block[:, i * 64 : i * 64 + 64]
            if j == 0:
                bm_ref[l : l + 1, :] = turned(block[:, 128:256])[64:65, 0:16]
    tail = total(MIDROWS, 32)
    for j in range(3):
        block = tail[j * 8 : j * 8 + 8]
        for i in range(3):
            wl_ref[i, j] = block[:, i * 64 : i * 64 + 64]
        if j == 0:
            bl_ref[...] = turned(block[:, 128:256])[64:65, 0:8]
    first = turned(total(MIDROWS + 32, 16)[:, 0:128])
    for i in range(3):
        for j in range(3):
            for c in range(2):
                at = i * 8 + c * 4 + j
                wf_ref[i, j, c : c + 1, :] = first[at : at + 1, 0:16]
    bf_ref[...] = first[24:25, 0:16]
    news = (parts[0] + parts[1]) + (parts[2] + parts[3])
    lane = lax.broadcasted_iota(jnp.int32, (8, 128), 1)
    sums = jnp.where(lane == 3, news[:, 0:128], tail[24:32, 0:128])
    rms_ref[...] = jnp.sqrt(sums * (1.0 / cells))[0:1, 0:4]


def moved(x, axis, step):
    n = lax.axis_size(axis)
    return lax.ppermute(x, axis, [(i, (i + step) % n) for i in range(n)])


def swapped(x, axis, bit):
    n = lax.axis_size(axis)
    return lax.ppermute(x, axis, [(i, i ^ bit) for i in range(n)])


def halos(own, top, bottom, width):
    height = own.shape[1]
    if height >= width:
        return moved(bottom, "space", 1), moved(top, "space", -1)
    hops = -(-width // height)
    up = jnp.concatenate([moved(own, "space", k) for k in range(hops, 0, -1)], axis=1)
    down = jnp.concatenate([moved(own, "space", -k) for k in range(1, hops + 1)], axis=1)
    return up[:, up.shape[1] - width :], down[:, :width]


def tables(h, space, nx):
    ny = h * space
    ty, tx = basis(ny), basis(nx)

    def two(table):
        high = table.astype(np.float32).astype(jnp.bfloat16)
        low = (table - high.astype(np.float64)).astype(np.float32).astype(jnp.bfloat16)
        return jnp.asarray(np.stack([high, low]))

    back_y = ty.T
    if h % 8:
        wide = np.zeros((2, ny, space, 2, h))
        for c in range(2):
            wide[c, :, :, c, :] = ty.T.reshape(ny, space, h)
        back_y = wide.reshape(2 * ny, 2 * ny)
    ring = (np.arange(space)[:, None] * h + np.arange(h + 2 * GPH)[None, :] - GPH) % ny
    spectral = [jnp.asarray(m.astype(np.float32)) for m in multipliers(ny, nx)]
    return [two(tx), two(back_y), two(tx.T), two(ty[ring])] + spectral


def vmem(count):
    return [pl.BlockSpec(memory_space=pltpu.VMEM)] * count


def per_device(velocity, w_first, b_first, w_mid, b_mid, w_last, b_last, offsets, cotangent):
    traj, h, nx = velocity.shape[1:]
    space = lax.axis_size("space")
    ny = h * space
    me_chan = lax.axis_index("chan")
    me_space = lax.axis_index("space")
    me = jnp.stack([me_chan, me_space]).astype(jnp.int32)
    rows = h + 2 * HALO
    shape = jax.ShapeDtypeStruct
    smem = pl.BlockSpec(memory_space=pltpu.SMEM)
    limit = pltpu.CompilerParams(vmem_limit_bytes=56 * 2**20)
    packed, own, top, bottom, cot_all = pl.pallas_call(
        functools.partial(prepare_kernel, h),
        out_shape=[
            shape((MIDROWS + 64, KW), bf16),
            shape((2, h, nx), f32),
            shape((2, min(h, HALO), nx), f32),
            shape((2, min(h, HALO), nx), f32),
            shape((space, 2, h, nx), f32),
        ],
        in_specs=[smem] + vmem(8),
        out_specs=vmem(5),
        scratch_shapes=[pltpu.VMEM((128, 128), f32), pltpu.VMEM((8, 128), f32)],
        compiler_params=limit,
        name="prepare",
    )(
        me, velocity, cotangent, jnp.swapaxes(w_mid, 3, 4), jnp.swapaxes(w_last, 2, 3), w_first,
        b_mid, b_first[None], b_last[None],
    )
    across = swapped(packed, "chan", 2)
    up, down = halos(own, top, bottom, HALO)
    across, up, down, cot_all = lax.optimization_barrier((across, up, down, cot_all))
    beside = swapped(packed, "chan", 1)
    diagonal = swapped(across, "chan", 1)
    cot_full = lax.all_to_all(cot_all, "space", 0, 0, tiled=True)
    if h % 8:
        cot_full = cot_full.reshape(space * 2 * h, nx)

    any_space = pl.BlockSpec(memory_space=pl.ANY)
    deep = h + 2 * DEEP
    prov, vp, vs, face, mix, x_all, g_all, wk, w7, wf, perm, squares = pl.pallas_call(
        functools.partial(forward_kernel, h),
        out_shape=[
            shape((space, 2, h, nx), f32),
            shape((2, rows, nx), f32),
            shape((nx // 128, rows * 8, 128), f32),
            shape((2, h + 4, nx), f32),
            shape(((h + 4) * 32, nx), f32),
            shape((NL + 1, h + 2, C, nx), bf16),
            shape((NL + 1, h + 2 * (NL + 1), C, nx), bf16),
            shape((NL * 3, C, KW), bf16),
            shape((3, 32, KW), bf16),
            shape((C, KW), bf16),
            shape((32, 32), f32),
            shape((8, KW), f32),
        ],
        in_specs=[smem] + vmem(8),
        out_specs=vmem(5) + [any_space, any_space] + vmem(5),
        scratch_shapes=[
            pltpu.VMEM((NL + 1, deep, C, nx), bf16),
            pltpu.VMEM((NL + 1, deep, C, nx), bf16),
            pltpu.VMEM((3, 32, KW), f32),
            pltpu.VMEM((nx // 128, (h + 4) * 8, 128), f32),
            pltpu.SemaphoreType.DMA((NL + 1,)),
            pltpu.SemaphoreType.DMA((NL + 1,)),
        ],
        compiler_params=limit,
        cost_estimate=pl.CostEstimate(
            flops=2 * 7 * deep * nx * 9 * C * C, bytes_accessed=2**25, transcendentals=6 * deep * nx * C
        ),
        name="forward",
    )(me, own, up, down, packed, beside, across, diagonal, offsets)

    everywhere = lax.all_to_all(prov, "space", 0, 0, tiled=True)
    if h % 8:
        everywhere = everywhere.reshape(space * 2 * h, nx)
    constants = tables(h, space, nx)
    vel_grad, keep, send = pl.pallas_call(
        functools.partial(backward_kernel, h),
        out_shape=[shape((2, h, nx), f32)] + [shape((2, MIDROWS + 48, KW), bf16)] * 2,
        in_specs=[smem] + vmem(12) + [any_space, any_space] + vmem(5),
        out_specs=vmem(3),
        scratch_shapes=[
            pltpu.VMEM((NL + 1, h + 2, C, nx), bf16),
            pltpu.VMEM((NL + 1, h + 2 * (NL + 1), C, nx), bf16),
            pltpu.VMEM((h + 14, 32, nx), bf16),
        ]
        + [pltpu.VMEM((h + 2 * l, C, nx), bf16) for l in range(6, 0, -1)]
        + [
            pltpu.VMEM((nx // 128, (h + 2 * GPH) * 8, 128), f32),
            pltpu.VMEM((2, h + 2 * GPH, nx), f32),
            pltpu.VMEM((7, 192, KW), f32),
            pltpu.VMEM((2, h + 2 * GPH, nx), f32),
            pltpu.VMEM((nx // 128, h * 8, 128), f32),
            pltpu.SemaphoreType.DMA((NL + 1,)),
            pltpu.SemaphoreType.DMA((NL + 1,)),
        ],
        compiler_params=limit,
        cost_estimate=pl.CostEstimate(
            flops=4 * 7 * deep * nx * 9 * C * C, bytes_accessed=2**25, transcendentals=0
        ),
        name="backward",
    )(me, cot_full, *constants, vp, vs, face, mix, x_all, g_all, wk, w7, wf, perm, squares)

    new_own = pl.pallas_call(
        functools.partial(project_kernel, h),
        out_shape=shape((2 * h + 8, nx), f32),
        in_specs=[smem] + vmem(8),
        out_specs=vmem(1)[0],
        compiler_params=limit,
        cost_estimate=pl.CostEstimate(flops=2**31, bytes_accessed=2**22, transcendentals=0),
        name="project",
    )(me, everywhere, *constants)

    pair = (keep.astype(f32) + swapped(send, "chan", 1).astype(f32)).astype(bf16)
    low = (pair[0].astype(f32) + swapped(pair[1], "chan", 2).astype(f32)).astype(bf16)
    bit = 1
    while 2 * bit < space:
        low = (low.astype(f32) + swapped(low, "space", bit).astype(f32)).astype(bf16)
        bit *= 2
    other = swapped(low, "space", bit)
    news = [new_own] + [swapped(new_own, "chan", k) for k in (1, 2, 3)]

    new_velocity, w_first_grad, b_first_grad, w_mid_grad, b_mid_grad, w_last_grad, b_last_grad, rms_stats = pl.pallas_call(
        functools.partial(finish_kernel, h, 2 * traj * ny * nx),
        out_shape=[
            shape((2, traj, h, nx), f32),
            shape((3, 3, 2, 16), f32),
            shape((1, 16), f32),
            shape((NL, 3, 3, 16, C), f32),
            shape((NL, 16), f32),
            shape((3, 3, 8, C), f32),
            shape((1, 8), f32),
            shape((1, 4), f32),
        ],
        in_specs=[smem] + vmem(6),
        out_specs=vmem(8),
        scratch_shapes=[pltpu.VMEM((4, 8, KW), f32)],
        compiler_params=limit,
        name="finish",
    )(me, low, other, *news)
    return (
        new_velocity,
        vel_grad[:, None],
        w_first_grad,
        b_first_grad[0],
        jnp.swapaxes(w_mid_grad, 3, 4),
        b_mid_grad,
        jnp.swapaxes(w_last_grad, 2, 3),
        b_last_grad[0],
        rms_stats[0],
    )


def solution(mesh):
    return jax.shard_map(
        per_device,
        mesh=mesh,
        in_specs=(
            P(None, None, "space", None),
            P(None, None, None, "chan"),
            P("chan"),
            P(None, None, None, None, "chan"),
            P(None, "chan"),
            P(None, None, None, "chan"),
            P("chan"),
            P(),
            P(None, None, "space", None),
        ),
        out_specs=(
            P(None, None, "space", None),
            P(None, "chan", "space", None),
            P(None, None, None, "chan"),
            P("chan"),
            P(None, None, None, None, "chan"),
            P(None, "chan"),
            P(None, None, None, "chan"),
            P("chan"),
            P(),
        ),
        check_vma=False,
    )
```

```python
import functools

import jax
import jax.numpy as jnp
import numpy as np
from jax import lax
from jax.experimental import pallas as pl
from jax.experimental.pallas import tpu as pltpu
from jax.sharding import PartitionSpec as P

f32 = jnp.float32
bf16 = jnp.bfloat16
highest = lax.Precision.HIGHEST
time_step = 0.2
viscosity = 0.256
HALO = 16
DEEP = 12
GPH = 8
C = 64
NL = 5
KW = 256
MIDROWS = NL * 3 * 16
A0 = 0.7978845608028654
A1 = 0.044715 * A0


def basis(length):
    half = length // 2
    pos = np.arange(length)[:, None]
    table = np.zeros((length, length))
    m = np.arange(half + 1)[None, :]
    table[:, : half + 1] = np.cos(2 * np.pi * ((pos * m) % length) / length) * np.sqrt(2.0 / length)
    table[:, 0] = np.sqrt(1.0 / length)
    table[:, half] = np.cos(np.pi * pos[:, 0]) * np.sqrt(1.0 / length)
    m = np.arange(1, half)[None, :]
    table[:, half + 1 :] = np.sin(2 * np.pi * ((pos * m) % length) / length) * np.sqrt(2.0 / length)
    return table


def multipliers(ny, nx):
    def modes(n):
        half = n // 2
        index = np.arange(n)
        wave = np.where(index <= half, index, index - half) * (2 * np.pi / n)
        return wave, index <= half

    ky, cy = modes(ny)
    kx, cx = modes(nx)
    ky, cy = ky[:, None], cy[:, None]
    kx, cx = kx[None, :], cx[None, :]
    sq = kx * kx + ky * ky
    inv = np.where(sq > 0, 1.0 / np.where(sq > 0, sq, 1.0), 0.0)
    sign = np.where(cx == cy, 1.0, -1.0)
    edge_x = (kx == 0) | (kx >= np.pi - 1e-9)
    edge_y = (ky == 0) | (ky >= np.pi - 1e-9)
    mxy = np.where(edge_x | edge_y, 0.0, sign * kx * ky * inv)
    mxx = 1.0 - kx * kx * inv
    myy = 1.0 - ky * ky * inv
    return mxx, myy, mxy


def project_spectral(u, v, mxx, myy, mxy):
    half_y, half_x = u.shape[0] // 2, u.shape[1] // 2

    def swap(a):
        a = jnp.concatenate([a[:, half_x:], a[:, :half_x]], axis=1)
        return jnp.concatenate([a[half_y:], a[:half_y]], axis=0)

    rows = lax.broadcasted_iota(jnp.int32, u.shape, 0)
    cols = lax.broadcasted_iota(jnp.int32, u.shape, 1)
    corner = jnp.where((rows == half_y) & (cols == half_x), -0.5, 0.0)
    return (
        mxx * u + mxy * swap(v) + corner * v,
        myy * v + mxy * swap(u) + corner * u,
    )


def halves(x):
    high = x.astype(bf16)
    return high, (x - high.astype(f32)).astype(bf16)


def product(a, b):
    def dot(x, y):
        return jnp.dot(x, y, preferred_element_type=f32)

    return dot(a[0], b[0]) + (dot(a[1], b[0]) + dot(a[0], b[1]))


def spectrum(h, field_ref, tx_ref, ty_ref):
    ny = field_ref.shape[0] * h if h % 8 == 0 else field_ref.shape[0] // 2
    if h % 8 == 0:
        fields = [field_ref[:, c].reshape(ny, KW) for c in range(2)]
        field = jnp.concatenate(fields, axis=0)
    else:
        field = field_ref[...]
    along = product(halves(field), halves(tx_ref[...]))
    table = halves(ty_ref[...])
    if h % 8 == 0:
        return [product(table, halves(along[c * ny : (c + 1) * ny])) for c in range(2)]
    out = product(table, halves(along))
    return out[:ny], out[ny:]


def project_back(trow, u, back_ref):
    back = halves(back_ref[...])
    return product(halves(product(trow, halves(u))), back)


def gelu_both(z):
    z2 = z * z
    t = jnp.tanh(z * (A0 + A1 * z2))
    h = 0.5 * t + 0.5
    a = z * h
    return a, h + a * (1.0 - h) * (2.0 * A0 + 6.0 * A1 * z2)


def lroll(x, s):
    return pltpu.roll(x, s % x.shape[1], 1)


def shifts(x):
    return jnp.concatenate([lroll(x, 1), x, lroll(x, -1)], axis=0)


def unshifts(x):
    return jnp.concatenate([lroll(x, -1), x, lroll(x, 1)], axis=0)


def spread(ref, first, values):
    for k in range(ref.shape[0]):
        ref[k, pl.ds(first, values.shape[0], stride=8), :] = values[:, k * 128 : k * 128 + 128]


def collect(ref, first, count):
    planes = [ref[k, pl.ds(first, count, stride=8), :] for k in range(ref.shape[0])]
    return jnp.concatenate(planes, axis=1)


def rows_of(ref, first, count):
    at = pl.ds(first if isinstance(first, int) else pl.multiple_of(first, 8), count)
    return jnp.concatenate([ref[k, at, :] for k in range(ref.shape[0])], axis=1)


def put_rows(ref, first, values):
    at = pl.ds(
        first if isinstance(first, int) else pl.multiple_of(first, 8), values.shape[0]
    )
    for k in range(ref.shape[0]):
        ref[k, at, :] = values[:, k * 128 : k * 128 + 128]


def group4(s):
    i = lax.broadcasted_iota(jnp.int32, s.shape, 0)
    s = s + jnp.where(i % 2 == 0, pltpu.roll(s, 7, 0), pltpu.roll(s, 1, 0))
    return s + jnp.where((i // 2) % 2 == 0, pltpu.roll(s, 6, 0), pltpu.roll(s, 2, 0))


def point_order(offs):
    row = lax.broadcasted_iota(jnp.int32, (32, 16), 0)
    point = (row // 8) * 4 + row % 4
    comp = (row // 4) % 2
    parts = [
        jnp.where((comp == c) & (offs[c : c + 1, :] == point), 1.0, 0.0).astype(f32)
        for c in range(2)
    ]
    return jnp.concatenate(parts, axis=1)


def blocks(n, most=27):
    count = -(-n // most)
    return count, -(-n // count)


def step_kernel(
    h, me_ref, vel_ref, up_ref, down_ref, w0, w1, w2, w3, offs_ref,
    cot_ref, tx_ref, ty_ref, back_ref, trow_ref, mxx_ref, myy_ref, mxy_ref,
    prov_ref, vel_grad_ref, keep_ref, send_ref,
    vp_ref, vs_ref, face_ref, mix_ref, xb, gb, wk_ref, w7_ref, wf_ref, w7k,
    gz7, gz6, gz5, gz4, gz3, gz2, gz1, f8, adv_ref, acc_ref, gp_ref, near8,
):
    rows = h + 2 * HALO
    me = me_ref[0]
    for k, piece in enumerate((w0, w1, w2, w3)):
        slot = jnp.bitwise_xor(me, k)
        at16 = pl.ds(pl.multiple_of(slot * 16, 16), 16)
        at8 = pl.ds(pl.multiple_of(slot * 8, 8), 8)
        for n in range(NL * 3):
            wk_ref[n, at16, :] = piece[n * 16 : n * 16 + 16]
        for j in range(3):
            block = piece[MIDROWS + j * 16 : MIDROWS + j * 16 + 16].astype(f32)
            w7k[j, at8, :] = block[0:8]
        wf_ref[at16, :] = piece[MIDROWS + 48 : MIDROWS + 64]
    perm = point_order(offs_ref[...])
    perm_low = perm.astype(bf16)
    for i in range(3):
        w7_ref[i] = jnp.dot(perm_low, w7k[i].astype(bf16), preferred_element_type=f32).astype(bf16)

    vp_ref[:, 0:HALO] = up_ref[...]
    vp_ref[:, HALO : HALO + h] = vel_ref[...]
    vp_ref[:, HALO + h :] = down_ref[...]
    for c in range(2):
        plane = vp_ref[c]
        for d in range(4):
            spread(vs_ref, c * 4 + d, lroll(plane, 1 - d))

    def vs_rows(y, n):
        return rows_of(vs_ref, (y + HALO) * 8, 8 * n)

    wfirst = wf_ref[:, 0:24]
    bias = jnp.broadcast_to(wf_ref[:, 24:25].astype(f32), (C, KW))
    n = h + 2 * (DEEP - 1)
    count, size = blocks(n)

    def first_block(k, _):
        top = jnp.minimum(k * size, n - size) - (DEEP - 1)
        for r in range(size):
            y = top + r
            x = vs_rows(y - 1, 3).astype(bf16)
            z = jnp.dot(wfirst, x, preferred_element_type=f32)
            a, d = gelu_both(z + bias)
            xb[0, y + DEEP] = a.astype(bf16)
            gb[0, y + DEEP] = d.astype(bf16)
        return 0

    lax.fori_loop(0, count, first_block, 0)
    for l in range(1, NL + 1):
        weight = wk_ref[3 * (l - 1) : 3 * l].reshape(192, KW)
        bias = jnp.broadcast_to(weight[0:C, 192:193].astype(f32), (C, KW))
        weight = weight[:, 0:192]
        n = h + 2 * (DEEP - 1 - l)
        count, size = blocks(n)

        def block(k, _, l=l, weight=weight, bias=bias, n=n, size=size):
            top = jnp.minimum(k * size, n - size) - (DEEP - 1 - l) + DEEP
            p0 = p1 = None
            for r in range(-1, size + 1):
                o = jnp.dot(weight, shifts(xb[l - 1, top + r]), preferred_element_type=f32)
                if r >= 1:
                    a, d = gelu_both(p1 + o[128:192] + bias)
                    xb[l, top + r - 1] = a.astype(bf16)
                    gb[l, top + r - 1] = d.astype(bf16)
                p1 = o[64:128] if p0 is None else p0 + o[64:128]
                p0 = o[0:64]
            return 0

        lax.fori_loop(0, count, block, 0)

    weight = w7_ref[...].reshape(96, KW)
    bias = jnp.broadcast_to(weight[0:32, 192:193].astype(f32), (32, KW))
    weight = weight[:, 0:192]
    row = lax.broadcasted_iota(jnp.int32, (32, KW), 0)
    point = (row // 8) * 4 + row % 4
    second = jnp.where((row // 4) % 2 == 0, 6, 9)
    base = jnp.where((point == 5) | (point == second), 0.5, 0.0).astype(f32)
    n = h + 4
    count, size = blocks(n, 12)

    def last_block(k, _):
        top = jnp.minimum(k * size, n - size) - 2
        p0 = p1 = None
        for r in range(-1, size + 1):
            o = jnp.dot(weight, shifts(xb[NL, top + r + DEEP]), preferred_element_type=f32)
            if r >= 1:
                y = top + r - 1
                s = p1 + o[64:96] + bias
                mean = group4(s[0:8] + s[8:16] + s[16:24] + s[24:32]) * (1.0 / 16.0)
                mix = s - jnp.concatenate([mean] * 4, axis=0) + base
                mix_ref[pl.ds(pl.multiple_of((y + 2) * 32, 32), 32), :] = mix
                m = mix * vs_rows(y - 1, 4)
                m = group4(m[0:8] + m[8:16] + m[16:24] + m[24:32])
                put_rows(f8, (y + 2) * 8, m)
            p1 = o[32:64] if p0 is None else p0 + o[32:64]
            p0 = o[0:32]
        return 0

    lax.fori_loop(0, count, last_block, 0)
    for c in range(2):
        face_ref[c] = collect(f8, c * 4, h + 4)
    ue = face_ref[0, 2 : 2 + h]
    vn = face_ref[1, 2 : 2 + h]
    vn_south = face_ref[1, 1 : 1 + h]
    total = [jnp.sum(ue * ue) + jnp.sum(vn * vn)]
    own = update = 0.0
    for c in range(2):
        q = vp_ref[c, HALO : HALO + h]
        north = vp_ref[c, HALO + 1 : HALO + 1 + h]
        south = vp_ref[c, HALO - 1 : HALO - 1 + h]
        east, west = lroll(q, -1), lroll(q, 1)
        lap = east + west + north + south - 4.0 * q
        fx = ue * (q + east) * 0.5
        adv = fx - lroll(fx, 1) + vn * (q + north) * 0.5 - vn_south * (south + q) * 0.5
        new = q + time_step * (viscosity * lap - adv)
        for k in range(prov_ref.shape[0]):
            prov_ref[k, c] = new
        own = own + jnp.sum(q * q)
        update = update + jnp.sum((new - q) * (new - q))
    lane = lax.broadcasted_iota(jnp.int32, (8, KW), 1)
    squares = jnp.where(
        lane == 0, own, jnp.where(lane == 1, total[0], jnp.where(lane == 2, update, 0.0))
    )

    n = h + 2 * GPH
    u, v = spectrum(h, cot_ref, tx_ref, ty_ref)
    u, v = project_spectral(u, v, mxx_ref[...], myy_ref[...], mxy_ref[...])
    trow = halves(trow_ref[me_ref[1]])
    gp_ref[0] = project_back(trow, u, back_ref)
    gp_ref[1] = project_back(trow, v, back_ref)

    m = n - 1
    fields = []
    gue = gvn = 0.0
    for c in range(2):
        g = -time_step * gp_ref[c, 0:m]
        g_north = -time_step * gp_ref[c, 1 : m + 1]
        q = vp_ref[c, HALO - GPH : HALO - GPH + m]
        q_north = vp_ref[c, HALO - GPH + 1 : HALO - GPH + 1 + m]
        gfx = g - lroll(g, -1)
        gfy = g - g_north
        gue = gue + gfx * (q + lroll(q, -1)) * 0.5
        gvn = gvn + gfy * (q + q_north) * 0.5
        adv_ref[c, 0:m] = gfy
        fields.append(gfx[GPH : GPH + h])
    for d in range(4):
        spread(f8, d, gue)
        spread(f8, 4 + d, gvn)
    ue = face_ref[0, 2 : 2 + h]
    vn = face_ref[1, 2 : 2 + h]
    vn_south = face_ref[1, 1 : 1 + h]
    for c in range(2):
        g = gp_ref[c, GPH : GPH + h]
        lap = (
            lroll(g, -1) + lroll(g, 1) + gp_ref[c, GPH + 1 : GPH + 1 + h]
            + gp_ref[c, GPH - 1 : GPH - 1 + h] - 4.0 * g
        )
        ex = fields[c] * ue
        ny = adv_ref[c, GPH : GPH + h] * vn
        sy = adv_ref[c, GPH - 1 : GPH - 1 + h] * vn_south
        vel_grad_ref[c] = g + time_step * viscosity * lap + 0.5 * (ex + lroll(ex, 1) + ny + sy)

    def f8_row(y):
        return rows_of(f8, (y + GPH) * 8, 8)

    def stencil_row(k, _):
        for r in range(2):
            y = 2 * k + r - 7
            face = f8_row(y)
            near = vs_rows(y - 1, 4)
            s = near[0:8] + near[8:16] + near[16:24] + near[24:32]
            mean = group4(s) * (1.0 / 16.0)
            gm = (near - jnp.concatenate([mean] * 4, axis=0)) * jnp.concatenate([face] * 4, axis=0)
            gz7[y + 7] = gm.astype(bf16)
        return 0

    lax.fori_loop(0, (h + 14) // 2, stencil_row, 0, unroll=4 if h >= 16 else 1)

    ones = jnp.ones((16, KW), bf16)

    def wgrad(columns, inputs):
        return lax.dot_general(
            jnp.concatenate(columns, axis=1),
            jnp.concatenate(inputs, axis=1),
            (((1,), (1,)), ((), ())),
            preferred_element_type=f32,
        )

    gzs = {7: gz7, 6: gz6, 5: gz5, 4: gz4, 3: gz3, 2: gz2, 1: gz1}
    for l in range(7, 1, -1):
        source, target = gzs[l], gzs[l - 1]
        if l == 7:
            parts = [w7_ref[i][:, 0:192].astype(f32) for i in range(3)]
            width = 32
        else:
            parts = [wk_ref[3 * (l - 2) + i][:, 0:192].astype(f32) for i in range(3)]
            width = C
        weight = jnp.concatenate(
            [
                jnp.concatenate([p[:, j * C : (j + 1) * C].T for j in range(3)], axis=1)
                for p in parts
            ],
            axis=0,
        ).astype(bf16)
        p0 = p1 = None
        acc = None
        for ys in (range(-l, h // 2), range(h // 2, h + l)):
            columns = {y: unshifts(source[y + l]) for y in ys}
            for y in ys:
                o = jnp.dot(weight, columns[y], preferred_element_type=f32)
                if y >= 2 - l:
                    ga = p1 + o[0:64]
                    target[y - 1 + l - 1] = (ga * gb[l - 2, y - 1 + DEEP].astype(f32)).astype(bf16)
                p1 = o[64:128] if p0 is None else p0 + o[64:128]
                p0 = o[128:192]
            own = [y for y in ys if 0 <= y < h]
            part = wgrad(
                [columns[y] for y in own],
                [
                    jnp.concatenate(
                        [xb[l - 2, y + DEEP - 1 : y + DEEP + 2].reshape(192, KW), ones], axis=0
                    )
                    for y in own
                ],
            )
            acc = part if acc is None else acc + part
        if l == 7:
            back = perm
            acc = jnp.concatenate(
                [
                    lax.dot_general(
                        back, acc[j * 32 : j * 32 + 32], (((0,), (0,)), ((), ())),
                        preferred_element_type=f32, precision=highest,
                    )
                    for j in range(3)
                ],
                axis=0,
            )
        acc_ref[l - 1, 0 : 3 * width, 0:208] = acc

    wfirst = wf_ref[:, 0:32].astype(f32).T.astype(bf16)
    source = gz1
    outs = {}
    for y in range(-1, h + 1):
        outs[y] = jnp.dot(wfirst[0:24], source[y + 1], preferred_element_type=f32)
    acc_ref[0, 0:64, 0:40] = wgrad(
        [source[y + 1] for y in range(h)],
        [
            jnp.concatenate(
                [vs_rows(y - 1, 3), jnp.ones((16, KW), f32)], axis=0
            ).astype(bf16)
            for y in range(h)
        ],
    )
    for y in range(h):
        total = outs[y + 1][0:8] + outs[y][8:16] + outs[y - 1][16:24]
        for k in range(4):
            at = y + 1 - k
            total = total + f8_row(at) * mix_ref[pl.ds((at + 2) * 32 + k * 8, 8), :]
        put_rows(near8, y * 8, total)
    for c in range(2):
        total = vel_grad_ref[c]
        for d in range(4):
            total = total + lroll(collect(near8, c * 4 + d, h), d - 1)
        vel_grad_ref[c] = total

    for k, other in enumerate((0, 2, 1, 3)):
        slot = jnp.bitwise_xor(me, other)
        pack_ref = (keep_ref, send_ref)[k // 2]
        k = k % 2
        for l in range(NL):
            for j in range(3):
                piece = acc_ref[l + 1, pl.ds(pl.multiple_of(j * 64 + slot * 16, 16), 16), :]
                pack_ref[k, (3 * l + j) * 16 : (3 * l + j) * 16 + 16, :] = piece.astype(bf16)
        last = [
            acc_ref[6, pl.ds(pl.multiple_of(j * 32 + slot * 8, 8), 8), :] for j in range(3)
        ]
        pack_ref[k, MIDROWS : MIDROWS + 32, :] = jnp.concatenate(
            last + [squares], axis=0
        ).astype(bf16)
        pack_ref[k, MIDROWS + 32 : MIDROWS + 48, :] = acc_ref[
            0, pl.ds(pl.multiple_of(slot * 16, 16), 16), :
        ].astype(bf16)


def project_kernel(h, me_ref, prov_ref, tx_ref, ty_ref, back_ref, trow_ref, mxx_ref, myy_ref, mxy_ref, out_ref):
    me_space = me_ref[1]
    trow = halves(trow_ref[me_space][GPH : GPH + h])
    u, v = spectrum(h, prov_ref, tx_ref, ty_ref)
    u, v = project_spectral(u, v, mxx_ref[...], myy_ref[...], mxy_ref[...])
    out_ref[0:h] = project_back(trow, u, back_ref)
    out_ref[h : 2 * h] = project_back(trow, v, back_ref)
    out_ref[2 * h :] = jnp.full((8, KW), jnp.sum(u * u) + jnp.sum(v * v), f32)


def prepare_kernel(h, me_ref, vel_ref, cot_ref, wm_ref, wl_ref, wf_ref, bm_ref, bf_ref, bl_ref, pack_ref, own_ref, top_ref, bottom_ref, cot_all_ref, tall, wide):
    me = me_ref[0]
    own = vel_ref[:, me]
    own_ref[...] = own
    if h >= HALO:
        top_ref[...] = own[:, :HALO]
        bottom_ref[...] = own[:, h - HALO :]
    cot = cot_ref[:, me]
    for k in range(cot_all_ref.shape[0]):
        cot_all_ref[k] = cot
    wide[...] = jnp.zeros_like(wide)
    wide[0:NL, 0:16] = bm_ref[...].astype(f32)
    wide[NL : NL + 1, 0:16] = bf_ref[...].astype(f32)
    wide[NL + 1 : NL + 2, 0:8] = bl_ref[...].astype(f32)
    columns = wide[...].T

    def column(k, count, width):
        return jnp.broadcast_to(columns[0:count, k : k + 1], (count, width))

    for l in range(NL):
        for i in range(3):
            parts = [wm_ref[l, i, j] for j in range(3)] + [column(l, 16, 64).astype(bf16)]
            at = (3 * l + i) * 16
            pack_ref[at : at + 16, :] = jnp.concatenate(parts, axis=1)
    for i in range(3):
        parts = [wl_ref[i, j].astype(f32) for j in range(3)] + [column(NL + 1, 8, 64)]
        block = jnp.concatenate(parts, axis=1)
        at = MIDROWS + i * 16
        pack_ref[at : at + 16, :] = jnp.concatenate([block, jnp.zeros_like(block)], axis=0).astype(bf16)
    tall[...] = jnp.zeros_like(tall)
    for i in range(3):
        for j in range(3):
            taps = wf_ref[i, j].astype(f32)
            for c in range(2):
                at = i * 8 + c * 4 + j
                tall[at : at + 1, 0:16] = taps[c : c + 1]
    tall[24:25, 0:16] = bf_ref[...].astype(f32)
    first = tall[...].T[0:16]
    pack_ref[MIDROWS + 48 :, :] = jnp.concatenate([first, jnp.zeros_like(first)], axis=1).astype(bf16)


def finish_kernel(h, cells, me_ref, low_ref, other_ref, n0, n1, n2, n3, new_ref, wf_ref, bf_ref, wm_ref, bm_ref, wl_ref, bl_ref, rms_ref, parts):
    me = me_ref[0]
    for k, piece in enumerate((n0, n1, n2, n3)):
        slot = jnp.bitwise_xor(me, k)
        new_ref[0, slot] = piece[0:h]
        new_ref[1, slot] = piece[h : 2 * h]
        parts[slot] = piece[2 * h :]

    def total(at, count):
        return low_ref[at : at + count, :].astype(f32) + other_ref[at : at + count, :].astype(f32)

    def turned(block):
        return jnp.concatenate([block, jnp.zeros((128 - block.shape[0], 128), f32)], axis=0).T

    for l in range(NL):
        for j in range(3):
            block = total((3 * l + j) * 16, 16)
            for i in range(3):
                wm_ref[l, i, j] = block[:, i * 64 : i * 64 + 64]
            if j == 0:
                bm_ref[l : l + 1, :] = turned(block[:, 128:256])[64:65, 0:16]
    tail = total(MIDROWS, 32)
    for j in range(3):
        block = tail[j * 8 : j * 8 + 8]
        for i in range(3):
            wl_ref[i, j] = block[:, i * 64 : i * 64 + 64]
        if j == 0:
            bl_ref[...] = turned(block[:, 128:256])[64:65, 0:8]
    first = turned(total(MIDROWS + 32, 16)[:, 0:128])
    for i in range(3):
        for j in range(3):
            for c in range(2):
                at = i * 8 + c * 4 + j
                wf_ref[i, j, c : c + 1, :] = first[at : at + 1, 0:16]
    bf_ref[...] = first[24:25, 0:16]
    news = (parts[0] + parts[1]) + (parts[2] + parts[3])
    lane = lax.broadcasted_iota(jnp.int32, (8, 128), 1)
    sums = jnp.where(lane == 3, news[:, 0:128], tail[24:32, 0:128])
    rms_ref[...] = jnp.sqrt(sums * (1.0 / cells))[0:1, 0:4]


def moved(x, axis, step):
    n = lax.axis_size(axis)
    return lax.ppermute(x, axis, [(i, (i + step) % n) for i in range(n)])


def swapped(x, axis, bit):
    n = lax.axis_size(axis)
    return lax.ppermute(x, axis, [(i, i ^ bit) for i in range(n)])


def halos(own, top, bottom, width):
    height = own.shape[1]
    if height >= width:
        return moved(bottom, "space", 1), moved(top, "space", -1)
    hops = -(-width // height)
    up = jnp.concatenate([moved(own, "space", k) for k in range(hops, 0, -1)], axis=1)
    down = jnp.concatenate([moved(own, "space", -k) for k in range(1, hops + 1)], axis=1)
    return up[:, up.shape[1] - width :], down[:, :width]


def tables(h, space, nx):
    ny = h * space
    ty, tx = basis(ny), basis(nx)

    def held(table):
        return jnp.asarray(np.ascontiguousarray(table).astype(np.float32))

    back_y = ty.T
    if h % 8:
        wide = np.zeros((2, ny, space, 2, h))
        for c in range(2):
            wide[c, :, :, c, :] = ty.T.reshape(ny, space, h)
        back_y = wide.reshape(2 * ny, 2 * ny)
    ring = (np.arange(space)[:, None] * h + np.arange(h + 2 * GPH)[None, :] - GPH) % ny
    spectral = [jnp.asarray(m.astype(np.float32)) for m in multipliers(ny, nx)]
    return [held(tx), held(back_y), held(tx.T), held(ty[ring])] + spectral


def vmem(count):
    return [pl.BlockSpec(memory_space=pltpu.VMEM)] * count


def per_device(velocity, w_first, b_first, w_mid, b_mid, w_last, b_last, offsets, cotangent):
    traj, h, nx = velocity.shape[1:]
    space = lax.axis_size("space")
    ny = h * space
    me_chan = lax.axis_index("chan")
    me_space = lax.axis_index("space")
    me = jnp.stack([me_chan, me_space]).astype(jnp.int32)
    rows = h + 2 * HALO
    shape = jax.ShapeDtypeStruct
    smem = pl.BlockSpec(memory_space=pltpu.SMEM)
    inside = pltpu.VMEM

    def limit(mebibytes):
        return pltpu.CompilerParams(vmem_limit_bytes=mebibytes * 2**20)

    def outside(x):
        return pltpu.with_memory_space_constraint(x, pltpu.HBM)

    packed, own, top, bottom, cot_all = pl.pallas_call(
        functools.partial(prepare_kernel, h),
        out_shape=[
            inside((MIDROWS + 64, KW), bf16),
            inside((2, h, nx), f32),
            inside((2, min(h, HALO), nx), f32),
            inside((2, min(h, HALO), nx), f32),
            inside((space, 2, h, nx), f32),
        ],
        in_specs=[smem] + vmem(8),
        out_specs=vmem(5),
        scratch_shapes=[pltpu.VMEM((128, 128), f32), pltpu.VMEM((8, 128), f32)],
        compiler_params=limit(16),
        name="prepare",
    )(
        me,
        *[
            outside(x)
            for x in (
                velocity, cotangent, jnp.swapaxes(w_mid, 3, 4), jnp.swapaxes(w_last, 2, 3),
                w_first, b_mid, b_first[None], b_last[None],
            )
        ],
    )
    across = swapped(packed, "chan", 2)
    up, down = halos(own, top, bottom, HALO)
    across, up, down = lax.optimization_barrier((across, up, down))
    beside = swapped(packed, "chan", 1)
    diagonal = swapped(across, "chan", 1)
    cot_full = lax.all_to_all(cot_all, "space", 0, 0, tiled=True)
    if h % 8:
        cot_full = cot_full.reshape(space * 2 * h, nx)

    deep = h + 2 * DEEP
    constants = [outside(x) for x in tables(h, space, nx)]
    prov, vel_grad, keep, send = pl.pallas_call(
        functools.partial(step_kernel, h),
        out_shape=[inside((space, 2, h, nx), f32), shape((2, h, nx), f32)]
        + [inside((2, MIDROWS + 48, KW), bf16)] * 2,
        in_specs=[smem] + vmem(16),
        out_specs=vmem(4),
        scratch_shapes=[
            inside((2, rows, nx), f32),
            inside((nx // 128, rows * 8, 128), f32),
            inside((2, h + 4, nx), f32),
            inside(((h + 4) * 32, nx), f32),
            inside((NL + 1, deep, C, nx), bf16),
            inside((NL + 1, deep, C, nx), bf16),
            inside((NL * 3, C, KW), bf16),
            inside((3, 32, KW), bf16),
            inside((C, KW), bf16),
            inside((3, 32, KW), f32),
            inside((h + 14, 32, nx), bf16),
        ]
        + [inside((h + 2 * l, C, nx), bf16) for l in range(6, 0, -1)]
        + [
            inside((nx // 128, (h + 2 * GPH) * 8, 128), f32),
            inside((2, h + 2 * GPH, nx), f32),
            inside((7, 192, KW), f32),
            inside((2, h + 2 * GPH, nx), f32),
            inside((nx // 128, h * 8, 128), f32),
        ],
        compiler_params=limit(52),
        cost_estimate=pl.CostEstimate(
            flops=6 * 7 * deep * nx * 9 * C * C, bytes_accessed=2**25, transcendentals=6 * deep * nx * C
        ),
        name="step",
    )(me, own, up, down, packed, beside, across, diagonal, outside(offsets), cot_full, *constants)
    everywhere = lax.all_to_all(prov, "space", 0, 0, tiled=True)
    if h % 8:
        everywhere = everywhere.reshape(space * 2 * h, nx)

    new_own = pl.pallas_call(
        functools.partial(project_kernel, h),
        out_shape=inside((2 * h + 8, nx), f32),
        in_specs=[smem] + vmem(8),
        out_specs=vmem(1)[0],
        compiler_params=limit(16),
        cost_estimate=pl.CostEstimate(flops=2**31, bytes_accessed=2**22, transcendentals=0),
        name="project",
    )(me, everywhere, *constants)

    pair = (keep.astype(f32) + swapped(send, "chan", 1).astype(f32)).astype(bf16)
    low = (pair[0].astype(f32) + swapped(pair[1], "chan", 2).astype(f32)).astype(bf16)
    bit = 1
    while 2 * bit < space:
        low = (low.astype(f32) + swapped(low, "space", bit).astype(f32)).astype(bf16)
        bit *= 2
    other = swapped(low, "space", bit)
    news = [new_own] + [swapped(new_own, "chan", k) for k in (1, 2, 3)]

    new_velocity, w_first_grad, b_first_grad, w_mid_grad, b_mid_grad, w_last_grad, b_last_grad, rms_stats = pl.pallas_call(
        functools.partial(finish_kernel, h, 2 * traj * ny * nx),
        out_shape=[
            shape((2, traj, h, nx), f32),
            shape((3, 3, 2, 16), f32),
            shape((1, 16), f32),
            shape((NL, 3, 3, 16, C), f32),
            shape((NL, 16), f32),
            shape((3, 3, 8, C), f32),
            shape((1, 8), f32),
            shape((1, 4), f32),
        ],
        in_specs=[smem] + vmem(6),
        out_specs=vmem(8),
        scratch_shapes=[pltpu.VMEM((4, 8, KW), f32)],
        compiler_params=limit(16),
        name="finish",
    )(me, low, other, *news)
    return (
        new_velocity,
        vel_grad[:, None],
        w_first_grad,
        b_first_grad[0],
        jnp.swapaxes(w_mid_grad, 3, 4),
        b_mid_grad,
        jnp.swapaxes(w_last_grad, 2, 3),
        b_last_grad[0],
        rms_stats[0],
    )


def solution(mesh):
    return jax.shard_map(
        per_device,
        mesh=mesh,
        in_specs=(
            P(None, None, "space", None),
            P(None, None, None, "chan"),
            P("chan"),
            P(None, None, None, None, "chan"),
            P(None, "chan"),
            P(None, None, None, "chan"),
            P("chan"),
            P(),
            P(None, None, "space", None),
        ),
        out_specs=(
            P(None, None, "space", None),
            P(None, "chan", "space", None),
            P(None, None, None, "chan"),
            P("chan"),
            P(None, None, None, None, "chan"),
            P(None, "chan"),
            P(None, None, None, "chan"),
            P("chan"),
            P(),
        ),
        check_vma=False,
    )
```

```python
import functools

import jax
import jax.numpy as jnp
import numpy as np
from jax import lax
from jax.experimental import pallas as pl
from jax.experimental.pallas import tpu as pltpu
from jax.sharding import PartitionSpec as P

f32 = jnp.float32
bf16 = jnp.bfloat16
highest = lax.Precision.HIGHEST
time_step = 0.2
viscosity = 0.256
HALO = 16
DEEP = 12
GPH = 8
C = 64
NL = 5
KW = 256
MIDROWS = NL * 3 * 16
TAILS = MIDROWS
LAST = TAILS + 128
FIRST = LAST + 48
SUMROWS = FIRST + 16
A0 = 0.7978845608028654
A1 = 0.044715 * A0


def basis(length):
    half = length // 2
    pos = np.arange(length)[:, None]
    table = np.zeros((length, length))
    m = np.arange(half + 1)[None, :]
    table[:, : half + 1] = np.cos(2 * np.pi * ((pos * m) % length) / length) * np.sqrt(2.0 / length)
    table[:, 0] = np.sqrt(1.0 / length)
    table[:, half] = np.cos(np.pi * pos[:, 0]) * np.sqrt(1.0 / length)
    m = np.arange(1, half)[None, :]
    table[:, half + 1 :] = np.sin(2 * np.pi * ((pos * m) % length) / length) * np.sqrt(2.0 / length)
    return table


def multipliers(ny, nx):
    def modes(n):
        half = n // 2
        index = np.arange(n)
        wave = np.where(index <= half, index, index - half) * (2 * np.pi / n)
        return wave, index <= half

    ky, cy = modes(ny)
    kx, cx = modes(nx)
    ky, cy = ky[:, None], cy[:, None]
    kx, cx = kx[None, :], cx[None, :]
    sq = kx * kx + ky * ky
    inv = np.where(sq > 0, 1.0 / np.where(sq > 0, sq, 1.0), 0.0)
    sign = np.where(cx == cy, 1.0, -1.0)
    edge_x = (kx == 0) | (kx >= np.pi - 1e-9)
    edge_y = (ky == 0) | (ky >= np.pi - 1e-9)
    mxy = np.where(edge_x | edge_y, 0.0, sign * kx * ky * inv)
    mxx = 1.0 - kx * kx * inv
    myy = 1.0 - ky * ky * inv
    return mxx, myy, mxy


def project_spectral(u, v, mxx, myy, mxy):
    half_y, half_x = u.shape[0] // 2, u.shape[1] // 2

    def swap(a):
        a = jnp.concatenate([a[:, half_x:], a[:, :half_x]], axis=1)
        return jnp.concatenate([a[half_y:], a[:half_y]], axis=0)

    rows = lax.broadcasted_iota(jnp.int32, u.shape, 0)
    cols = lax.broadcasted_iota(jnp.int32, u.shape, 1)
    corner = jnp.where((rows == half_y) & (cols == half_x), -0.5, 0.0)
    return (
        mxx * u + mxy * swap(v) + corner * v,
        myy * v + mxy * swap(u) + corner * u,
    )


def halves(x):
    high = x.astype(bf16)
    return high, (x - high.astype(f32)).astype(bf16)


def product(a, b):
    def dot(x, y):
        return jnp.dot(x, y, preferred_element_type=f32)

    return dot(a[0], b[0]) + (dot(a[1], b[0]) + dot(a[0], b[1]))


def spectrum(h, field_ref, tx_ref, ty_ref):
    ny = field_ref.shape[0] * h if h % 8 == 0 else field_ref.shape[0] // 2
    if h % 8 == 0:
        fields = [field_ref[:, c].reshape(ny, KW) for c in range(2)]
        field = jnp.concatenate(fields, axis=0).astype(f32)
    else:
        field = field_ref[...].astype(f32)
    along = product(halves(field), halves(tx_ref[...]))
    table = halves(ty_ref[...])
    if h % 8 == 0:
        return [product(table, halves(along[c * ny : (c + 1) * ny])) for c in range(2)]
    out = product(table, halves(along))
    return out[:ny], out[ny:]


def project_back(trow, u, back_ref):
    back = halves(back_ref[...])
    return product(halves(product(trow, halves(u))), back)


def gelu(z):
    t = jnp.tanh(z * (A0 + A1 * (z * z)))
    return z * (0.5 * t + 0.5)


def gelu_slope(z):
    z2 = z * z
    t = jnp.tanh(z * (A0 + A1 * z2))
    return (0.5 * t + 0.5) + (z * (0.5 * A0 + 1.5 * A1 * z2)) * (1.0 - t * t)


def lroll(x, s):
    return pltpu.roll(x, s % x.shape[1], 1)


def shifts(x):
    return jnp.concatenate([lroll(x, 1), x, lroll(x, -1)], axis=0)


def unshifts(x):
    return jnp.concatenate([lroll(x, -1), x, lroll(x, 1)], axis=0)


def spread(ref, first, values):
    for k in range(ref.shape[0]):
        ref[k, pl.ds(first, values.shape[0], stride=8), :] = values[:, k * 128 : k * 128 + 128]


def collect(ref, first, count):
    planes = [ref[k, pl.ds(first, count, stride=8), :] for k in range(ref.shape[0])]
    return jnp.concatenate(planes, axis=1)


def rows_of(ref, first, count):
    at = pl.ds(first if isinstance(first, int) else pl.multiple_of(first, 8), count)
    return jnp.concatenate([ref[k, at, :] for k in range(ref.shape[0])], axis=1)


def put_rows(ref, first, values):
    at = pl.ds(
        first if isinstance(first, int) else pl.multiple_of(first, 8), values.shape[0]
    )
    for k in range(ref.shape[0]):
        ref[k, at, :] = values[:, k * 128 : k * 128 + 128]


def group4(s):
    i = lax.broadcasted_iota(jnp.int32, s.shape, 0)
    s = s + jnp.where(i % 2 == 0, pltpu.roll(s, 7, 0), pltpu.roll(s, 1, 0))
    return s + jnp.where((i // 2) % 2 == 0, pltpu.roll(s, 6, 0), pltpu.roll(s, 2, 0))


def point_order(offs):
    row = lax.broadcasted_iota(jnp.int32, (32, 16), 0)
    point = (row // 8) * 4 + row % 4
    comp = (row // 4) % 2
    parts = [
        jnp.where((comp == c) & (offs[c : c + 1, :] == point), 1.0, 0.0).astype(f32)
        for c in range(2)
    ]
    return jnp.concatenate(parts, axis=1)


def blocks(n, most=27):
    count = -(-n // most)
    return count, -(-n // count)


def step_kernel(
    h, vel_ref, up_ref, down_ref, w0, w1, w2, w3, offs_ref,
    cot_ref, *rest,
):
    held = rest[:7]
    (
    prov_ref, vel_grad_ref, keep_ref, send_ref,
    tx_ref, ty_ref, back_ref, trow_ref, mxx_ref, myy_ref, mxy_ref,
    vp_ref, vs_ref, face_ref, mix_ref, xb, zb, wk_ref, w7_ref, wf_ref, w7k,
    gz7, gz6, gz5, gz4, gz3, gz2, gz1, f8, adv_ref, acc_ref, gp_ref, near8, sems,
    ) = rest[7:]
    loads = [
        pltpu.make_async_copy(table.at[lax.axis_index("space")] if k == 3 else table, place, sems.at[k])
        for k, (table, place) in enumerate(
            zip(held, (tx_ref, ty_ref, back_ref, trow_ref, mxx_ref, myy_ref, mxy_ref))
        )
    ]
    for load in loads:
        load.start()
    rows = h + 2 * HALO
    me = lax.axis_index("chan")
    for k, piece in enumerate((w0, w1, w2, w3)):
        slot = jnp.bitwise_xor(me, k)
        at16 = pl.ds(pl.multiple_of(slot * 16, 16), 16)
        at8 = pl.ds(pl.multiple_of(slot * 8, 8), 8)
        for n in range(NL * 3):
            wk_ref[n, at16, :] = piece[n * 16 : n * 16 + 16]
        for j in range(3):
            block = piece[MIDROWS + j * 16 : MIDROWS + j * 16 + 16].astype(f32)
            w7k[j, at8, :] = block[0:8]
        wf_ref[at16, :] = piece[MIDROWS + 48 : MIDROWS + 64]
    perm = point_order(offs_ref[...])
    perm_low = perm.astype(bf16)
    for i in range(3):
        w7_ref[i] = jnp.dot(perm_low, w7k[i].astype(bf16), preferred_element_type=f32).astype(bf16)

    vp_ref[:, 0:HALO] = up_ref[...]
    vp_ref[:, HALO : HALO + h] = vel_ref[...]
    vp_ref[:, HALO + h :] = down_ref[...]
    for c in range(2):
        plane = vp_ref[c]
        for d in range(4):
            spread(vs_ref, c * 4 + d, lroll(plane, 1 - d))

    def vs_rows(y, n):
        return rows_of(vs_ref, (y + HALO) * 8, 8 * n)

    ones = jnp.ones((16, KW), bf16)

    wfirst = wf_ref[:, 0:32]
    n = h + 2 * (DEEP - 1)
    count, size = blocks(n)

    def first_block(k, _):
        top = k * size - (DEEP - 1)
        for r in range(size):
            y = top + r
            x = jnp.concatenate([vs_rows(y - 1, 3), jnp.ones((8, KW), f32)], axis=0)
            z = jnp.dot(wfirst, x.astype(bf16), preferred_element_type=f32)
            zb[0, y + DEEP] = z
            xb[0, y + DEEP] = gelu(z).astype(bf16)
        return 0

    lax.fori_loop(0, count, first_block, 0)

    def rows_through(source, weight, width, first, n, most, done):
        count, size = blocks(n, most)

        def taps(row):
            x = jnp.concatenate([shifts(source(row)), ones], axis=0)
            o = jnp.dot(weight, x, preferred_element_type=f32)
            return [o[i * width : (i + 1) * width] for i in range(3)]

        def block(k, carry):
            p0, p1 = carry
            for r in range(size):
                row = first + k * size + r
                o = taps(row + 1)
                done(row, p1 + o[2])
                p0, p1 = o[0], p0 + o[1]
            return p0, p1

        before, here = taps(first - 1), taps(first)
        lax.fori_loop(0, count, block, (here[0], before[0] + here[1]))

    for l in range(1, NL + 1):

        def done(row, z, l=l):
            zb[l, row] = z
            xb[l, row] = gelu(z).astype(bf16)

        rows_through(
            lambda row, l=l: xb[l - 1, row],
            wk_ref[3 * (l - 1) : 3 * l].reshape(192, KW)[:, 0:208],
            C, 1 + l, h + 2 * (DEEP - 1 - l), 27, done,
        )

    row = lax.broadcasted_iota(jnp.int32, (32, KW), 0)
    point = (row // 8) * 4 + row % 4
    second = jnp.where((row // 4) % 2 == 0, 6, 9)
    base = jnp.where((point == 5) | (point == second), 0.5, 0.0).astype(f32)

    def mixed(row, s):
        y = row - DEEP
        mean = group4(s[0:8] + s[8:16] + s[16:24] + s[24:32]) * (1.0 / 16.0)
        mix = s - jnp.concatenate([mean] * 4, axis=0) + base
        mix_ref[pl.ds(pl.multiple_of((y + 2) * 32, 32), 32), :] = mix
        m = mix * vs_rows(y - 1, 4)
        m = group4(m[0:8] + m[8:16] + m[16:24] + m[24:32])
        put_rows(f8, (y + 2) * 8, m)

    rows_through(
        lambda row: xb[NL, row], w7_ref[...].reshape(96, KW)[:, 0:208], 32, DEEP - 2, h + 4, 18, mixed
    )
    for c in range(2):
        face_ref[c] = collect(f8, c * 4, h + 4)
    ue = face_ref[0, 2 : 2 + h]
    vn = face_ref[1, 2 : 2 + h]
    vn_south = face_ref[1, 1 : 1 + h]
    total = [jnp.sum(ue * ue) + jnp.sum(vn * vn)]
    own = update = 0.0
    for c in range(2):
        q = vp_ref[c, HALO : HALO + h]
        north = vp_ref[c, HALO + 1 : HALO + 1 + h]
        south = vp_ref[c, HALO - 1 : HALO - 1 + h]
        east, west = lroll(q, -1), lroll(q, 1)
        lap = east + west + north + south - 4.0 * q
        fx = ue * (q + east) * 0.5
        adv = fx - lroll(fx, 1) + vn * (q + north) * 0.5 - vn_south * (south + q) * 0.5
        new = q + time_step * (viscosity * lap - adv)
        for k in range(prov_ref.shape[0]):
            prov_ref[k, c] = new.astype(prov_ref.dtype)
        own = own + jnp.sum(q * q)
        update = update + jnp.sum((new - q) * (new - q))
    lane = lax.broadcasted_iota(jnp.int32, (8, KW), 1)
    squares = jnp.where(
        lane == 0, own, jnp.where(lane == 1, total[0], jnp.where(lane == 2, update, 0.0))
    )

    for load in loads:
        load.wait()

    n = h + 2 * GPH
    u, v = spectrum(h, cot_ref, tx_ref, ty_ref)
    u, v = project_spectral(u, v, mxx_ref[...], myy_ref[...], mxy_ref[...])
    trow = halves(trow_ref[...])
    gp_ref[0] = project_back(trow, u, back_ref)
    gp_ref[1] = project_back(trow, v, back_ref)

    m = n - 1
    fields = []
    gue = gvn = 0.0
    for c in range(2):
        g = -time_step * gp_ref[c, 0:m]
        g_north = -time_step * gp_ref[c, 1 : m + 1]
        q = vp_ref[c, HALO - GPH : HALO - GPH + m]
        q_north = vp_ref[c, HALO - GPH + 1 : HALO - GPH + 1 + m]
        gfx = g - lroll(g, -1)
        gfy = g - g_north
        gue = gue + gfx * (q + lroll(q, -1)) * 0.5
        gvn = gvn + gfy * (q + q_north) * 0.5
        adv_ref[c, 0:m] = gfy
        fields.append(gfx[GPH : GPH + h])
    for d in range(4):
        spread(f8, d, gue)
        spread(f8, 4 + d, gvn)
    ue = face_ref[0, 2 : 2 + h]
    vn = face_ref[1, 2 : 2 + h]
    vn_south = face_ref[1, 1 : 1 + h]
    for c in range(2):
        g = gp_ref[c, GPH : GPH + h]
        lap = (
            lroll(g, -1) + lroll(g, 1) + gp_ref[c, GPH + 1 : GPH + 1 + h]
            + gp_ref[c, GPH - 1 : GPH - 1 + h] - 4.0 * g
        )
        ex = fields[c] * ue
        ny = adv_ref[c, GPH : GPH + h] * vn
        sy = adv_ref[c, GPH - 1 : GPH - 1 + h] * vn_south
        vel_grad_ref[c] = g + time_step * viscosity * lap + 0.5 * (ex + lroll(ex, 1) + ny + sy)

    def f8_row(y):
        return rows_of(f8, (y + GPH) * 8, 8)

    def stencil_row(k, _):
        for r in range(2):
            y = 2 * k + r - 7
            face = f8_row(y)
            near = vs_rows(y - 1, 4)
            s = near[0:8] + near[8:16] + near[16:24] + near[24:32]
            mean = group4(s) * (1.0 / 16.0)
            gm = (near - jnp.concatenate([mean] * 4, axis=0)) * jnp.concatenate([face] * 4, axis=0)
            gz7[y + 7] = gm.astype(bf16)
        return 0

    lax.fori_loop(0, (h + 14) // 2, stencil_row, 0, unroll=4 if h >= 16 else 1)

    def wgrad(columns, inputs):
        return lax.dot_general(
            jnp.concatenate(columns, axis=1),
            jnp.concatenate(inputs, axis=1),
            (((1,), (1,)), ((), ())),
            preferred_element_type=f32,
        )

    gzs = {7: gz7, 6: gz6, 5: gz5, 4: gz4, 3: gz3, 2: gz2, 1: gz1}
    for l in range(7, 1, -1):
        source, target = gzs[l], gzs[l - 1]
        if l == 7:
            parts = [w7_ref[i][:, 0:192].astype(f32) for i in range(3)]
            width = 32
        else:
            parts = [wk_ref[3 * (l - 2) + i][:, 0:192].astype(f32) for i in range(3)]
            width = C
        weight = jnp.concatenate(
            [
                jnp.concatenate([p[:, j * C : (j + 1) * C].T for j in range(3)], axis=1)
                for p in parts
            ],
            axis=0,
        ).astype(bf16)
        p0 = p1 = None
        acc = None
        for ys in (range(-l, h // 2), range(h // 2, h + l)):
            columns = {y: unshifts(source[y + l]) for y in ys}
            for y in ys:
                o = jnp.dot(weight, columns[y], preferred_element_type=f32)
                if y >= 2 - l:
                    ga = p1 + o[0:64]
                    slope = gelu_slope(zb[l - 2, y - 1 + DEEP])
                    target[y - 1 + l - 1] = (ga * slope).astype(bf16)
                p1 = o[64:128] if p0 is None else p0 + o[64:128]
                p0 = o[128:192]
            own = [y for y in ys if 0 <= y < h]
            part = wgrad(
                [columns[y] for y in own],
                [
                    jnp.concatenate(
                        [xb[l - 2, y + DEEP - 1 : y + DEEP + 2].reshape(192, KW), ones], axis=0
                    )
                    for y in own
                ],
            )
            acc = part if acc is None else acc + part
        if l == 7:
            back = perm
            acc = jnp.concatenate(
                [
                    lax.dot_general(
                        back, acc[j * 32 : j * 32 + 32], (((0,), (0,)), ((), ())),
                        preferred_element_type=f32, precision=highest,
                    )
                    for j in range(3)
                ],
                axis=0,
            )
        acc_ref[l - 1, 0 : 3 * width, 0:208] = acc

    wfirst = wf_ref[:, 0:32].astype(f32).T.astype(bf16)
    source = gz1
    outs = {}
    for y in range(-1, h + 1):
        outs[y] = jnp.dot(wfirst[0:24], source[y + 1], preferred_element_type=f32)
    acc_ref[0, 0:64, 0:40] = wgrad(
        [source[y + 1] for y in range(h)],
        [
            jnp.concatenate(
                [vs_rows(y - 1, 3), jnp.ones((16, KW), f32)], axis=0
            ).astype(bf16)
            for y in range(h)
        ],
    )
    for y in range(h):
        total = outs[y + 1][0:8] + outs[y][8:16] + outs[y - 1][16:24]
        for k in range(4):
            at = y + 1 - k
            total = total + f8_row(at) * mix_ref[pl.ds((at + 2) * 32 + k * 8, 8), :]
        put_rows(near8, y * 8, total)
    for c in range(2):
        total = vel_grad_ref[c]
        for d in range(4):
            total = total + lroll(collect(near8, c * 4 + d, h), d - 1)
        vel_grad_ref[c] = total

    lane = lax.broadcasted_iota(jnp.int32, (16, 64), 1)
    for k, other in enumerate((0, 2, 1, 3)):
        slot = jnp.bitwise_xor(me, other)
        pack_ref = (keep_ref, send_ref)[k // 2]
        k = k % 2
        tails = []
        bias = jnp.zeros((16, 64), f32)
        for l in range(NL):
            for j in range(3):
                piece = acc_ref[l + 1, pl.ds(pl.multiple_of(j * 64 + slot * 16, 16), 16), :]
                at = (3 * l + j) * 16
                pack_ref[k, at : at + 16, :] = piece[:, 0:128].astype(bf16)
                tails.append(piece[:, 128:192])
                if j == 0:
                    bias = jnp.where(lane == l, jnp.broadcast_to(piece[:, 192:193], (16, 64)), bias)
        tails.append(bias)
        for n in range(8):
            at = TAILS + 16 * n
            pack_ref[k, at : at + 16, :] = jnp.concatenate(tails[2 * n : 2 * n + 2], axis=1).astype(bf16)
        last = [
            acc_ref[6, pl.ds(pl.multiple_of(j * 32 + slot * 8, 8), 8), :] for j in range(3)
        ]
        tails = [p[:, 128:192] for p in last]
        tails.append(jnp.broadcast_to(last[0][:, 192:193], (8, 64)))
        groups = [p[:, 0:128] for p in last]
        groups += [jnp.concatenate(tails[0:2], axis=1), jnp.concatenate(tails[2:4], axis=1)]
        groups.append(squares[:, 0:128])
        pack_ref[k, LAST:FIRST, :] = jnp.concatenate(groups, axis=0).astype(bf16)
        pack_ref[k, FIRST:SUMROWS, :] = acc_ref[
            0, pl.ds(pl.multiple_of(slot * 16, 16), 16), 0:128
        ].astype(bf16)


def project_kernel(h, prov_ref, tx_ref, ty_ref, back_ref, trow_ref, mxx_ref, myy_ref, mxy_ref, out_ref):
    trow = halves(trow_ref[GPH : GPH + h])
    u, v = spectrum(h, prov_ref, tx_ref, ty_ref)
    u, v = project_spectral(u, v, mxx_ref[...], myy_ref[...], mxy_ref[...])
    out_ref[0:h] = project_back(trow, u, back_ref)
    out_ref[h : 2 * h] = project_back(trow, v, back_ref)
    out_ref[2 * h :] = jnp.full((8, KW), jnp.sum(u * u) + jnp.sum(v * v), f32)


def prepare_kernel(h, vel_ref, wm_ref, wl_ref, wf_ref, bm_ref, bf_ref, bl_ref, pack_ref, own_ref, top_ref, bottom_ref, tall, wide):
    me = lax.axis_index("chan")
    own = vel_ref[:, me]
    own_ref[...] = own
    if h >= HALO:
        top_ref[...] = own[:, :HALO]
        bottom_ref[...] = own[:, h - HALO :]
    wide[...] = jnp.zeros_like(wide)
    wide[0:NL, 0:16] = bm_ref[...].astype(f32)
    wide[NL : NL + 1, 0:16] = bf_ref[...].astype(f32)
    wide[NL + 1 : NL + 2, 0:8] = bl_ref[...].astype(f32)
    columns = wide[...].T

    def column(k, count, i):
        lane = lax.broadcasted_iota(jnp.int32, (count, 64), 1)
        here = jnp.broadcast_to(columns[0:count, k : k + 1], (count, 64))
        return jnp.where((lane == 0) & (i == 1), here, 0.0)

    for l in range(NL):
        for i in range(3):
            parts = [wm_ref[l, i, j] for j in range(3)] + [column(l, 16, i).astype(bf16)]
            at = (3 * l + i) * 16
            pack_ref[at : at + 16, :] = jnp.concatenate(parts, axis=1)
    for i in range(3):
        parts = [wl_ref[i, j].astype(f32) for j in range(3)] + [column(NL + 1, 8, i)]
        block = jnp.concatenate(parts, axis=1)
        at = MIDROWS + i * 16
        pack_ref[at : at + 16, :] = jnp.concatenate([block, jnp.zeros_like(block)], axis=0).astype(bf16)
    tall[...] = jnp.zeros_like(tall)
    for i in range(3):
        for j in range(3):
            taps = wf_ref[i, j].astype(f32)
            for c in range(2):
                at = i * 8 + c * 4 + j
                tall[at : at + 1, 0:16] = taps[c : c + 1]
    tall[24:25, 0:16] = bf_ref[...].astype(f32)
    first = tall[...].T[0:16]
    pack_ref[MIDROWS + 48 :, :] = jnp.concatenate([first, jnp.zeros_like(first)], axis=1).astype(bf16)


def finish_kernel(h, cells, low_ref, other_ref, n0, n1, n2, n3, new_ref, wf_ref, bf_ref, wm_ref, bm_ref, wl_ref, bl_ref, rms_ref, parts):
    me = lax.axis_index("chan")
    for k, piece in enumerate((n0, n1, n2, n3)):
        slot = jnp.bitwise_xor(me, k)
        new_ref[0, slot] = piece[0:h]
        new_ref[1, slot] = piece[h : 2 * h]
        parts[slot] = piece[2 * h :]

    def total(at, count):
        return low_ref[at : at + count, :].astype(f32) + other_ref[at : at + count, :].astype(f32)

    def turned(block):
        return jnp.concatenate([block, jnp.zeros((128 - block.shape[0], 128), f32)], axis=0).T

    for l in range(NL):
        for j in range(3):
            n = 3 * l + j
            block = total(n * 16, 16)
            tail = total(TAILS + (n // 2) * 16, 16)
            wm_ref[l, 0, j] = block[:, 0:64]
            wm_ref[l, 1, j] = block[:, 64:128]
            wm_ref[l, 2, j] = tail[:, 64 * (n % 2) : 64 * (n % 2) + 64]
    bm_ref[...] = turned(total(TAILS + 112, 16))[64 : 64 + NL, 0:16]
    tail = total(LAST, 48)
    for j in range(3):
        wl_ref[0, j] = tail[j * 8 : j * 8 + 8, 0:64]
        wl_ref[1, j] = tail[j * 8 : j * 8 + 8, 64:128]
    wl_ref[2, 0] = tail[24:32, 0:64]
    wl_ref[2, 1] = tail[24:32, 64:128]
    wl_ref[2, 2] = tail[32:40, 0:64]
    bl_ref[...] = turned(tail[32:40])[64:65, 0:8]
    first = turned(total(FIRST, 16))
    for i in range(3):
        for j in range(3):
            for c in range(2):
                at = i * 8 + c * 4 + j
                wf_ref[i, j, c : c + 1, :] = first[at : at + 1, 0:16]
    bf_ref[...] = first[24:25, 0:16]
    news = (parts[0] + parts[1]) + (parts[2] + parts[3])
    lane = lax.broadcasted_iota(jnp.int32, (8, 128), 1)
    sums = jnp.where(lane == 3, news[:, 0:128], tail[40:48])
    rms_ref[...] = jnp.sqrt(sums * (1.0 / cells))[0:1, 0:4]


def moved(x, axis, step):
    n = lax.axis_size(axis)
    return lax.ppermute(x, axis, [(i, (i + step) % n) for i in range(n)])


def swapped(x, axis, bit):
    n = lax.axis_size(axis)
    return lax.ppermute(x, axis, [(i, i ^ bit) for i in range(n)])


def halos(own, top, bottom, width):
    height = own.shape[1]
    if height >= width:
        return moved(bottom, "space", 1), moved(top, "space", -1)
    hops = -(-width // height)
    up = jnp.concatenate([moved(own, "space", k) for k in range(hops, 0, -1)], axis=1)
    down = jnp.concatenate([moved(own, "space", -k) for k in range(1, hops + 1)], axis=1)
    return up[:, up.shape[1] - width :], down[:, :width]


def tables(h, space, nx):
    ny = h * space
    ty, tx = basis(ny), basis(nx)

    def held(table):
        return jnp.asarray(np.ascontiguousarray(table).astype(np.float32))

    back_y = ty.T
    if h % 8:
        wide = np.zeros((2, ny, space, 2, h))
        for c in range(2):
            wide[c, :, :, c, :] = ty.T.reshape(ny, space, h)
        back_y = wide.reshape(2 * ny, 2 * ny)
    ring = (np.arange(space)[:, None] * h + np.arange(h + 2 * GPH)[None, :] - GPH) % ny
    spectral = [jnp.asarray(m.astype(np.float32)) for m in multipliers(ny, nx)]
    return [held(tx), held(back_y), held(tx.T), held(ty[ring])] + spectral


def vmem(count):
    return [pl.BlockSpec(memory_space=pltpu.VMEM)] * count


def per_device(velocity, w_first, b_first, w_mid, b_mid, w_last, b_last, offsets, cotangent):
    traj, h, nx = velocity.shape[1:]
    space = lax.axis_size("space")
    ny = h * space
    me_chan = lax.axis_index("chan")
    rows = h + 2 * HALO
    shape = jax.ShapeDtypeStruct
    inside = pltpu.VMEM

    def limit(mebibytes):
        return pltpu.CompilerParams(vmem_limit_bytes=mebibytes * 2**20)

    def outside(x):
        return pltpu.with_memory_space_constraint(x, pltpu.HBM)

    own_cot = lax.dynamic_index_in_dim(cotangent, me_chan, 1, keepdims=False).astype(bf16)
    cot_all = jnp.broadcast_to(own_cot[None], (space,) + own_cot.shape)
    packed, own, top, bottom = pl.pallas_call(
        functools.partial(prepare_kernel, h),
        out_shape=[
            inside((MIDROWS + 64, KW), bf16),
            inside((2, h, nx), f32),
            inside((2, min(h, HALO), nx), f32),
            inside((2, min(h, HALO), nx), f32),
        ],
        in_specs=vmem(7),
        out_specs=vmem(4),
        scratch_shapes=[pltpu.VMEM((128, 128), f32), pltpu.VMEM((8, 128), f32)],
        compiler_params=limit(16),
        name="prepare",
    )(
        *[
            outside(x)
            for x in (
                velocity, jnp.swapaxes(w_mid, 3, 4), jnp.swapaxes(w_last, 2, 3),
                w_first, b_mid, b_first[None], b_last[None],
            )
        ],
    )
    across = swapped(packed, "chan", 2)
    up, down = halos(own, top, bottom, HALO)
    across, up, down = lax.optimization_barrier((across, up, down))
    beside = swapped(packed, "chan", 1)
    diagonal = swapped(across, "chan", 1)
    cot_full = lax.all_to_all(cot_all, "space", 0, 0, tiled=True)
    if h % 8:
        cot_full = cot_full.reshape(space * 2 * h, nx)

    deep = h + 2 * DEEP
    constants = [outside(x) for x in tables(h, space, nx)]
    places = [inside(x.shape[1:] if k == 3 else x.shape, f32) for k, x in enumerate(constants)]
    prov, vel_grad, keep, send, *constants = pl.pallas_call(
        functools.partial(step_kernel, h),
        out_shape=[inside((space, 2, h, nx), bf16), shape((2, h, nx), f32)]
        + [inside((2, SUMROWS, 128), bf16)] * 2
        + places,
        in_specs=vmem(9) + [pl.BlockSpec(memory_space=pl.ANY)] * 7,
        out_specs=vmem(11),
        scratch_shapes=[
            inside((2, rows, nx), f32),
            inside((nx // 128, rows * 8, 128), f32),
            inside((2, h + 4, nx), f32),
            inside(((h + 4) * 32, nx), f32),
            inside((NL + 1, deep, C, nx), bf16),
            inside((NL + 1, deep, C, nx), f32),
            inside((NL * 3, C, KW), bf16),
            inside((3, 32, KW), bf16),
            inside((C, KW), bf16),
            inside((3, 32, KW), f32),
            inside((h + 14, 32, nx), bf16),
        ]
        + [inside((h + 2 * l, C, nx), bf16) for l in range(6, 0, -1)]
        + [
            inside((nx // 128, (h + 2 * GPH) * 8, 128), f32),
            inside((2, h + 2 * GPH, nx), f32),
            inside((7, 192, KW), f32),
            inside((2, h + 2 * GPH, nx), f32),
            inside((nx // 128, h * 8, 128), f32),
        ]
        + [pltpu.SemaphoreType.DMA((7,))],
        compiler_params=limit(50),
        cost_estimate=pl.CostEstimate(
            flops=6 * 7 * deep * nx * 9 * C * C, bytes_accessed=2**25, transcendentals=6 * deep * nx * C
        ),
        name="step",
    )(own, up, down, packed, beside, across, diagonal, outside(offsets), cot_full, *constants)
    everywhere = lax.all_to_all(prov, "space", 0, 0, tiled=True)
    if h % 8:
        everywhere = everywhere.reshape(space * 2 * h, nx)

    new_own = pl.pallas_call(
        functools.partial(project_kernel, h),
        out_shape=inside((2 * h + 8, nx), f32),
        in_specs=vmem(8),
        out_specs=vmem(1)[0],
        compiler_params=limit(16),
        cost_estimate=pl.CostEstimate(flops=2**31, bytes_accessed=2**22, transcendentals=0),
        name="project",
    )(everywhere, *constants)

    pair = (keep.astype(f32) + swapped(send, "chan", 1).astype(f32)).astype(bf16)
    low = (pair[0].astype(f32) + swapped(pair[1], "chan", 2).astype(f32)).astype(bf16)
    bit = 1
    while 2 * bit < space:
        low = (low.astype(f32) + swapped(low, "space", bit).astype(f32)).astype(bf16)
        bit *= 2
    other = swapped(low, "space", bit)
    news = [new_own] + [swapped(new_own, "chan", k) for k in (1, 2, 3)]

    new_velocity, w_first_grad, b_first_grad, w_mid_grad, b_mid_grad, w_last_grad, b_last_grad, rms_stats = pl.pallas_call(
        functools.partial(finish_kernel, h, 2 * traj * ny * nx),
        out_shape=[
            shape((2, traj, h, nx), f32),
            shape((3, 3, 2, 16), f32),
            shape((1, 16), f32),
            shape((NL, 3, 3, 16, C), f32),
            shape((NL, 16), f32),
            shape((3, 3, 8, C), f32),
            shape((1, 8), f32),
            shape((1, 4), f32),
        ],
        in_specs=vmem(6),
        out_specs=vmem(8),
        scratch_shapes=[pltpu.VMEM((4, 8, KW), f32)],
        compiler_params=limit(16),
        name="finish",
    )(low, other, *news)
    return (
        new_velocity,
        vel_grad[:, None],
        w_first_grad,
        b_first_grad[0],
        jnp.swapaxes(w_mid_grad, 3, 4),
        b_mid_grad,
        jnp.swapaxes(w_last_grad, 2, 3),
        b_last_grad[0],
        rms_stats[0],
    )


def solution(mesh):
    return jax.shard_map(
        per_device,
        mesh=mesh,
        in_specs=(
            P(None, None, "space", None),
            P(None, None, None, "chan"),
            P("chan"),
            P(None, None, None, None, "chan"),
            P(None, "chan"),
            P(None, None, None, "chan"),
            P("chan"),
            P(),
            P(None, None, "space", None),
        ),
        out_specs=(
            P(None, None, "space", None),
            P(None, "chan", "space", None),
            P(None, None, None, "chan"),
            P("chan"),
            P(None, None, None, None, "chan"),
            P(None, "chan"),
            P(None, None, None, "chan"),
            P("chan"),
            P(),
        ),
        check_vma=False,
    )
```

```python
import functools

import jax
import jax.numpy as jnp
import numpy as np
from jax import lax
from jax.experimental import pallas as pl
from jax.experimental.pallas import tpu as pltpu
from jax.sharding import PartitionSpec as P

f32 = jnp.float32
bf16 = jnp.bfloat16
highest = lax.Precision.HIGHEST
time_step = 0.2
viscosity = 0.256
HALO = 16
DEEP = 12
GPH = 8
C = 64
NL = 5
KW = 256
MIDROWS = NL * 3 * 16
TAILS = MIDROWS
LAST = TAILS + 128
FIRST = LAST + 48
SUMROWS = FIRST + 16
A0 = 0.7978845608028654
A1 = 0.044715 * A0


def basis(length):
    half = length // 2
    pos = np.arange(length)[:, None]
    table = np.zeros((length, length))
    m = np.arange(half + 1)[None, :]
    table[:, : half + 1] = np.cos(2 * np.pi * ((pos * m) % length) / length) * np.sqrt(2.0 / length)
    table[:, 0] = np.sqrt(1.0 / length)
    table[:, half] = np.cos(np.pi * pos[:, 0]) * np.sqrt(1.0 / length)
    m = np.arange(1, half)[None, :]
    table[:, half + 1 :] = np.sin(2 * np.pi * ((pos * m) % length) / length) * np.sqrt(2.0 / length)
    return table


def multipliers(ny, nx):
    def modes(n):
        half = n // 2
        index = np.arange(n)
        wave = np.where(index <= half, index, index - half) * (2 * np.pi / n)
        return wave, index <= half

    ky, cy = modes(ny)
    kx, cx = modes(nx)
    ky, cy = ky[:, None], cy[:, None]
    kx, cx = kx[None, :], cx[None, :]
    sq = kx * kx + ky * ky
    inv = np.where(sq > 0, 1.0 / np.where(sq > 0, sq, 1.0), 0.0)
    sign = np.where(cx == cy, 1.0, -1.0)
    edge_x = (kx == 0) | (kx >= np.pi - 1e-9)
    edge_y = (ky == 0) | (ky >= np.pi - 1e-9)
    mxy = np.where(edge_x | edge_y, 0.0, sign * kx * ky * inv)
    mxx = 1.0 - kx * kx * inv
    myy = 1.0 - ky * ky * inv
    return mxx, myy, mxy


def project_spectral(u, v, mxx, myy, mxy):
    half_y, half_x = u.shape[0] // 2, u.shape[1] // 2

    def swap(a):
        a = jnp.concatenate([a[:, half_x:], a[:, :half_x]], axis=1)
        return jnp.concatenate([a[half_y:], a[:half_y]], axis=0)

    rows = lax.broadcasted_iota(jnp.int32, u.shape, 0)
    cols = lax.broadcasted_iota(jnp.int32, u.shape, 1)
    corner = jnp.where((rows == half_y) & (cols == half_x), -0.5, 0.0)
    return (
        mxx * u + mxy * swap(v) + corner * v,
        myy * v + mxy * swap(u) + corner * u,
    )


def halves(x):
    high = x.astype(bf16)
    return high, (x - high.astype(f32)).astype(bf16)


def product(a, b):
    def dot(x, y):
        return jnp.dot(x, y, preferred_element_type=f32)

    return dot(a[0], b[0]) + (dot(a[1], b[0]) + dot(a[0], b[1]))


def spectrum(h, field_ref, tx_ref, ty_ref):
    ny = field_ref.shape[0] * h if h % 8 == 0 else field_ref.shape[0] // 2
    if h % 8 == 0:
        fields = [field_ref[:, c].reshape(ny, KW) for c in range(2)]
        field = jnp.concatenate(fields, axis=0).astype(f32)
    else:
        field = field_ref[...].astype(f32)
    along = product(halves(field), halves(tx_ref[...]))
    table = halves(ty_ref[...])
    if h % 8 == 0:
        return [product(table, halves(along[c * ny : (c + 1) * ny])) for c in range(2)]
    out = product(table, halves(along))
    return out[:ny], out[ny:]


def project_back(trow, u, back_ref):
    back = halves(back_ref[...])
    return product(halves(product(trow, halves(u))), back)


def gelu(z):
    t = jnp.tanh(z * (A0 + A1 * (z * z)))
    return z * (0.5 * t + 0.5)


def gelu_slope(z):
    z2 = z * z
    t = jnp.tanh(z * (A0 + A1 * z2))
    return (0.5 * t + 0.5) + (z * (0.5 * A0 + 1.5 * A1 * z2)) * (1.0 - t * t)


def lroll(x, s):
    return pltpu.roll(x, s % x.shape[1], 1)


def shifts(x):
    return jnp.concatenate([lroll(x, 1), x, lroll(x, -1)], axis=0)


def unshifts(x):
    return jnp.concatenate([lroll(x, -1), x, lroll(x, 1)], axis=0)


def spread(ref, first, values):
    for k in range(ref.shape[0]):
        ref[k, pl.ds(first, values.shape[0], stride=8), :] = values[:, k * 128 : k * 128 + 128]


def collect(ref, first, count):
    planes = [ref[k, pl.ds(first, count, stride=8), :] for k in range(ref.shape[0])]
    return jnp.concatenate(planes, axis=1)


def rows_of(ref, first, count):
    at = pl.ds(first if isinstance(first, int) else pl.multiple_of(first, 8), count)
    return jnp.concatenate([ref[k, at, :] for k in range(ref.shape[0])], axis=1)


def put_rows(ref, first, values):
    at = pl.ds(
        first if isinstance(first, int) else pl.multiple_of(first, 8), values.shape[0]
    )
    for k in range(ref.shape[0]):
        ref[k, at, :] = values[:, k * 128 : k * 128 + 128]


def group4(s):
    i = lax.broadcasted_iota(jnp.int32, s.shape, 0)
    s = s + jnp.where(i % 2 == 0, pltpu.roll(s, 7, 0), pltpu.roll(s, 1, 0))
    return s + jnp.where((i // 2) % 2 == 0, pltpu.roll(s, 6, 0), pltpu.roll(s, 2, 0))


def point_order(offs):
    row = lax.broadcasted_iota(jnp.int32, (32, 16), 0)
    point = (row // 8) * 4 + row % 4
    comp = (row // 4) % 2
    parts = [
        jnp.where((comp == c) & (offs[c : c + 1, :] == point), 1.0, 0.0).astype(f32)
        for c in range(2)
    ]
    return jnp.concatenate(parts, axis=1)


def blocks(n, most=27):
    count = -(-n // most)
    return count, -(-n // count)


def step_kernel(
    h, vel_ref, up_ref, down_ref, w0, w1, w2, w3, offs_ref,
    cot_ref, *rest,
):
    held = rest[:7]
    (
    prov_ref, vel_grad_ref, keep_ref, send_ref,
    tx_ref, ty_ref, back_ref, trow_ref, mxx_ref, myy_ref, mxy_ref,
    vp_ref, vs_ref, face_ref, mix_ref, xb, zb, wk_ref, w7_ref, wf_ref, w7k,
    gz7, gz6, gz5, gz4, gz3, gz2, gz1, f8, adv_ref, acc_ref, gp_ref, near8, sems,
    ) = rest[7:]
    loads = [
        pltpu.make_async_copy(table.at[lax.axis_index("space")] if k == 3 else table, place, sems.at[k])
        for k, (table, place) in enumerate(
            zip(held, (tx_ref, ty_ref, back_ref, trow_ref, mxx_ref, myy_ref, mxy_ref))
        )
    ]
    for load in loads:
        load.start()
    rows = h + 2 * HALO
    me = lax.axis_index("chan")
    for k, piece in enumerate((w0, w1, w2, w3)):
        slot = jnp.bitwise_xor(me, k)
        at16 = pl.ds(pl.multiple_of(slot * 16, 16), 16)
        at8 = pl.ds(pl.multiple_of(slot * 8, 8), 8)
        for n in range(NL * 3):
            wk_ref[n, at16, :] = piece[n * 16 : n * 16 + 16]
        for j in range(3):
            block = piece[MIDROWS + j * 16 : MIDROWS + j * 16 + 16].astype(f32)
            w7k[j, at8, :] = block[0:8]
        wf_ref[at16, :] = piece[MIDROWS + 48 : MIDROWS + 64]
    perm = point_order(offs_ref[...])
    perm_low = perm.astype(bf16)
    for i in range(3):
        w7_ref[i] = jnp.dot(perm_low, w7k[i].astype(bf16), preferred_element_type=f32).astype(bf16)

    vp_ref[:, 0:HALO] = up_ref[...]
    vp_ref[:, HALO : HALO + h] = vel_ref[...]
    vp_ref[:, HALO + h :] = down_ref[...]
    for c in range(2):
        plane = vp_ref[c]
        for d in range(4):
            spread(vs_ref, c * 4 + d, lroll(plane, 1 - d))

    def vs_rows(y, n):
        return rows_of(vs_ref, (y + HALO) * 8, 8 * n)

    ones = jnp.ones((16, KW), bf16)

    wfirst = wf_ref[:, 0:32]
    n = h + 2 * (DEEP - 1)
    count, size = blocks(n, 60)

    def first_block(k, _):
        top = k * size - (DEEP - 1)
        for r in range(size):
            y = top + r
            x = jnp.concatenate([vs_rows(y - 1, 3), jnp.ones((8, KW), f32)], axis=0)
            z = jnp.dot(wfirst, x.astype(bf16), preferred_element_type=f32)
            zb[0, y + DEEP] = z
            xb[0, y + DEEP] = gelu(z).astype(bf16)
        return 0

    lax.fori_loop(0, count, first_block, 0)

    def rows_through(source, weight, width, first, n, most, done):
        count, size = blocks(n, most)

        def taps(row):
            x = jnp.concatenate([shifts(source(row)), ones], axis=0)
            o = jnp.dot(weight, x, preferred_element_type=f32)
            return [o[i * width : (i + 1) * width] for i in range(3)]

        def block(k, carry):
            p0, p1 = carry
            for r in range(size):
                row = first + k * size + r
                o = taps(row + 1)
                done(row, p1 + o[2])
                p0, p1 = o[0], p0 + o[1]
            return p0, p1

        before, here = taps(first - 1), taps(first)
        lax.fori_loop(0, count, block, (here[0], before[0] + here[1]))

    for l in range(1, NL + 1):

        def done(row, z, l=l):
            zb[l, row] = z
            xb[l, row] = gelu(z).astype(bf16)

        rows_through(
            lambda row, l=l: xb[l - 1, row],
            wk_ref[3 * (l - 1) : 3 * l].reshape(192, KW)[:, 0:208],
            C, 1 + l, h + 2 * (DEEP - 1 - l), 60, done,
        )

    row = lax.broadcasted_iota(jnp.int32, (32, KW), 0)
    point = (row // 8) * 4 + row % 4
    second = jnp.where((row // 4) % 2 == 0, 6, 9)
    base = jnp.where((point == 5) | (point == second), 0.5, 0.0).astype(f32)

    def mixed(row, s):
        y = row - DEEP
        mean = group4(s[0:8] + s[8:16] + s[16:24] + s[24:32]) * (1.0 / 16.0)
        mix = s - jnp.concatenate([mean] * 4, axis=0) + base
        mix_ref[pl.ds(pl.multiple_of((y + 2) * 32, 32), 32), :] = mix
        m = mix * vs_rows(y - 1, 4)
        m = group4(m[0:8] + m[8:16] + m[16:24] + m[24:32])
        put_rows(f8, (y + 2) * 8, m)

    rows_through(
        lambda row: xb[NL, row], w7_ref[...].reshape(96, KW)[:, 0:208], 32, DEEP - 2, h + 4, 18, mixed
    )
    for c in range(2):
        face_ref[c] = collect(f8, c * 4, h + 4)
    ue = face_ref[0, 2 : 2 + h]
    vn = face_ref[1, 2 : 2 + h]
    vn_south = face_ref[1, 1 : 1 + h]
    total = [jnp.sum(ue * ue) + jnp.sum(vn * vn)]
    own = update = 0.0
    for c in range(2):
        q = vp_ref[c, HALO : HALO + h]
        north = vp_ref[c, HALO + 1 : HALO + 1 + h]
        south = vp_ref[c, HALO - 1 : HALO - 1 + h]
        east, west = lroll(q, -1), lroll(q, 1)
        lap = east + west + north + south - 4.0 * q
        fx = ue * (q + east) * 0.5
        adv = fx - lroll(fx, 1) + vn * (q + north) * 0.5 - vn_south * (south + q) * 0.5
        new = q + time_step * (viscosity * lap - adv)
        for k in range(prov_ref.shape[0]):
            prov_ref[k, c] = new.astype(prov_ref.dtype)
        own = own + jnp.sum(q * q)
        update = update + jnp.sum((new - q) * (new - q))
    lane = lax.broadcasted_iota(jnp.int32, (8, KW), 1)
    squares = jnp.where(
        lane == 0, own, jnp.where(lane == 1, total[0], jnp.where(lane == 2, update, 0.0))
    )

    for load in loads:
        load.wait()

    n = h + 2 * GPH
    u, v = spectrum(h, cot_ref, tx_ref, ty_ref)
    u, v = project_spectral(u, v, mxx_ref[...], myy_ref[...], mxy_ref[...])
    trow = halves(trow_ref[...])
    gp_ref[0] = project_back(trow, u, back_ref)
    gp_ref[1] = project_back(trow, v, back_ref)

    m = n - 1
    fields = []
    gue = gvn = 0.0
    for c in range(2):
        g = -time_step * gp_ref[c, 0:m]
        g_north = -time_step * gp_ref[c, 1 : m + 1]
        q = vp_ref[c, HALO - GPH : HALO - GPH + m]
        q_north = vp_ref[c, HALO - GPH + 1 : HALO - GPH + 1 + m]
        gfx = g - lroll(g, -1)
        gfy = g - g_north
        gue = gue + gfx * (q + lroll(q, -1)) * 0.5
        gvn = gvn + gfy * (q + q_north) * 0.5
        adv_ref[c, 0:m] = gfy
        fields.append(gfx[GPH : GPH + h])
    for d in range(4):
        spread(f8, d, gue)
        spread(f8, 4 + d, gvn)
    ue = face_ref[0, 2 : 2 + h]
    vn = face_ref[1, 2 : 2 + h]
    vn_south = face_ref[1, 1 : 1 + h]
    for c in range(2):
        g = gp_ref[c, GPH : GPH + h]
        lap = (
            lroll(g, -1) + lroll(g, 1) + gp_ref[c, GPH + 1 : GPH + 1 + h]
            + gp_ref[c, GPH - 1 : GPH - 1 + h] - 4.0 * g
        )
        ex = fields[c] * ue
        ny = adv_ref[c, GPH : GPH + h] * vn
        sy = adv_ref[c, GPH - 1 : GPH - 1 + h] * vn_south
        vel_grad_ref[c] = g + time_step * viscosity * lap + 0.5 * (ex + lroll(ex, 1) + ny + sy)

    def f8_row(y):
        return rows_of(f8, (y + GPH) * 8, 8)

    def stencil_row(k, _):
        for r in range(2):
            y = 2 * k + r - 7
            face = f8_row(y)
            near = vs_rows(y - 1, 4)
            s = near[0:8] + near[8:16] + near[16:24] + near[24:32]
            mean = group4(s) * (1.0 / 16.0)
            gm = (near - jnp.concatenate([mean] * 4, axis=0)) * jnp.concatenate([face] * 4, axis=0)
            gz7[y + 7] = gm.astype(bf16)
        return 0

    lax.fori_loop(0, (h + 14) // 2, stencil_row, 0, unroll=4 if h >= 16 else 1)

    def wgrad(columns, inputs):
        return lax.dot_general(
            jnp.concatenate(columns, axis=1),
            jnp.concatenate(inputs, axis=1),
            (((1,), (1,)), ((), ())),
            preferred_element_type=f32,
        )

    gzs = {7: gz7, 6: gz6, 5: gz5, 4: gz4, 3: gz3, 2: gz2, 1: gz1}
    for l in range(7, 1, -1):
        source, target = gzs[l], gzs[l - 1]
        if l == 7:
            parts = [w7_ref[i][:, 0:192].astype(f32) for i in range(3)]
            width = 32
        else:
            parts = [wk_ref[3 * (l - 2) + i][:, 0:192].astype(f32) for i in range(3)]
            width = C
        weight = jnp.concatenate(
            [
                jnp.concatenate([p[:, j * C : (j + 1) * C].T for j in range(3)], axis=1)
                for p in parts
            ],
            axis=0,
        ).astype(bf16)
        p0 = p1 = None
        acc = None
        for ys in (range(-l, h // 2), range(h // 2, h + l)):
            columns = {y: unshifts(source[y + l]) for y in ys}
            for y in ys:
                o = jnp.dot(weight, columns[y], preferred_element_type=f32)
                if y >= 2 - l:
                    ga = p1 + o[0:64]
                    slope = gelu_slope(zb[l - 2, y - 1 + DEEP])
                    target[y - 1 + l - 1] = (ga * slope).astype(bf16)
                p1 = o[64:128] if p0 is None else p0 + o[64:128]
                p0 = o[128:192]
            own = [y for y in ys if 0 <= y < h]
            part = wgrad(
                [columns[y] for y in own],
                [
                    jnp.concatenate(
                        [xb[l - 2, y + DEEP - 1 : y + DEEP + 2].reshape(192, KW), ones], axis=0
                    )
                    for y in own
                ],
            )
            acc = part if acc is None else acc + part
        if l == 7:
            back = perm
            acc = jnp.concatenate(
                [
                    lax.dot_general(
                        back, acc[j * 32 : j * 32 + 32], (((0,), (0,)), ((), ())),
                        preferred_element_type=f32, precision=highest,
                    )
                    for j in range(3)
                ],
                axis=0,
            )
        acc_ref[l - 1, 0 : 3 * width, 0:208] = acc

    wfirst = wf_ref[:, 0:32].astype(f32).T.astype(bf16)
    source = gz1
    outs = {}
    for y in range(-1, h + 1):
        outs[y] = jnp.dot(wfirst[0:24], source[y + 1], preferred_element_type=f32)
    acc_ref[0, 0:64, 0:40] = wgrad(
        [source[y + 1] for y in range(h)],
        [
            jnp.concatenate(
                [vs_rows(y - 1, 3), jnp.ones((16, KW), f32)], axis=0
            ).astype(bf16)
            for y in range(h)
        ],
    )
    for y in range(h):
        total = outs[y + 1][0:8] + outs[y][8:16] + outs[y - 1][16:24]
        for k in range(4):
            at = y + 1 - k
            total = total + f8_row(at) * mix_ref[pl.ds((at + 2) * 32 + k * 8, 8), :]
        put_rows(near8, y * 8, total)
    for c in range(2):
        total = vel_grad_ref[c]
        for d in range(4):
            total = total + lroll(collect(near8, c * 4 + d, h), d - 1)
        vel_grad_ref[c] = total

    lane = lax.broadcasted_iota(jnp.int32, (16, 64), 1)
    for k, other in enumerate((0, 2, 1, 3)):
        slot = jnp.bitwise_xor(me, other)
        pack_ref = (keep_ref, send_ref)[k // 2]
        k = k % 2
        tails = []
        bias = jnp.zeros((16, 64), f32)
        for l in range(NL):
            for j in range(3):
                piece = acc_ref[l + 1, pl.ds(pl.multiple_of(j * 64 + slot * 16, 16), 16), :]
                at = (3 * l + j) * 16
                pack_ref[k, at : at + 16, :] = piece[:, 0:128].astype(bf16)
                tails.append(piece[:, 128:192])
                if j == 0:
                    bias = jnp.where(lane == l, jnp.broadcast_to(piece[:, 192:193], (16, 64)), bias)
        tails.append(bias)
        for n in range(8):
            at = TAILS + 16 * n
            pack_ref[k, at : at + 16, :] = jnp.concatenate(tails[2 * n : 2 * n + 2], axis=1).astype(bf16)
        last = [
            acc_ref[6, pl.ds(pl.multiple_of(j * 32 + slot * 8, 8), 8), :] for j in range(3)
        ]
        tails = [p[:, 128:192] for p in last]
        tails.append(jnp.broadcast_to(last[0][:, 192:193], (8, 64)))
        groups = [p[:, 0:128] for p in last]
        groups += [jnp.concatenate(tails[0:2], axis=1), jnp.concatenate(tails[2:4], axis=1)]
        groups.append(squares[:, 0:128])
        pack_ref[k, LAST:FIRST, :] = jnp.concatenate(groups, axis=0).astype(bf16)
        pack_ref[k, FIRST:SUMROWS, :] = acc_ref[
            0, pl.ds(pl.multiple_of(slot * 16, 16), 16), 0:128
        ].astype(bf16)


def project_kernel(h, prov_ref, tx_ref, ty_ref, back_ref, trow_ref, mxx_ref, myy_ref, mxy_ref, out_ref):
    trow = halves(trow_ref[GPH : GPH + h])
    u, v = spectrum(h, prov_ref, tx_ref, ty_ref)
    u, v = project_spectral(u, v, mxx_ref[...], myy_ref[...], mxy_ref[...])
    out_ref[0:h] = project_back(trow, u, back_ref)
    out_ref[h : 2 * h] = project_back(trow, v, back_ref)
    out_ref[2 * h :] = jnp.full((8, KW), jnp.sum(u * u) + jnp.sum(v * v), f32)


def prepare_kernel(h, vel_ref, wm_ref, wl_ref, wf_ref, bm_ref, bf_ref, bl_ref, pack_ref, own_ref, top_ref, bottom_ref, tall, wide):
    me = lax.axis_index("chan")
    own = vel_ref[:, me]
    own_ref[...] = own
    if h >= HALO:
        top_ref[...] = own[:, :HALO]
        bottom_ref[...] = own[:, h - HALO :]
    wide[...] = jnp.zeros_like(wide)
    wide[0:NL, 0:16] = bm_ref[...].astype(f32)
    wide[NL : NL + 1, 0:16] = bf_ref[...].astype(f32)
    wide[NL + 1 : NL + 2, 0:8] = bl_ref[...].astype(f32)
    columns = wide[...].T

    def column(k, count, i):
        lane = lax.broadcasted_iota(jnp.int32, (count, 64), 1)
        here = jnp.broadcast_to(columns[0:count, k : k + 1], (count, 64))
        return jnp.where((lane == 0) & (i == 1), here, 0.0)

    for l in range(NL):
        for i in range(3):
            parts = [wm_ref[l, i, j] for j in range(3)] + [column(l, 16, i).astype(bf16)]
            at = (3 * l + i) * 16
            pack_ref[at : at + 16, :] = jnp.concatenate(parts, axis=1)
    for i in range(3):
        parts = [wl_ref[i, j].astype(f32) for j in range(3)] + [column(NL + 1, 8, i)]
        block = jnp.concatenate(parts, axis=1)
        at = MIDROWS + i * 16
        pack_ref[at : at + 16, :] = jnp.concatenate([block, jnp.zeros_like(block)], axis=0).astype(bf16)
    tall[...] = jnp.zeros_like(tall)
    for i in range(3):
        for j in range(3):
            taps = wf_ref[i, j].astype(f32)
            for c in range(2):
                at = i * 8 + c * 4 + j
                tall[at : at + 1, 0:16] = taps[c : c + 1]
    tall[24:25, 0:16] = bf_ref[...].astype(f32)
    first = tall[...].T[0:16]
    pack_ref[MIDROWS + 48 :, :] = jnp.concatenate([first, jnp.zeros_like(first)], axis=1).astype(bf16)


def finish_kernel(h, cells, low_ref, other_ref, n0, n1, n2, n3, new_ref, wf_ref, bf_ref, wm_ref, bm_ref, wl_ref, bl_ref, rms_ref, parts):
    me = lax.axis_index("chan")
    for k, piece in enumerate((n0, n1, n2, n3)):
        slot = jnp.bitwise_xor(me, k)
        new_ref[0, slot] = piece[0:h]
        new_ref[1, slot] = piece[h : 2 * h]
        parts[slot] = piece[2 * h :]

    def total(at, count):
        return low_ref[at : at + count, :].astype(f32) + other_ref[at : at + count, :].astype(f32)

    def turned(block):
        return jnp.concatenate([block, jnp.zeros((128 - block.shape[0], 128), f32)], axis=0).T

    for l in range(NL):
        for j in range(3):
            n = 3 * l + j
            block = total(n * 16, 16)
            tail = total(TAILS + (n // 2) * 16, 16)
            wm_ref[l, 0, j] = block[:, 0:64]
            wm_ref[l, 1, j] = block[:, 64:128]
            wm_ref[l, 2, j] = tail[:, 64 * (n % 2) : 64 * (n % 2) + 64]
    bm_ref[...] = turned(total(TAILS + 112, 16))[64 : 64 + NL, 0:16]
    tail = total(LAST, 48)
    for j in range(3):
        wl_ref[0, j] = tail[j * 8 : j * 8 + 8, 0:64]
        wl_ref[1, j] = tail[j * 8 : j * 8 + 8, 64:128]
    wl_ref[2, 0] = tail[24:32, 0:64]
    wl_ref[2, 1] = tail[24:32, 64:128]
    wl_ref[2, 2] = tail[32:40, 0:64]
    bl_ref[...] = turned(tail[32:40])[64:65, 0:8]
    first = turned(total(FIRST, 16))
    for i in range(3):
        for j in range(3):
            for c in range(2):
                at = i * 8 + c * 4 + j
                wf_ref[i, j, c : c + 1, :] = first[at : at + 1, 0:16]
    bf_ref[...] = first[24:25, 0:16]
    news = (parts[0] + parts[1]) + (parts[2] + parts[3])
    lane = lax.broadcasted_iota(jnp.int32, (8, 128), 1)
    sums = jnp.where(lane == 3, news[:, 0:128], tail[40:48])
    rms_ref[...] = jnp.sqrt(sums * (1.0 / cells))[0:1, 0:4]


def moved(x, axis, step):
    n = lax.axis_size(axis)
    return lax.ppermute(x, axis, [(i, (i + step) % n) for i in range(n)])


def swapped(x, axis, bit):
    n = lax.axis_size(axis)
    return lax.ppermute(x, axis, [(i, i ^ bit) for i in range(n)])


def halos(own, top, bottom, width):
    height = own.shape[1]
    if height >= width:
        return moved(bottom, "space", 1), moved(top, "space", -1)
    hops = -(-width // height)
    up = jnp.concatenate([moved(own, "space", k) for k in range(hops, 0, -1)], axis=1)
    down = jnp.concatenate([moved(own, "space", -k) for k in range(1, hops + 1)], axis=1)
    return up[:, up.shape[1] - width :], down[:, :width]


def tables(h, space, nx):
    ny = h * space
    ty, tx = basis(ny), basis(nx)

    def held(table):
        return jnp.asarray(np.ascontiguousarray(table).astype(np.float32))

    back_y = ty.T
    if h % 8:
        wide = np.zeros((2, ny, space, 2, h))
        for c in range(2):
            wide[c, :, :, c, :] = ty.T.reshape(ny, space, h)
        back_y = wide.reshape(2 * ny, 2 * ny)
    ring = (np.arange(space)[:, None] * h + np.arange(h + 2 * GPH)[None, :] - GPH) % ny
    spectral = [jnp.asarray(m.astype(np.float32)) for m in multipliers(ny, nx)]
    return [held(tx), held(back_y), held(tx.T), held(ty[ring])] + spectral


def vmem(count):
    return [pl.BlockSpec(memory_space=pltpu.VMEM)] * count


def per_device(velocity, w_first, b_first, w_mid, b_mid, w_last, b_last, offsets, cotangent):
    traj, h, nx = velocity.shape[1:]
    space = lax.axis_size("space")
    ny = h * space
    me_chan = lax.axis_index("chan")
    rows = h + 2 * HALO
    shape = jax.ShapeDtypeStruct
    inside = pltpu.VMEM

    def limit(mebibytes):
        return pltpu.CompilerParams(vmem_limit_bytes=mebibytes * 2**20)

    def outside(x):
        return pltpu.with_memory_space_constraint(x, pltpu.HBM)

    own_cot = lax.dynamic_index_in_dim(cotangent, me_chan, 1, keepdims=False).astype(bf16)
    cot_all = jnp.broadcast_to(own_cot[None], (space,) + own_cot.shape)
    packed, own, top, bottom = pl.pallas_call(
        functools.partial(prepare_kernel, h),
        out_shape=[
            inside((MIDROWS + 64, KW), bf16),
            inside((2, h, nx), f32),
            inside((2, min(h, HALO), nx), f32),
            inside((2, min(h, HALO), nx), f32),
        ],
        in_specs=vmem(7),
        out_specs=vmem(4),
        scratch_shapes=[pltpu.VMEM((128, 128), f32), pltpu.VMEM((8, 128), f32)],
        compiler_params=limit(16),
        name="prepare",
    )(
        *[
            outside(x)
            for x in (
                velocity, jnp.swapaxes(w_mid, 3, 4), jnp.swapaxes(w_last, 2, 3),
                w_first, b_mid, b_first[None], b_last[None],
            )
        ],
    )
    across = swapped(packed, "chan", 2)
    up, down = halos(own, top, bottom, HALO)
    across, up, down = lax.optimization_barrier((across, up, down))
    beside = swapped(packed, "chan", 1)
    diagonal = swapped(across, "chan", 1)
    cot_full = lax.all_to_all(cot_all, "space", 0, 0, tiled=True)
    if h % 8:
        cot_full = cot_full.reshape(space * 2 * h, nx)

    deep = h + 2 * DEEP
    constants = [outside(x) for x in tables(h, space, nx)]
    places = [inside(x.shape[1:] if k == 3 else x.shape, f32) for k, x in enumerate(constants)]
    prov, vel_grad, keep, send, *constants = pl.pallas_call(
        functools.partial(step_kernel, h),
        out_shape=[inside((space, 2, h, nx), bf16), shape((2, h, nx), f32)]
        + [inside((2, SUMROWS, 128), bf16)] * 2
        + places,
        in_specs=vmem(9) + [pl.BlockSpec(memory_space=pl.ANY)] * 7,
        out_specs=vmem(11),
        scratch_shapes=[
            inside((2, rows, nx), f32),
            inside((nx // 128, rows * 8, 128), f32),
            inside((2, h + 4, nx), f32),
            inside(((h + 4) * 32, nx), f32),
            inside((NL + 1, deep, C, nx), bf16),
            inside((NL + 1, deep, C, nx), f32),
            inside((NL * 3, C, KW), bf16),
            inside((3, 32, KW), bf16),
            inside((C, KW), bf16),
            inside((3, 32, KW), f32),
            inside((h + 14, 32, nx), bf16),
        ]
        + [inside((h + 2 * l, C, nx), bf16) for l in range(6, 0, -1)]
        + [
            inside((nx // 128, (h + 2 * GPH) * 8, 128), f32),
            inside((2, h + 2 * GPH, nx), f32),
            inside((7, 192, KW), f32),
            inside((2, h + 2 * GPH, nx), f32),
            inside((nx // 128, h * 8, 128), f32),
        ]
        + [pltpu.SemaphoreType.DMA((7,))],
        compiler_params=limit(50),
        cost_estimate=pl.CostEstimate(
            flops=6 * 7 * deep * nx * 9 * C * C, bytes_accessed=2**25, transcendentals=6 * deep * nx * C
        ),
        name="step",
    )(own, up, down, packed, beside, across, diagonal, outside(offsets), cot_full, *constants)
    everywhere = lax.all_to_all(prov, "space", 0, 0, tiled=True)
    if h % 8:
        everywhere = everywhere.reshape(space * 2 * h, nx)

    new_own = pl.pallas_call(
        functools.partial(project_kernel, h),
        out_shape=inside((2 * h + 8, nx), f32),
        in_specs=vmem(8),
        out_specs=vmem(1)[0],
        compiler_params=limit(16),
        cost_estimate=pl.CostEstimate(flops=2**31, bytes_accessed=2**22, transcendentals=0),
        name="project",
    )(everywhere, *constants)

    pair = (keep.astype(f32) + swapped(send, "chan", 1).astype(f32)).astype(bf16)
    low = (pair[0].astype(f32) + swapped(pair[1], "chan", 2).astype(f32)).astype(bf16)
    bit = 1
    while 2 * bit < space:
        low = (low.astype(f32) + swapped(low, "space", bit).astype(f32)).astype(bf16)
        bit *= 2
    low, _ = lax.optimization_barrier((low, new_own))
    new_across = swapped(new_own, "chan", 2)
    other = swapped(low, "space", bit)
    news = [new_own, swapped(new_own, "chan", 1), new_across, swapped(new_across, "chan", 1)]

    new_velocity, w_first_grad, b_first_grad, w_mid_grad, b_mid_grad, w_last_grad, b_last_grad, rms_stats = pl.pallas_call(
        functools.partial(finish_kernel, h, 2 * traj * ny * nx),
        out_shape=[
            shape((2, traj, h, nx), f32),
            shape((3, 3, 2, 16), f32),
            shape((1, 16), f32),
            shape((NL, 3, 3, 16, C), f32),
            shape((NL, 16), f32),
            shape((3, 3, 8, C), f32),
            shape((1, 8), f32),
            shape((1, 4), f32),
        ],
        in_specs=vmem(6),
        out_specs=vmem(8),
        scratch_shapes=[pltpu.VMEM((4, 8, KW), f32)],
        compiler_params=limit(16),
        name="finish",
    )(low, other, *news)
    return (
        new_velocity,
        vel_grad[:, None],
        w_first_grad,
        b_first_grad[0],
        jnp.swapaxes(w_mid_grad, 3, 4),
        b_mid_grad,
        jnp.swapaxes(w_last_grad, 2, 3),
        b_last_grad[0],
        rms_stats[0],
    )


def solution(mesh):
    return jax.shard_map(
        per_device,
        mesh=mesh,
        in_specs=(
            P(None, None, "space", None),
            P(None, None, None, "chan"),
            P("chan"),
            P(None, None, None, None, "chan"),
            P(None, "chan"),
            P(None, None, None, "chan"),
            P("chan"),
            P(),
            P(None, None, "space", None),
        ),
        out_specs=(
            P(None, None, "space", None),
            P(None, "chan", "space", None),
            P(None, None, None, "chan"),
            P("chan"),
            P(None, None, None, None, "chan"),
            P(None, "chan"),
            P(None, None, None, "chan"),
            P("chan"),
            P(),
        ),
        check_vma=False,
    )
```

```python
import functools

import jax
import jax.numpy as jnp
import numpy as np
from jax import lax
from jax.experimental import pallas as pl
from jax.experimental.pallas import tpu as pltpu
from jax.sharding import PartitionSpec as P

f32 = jnp.float32
bf16 = jnp.bfloat16
highest = lax.Precision.HIGHEST
time_step = 0.2
viscosity = 0.256
HALO = 16
DEEP = 12
GPH = 8
C = 64
NL = 5
KW = 256
MIDROWS = NL * 3 * 16
TAILS = MIDROWS
LAST = TAILS + 128
FIRST = LAST + 48
SUMROWS = FIRST + 16
A0 = 0.7978845608028654
A1 = 0.044715 * A0


def basis(length):
    half = length // 2
    pos = np.arange(length)[:, None]
    table = np.zeros((length, length))
    m = np.arange(half + 1)[None, :]
    table[:, : half + 1] = np.cos(2 * np.pi * ((pos * m) % length) / length) * np.sqrt(2.0 / length)
    table[:, 0] = np.sqrt(1.0 / length)
    table[:, half] = np.cos(np.pi * pos[:, 0]) * np.sqrt(1.0 / length)
    m = np.arange(1, half)[None, :]
    table[:, half + 1 :] = np.sin(2 * np.pi * ((pos * m) % length) / length) * np.sqrt(2.0 / length)
    return table


def multipliers(ny, nx):
    def modes(n):
        half = n // 2
        index = np.arange(n)
        wave = np.where(index <= half, index, index - half) * (2 * np.pi / n)
        return wave, index <= half

    ky, cy = modes(ny)
    kx, cx = modes(nx)
    ky, cy = ky[:, None], cy[:, None]
    kx, cx = kx[None, :], cx[None, :]
    sq = kx * kx + ky * ky
    inv = np.where(sq > 0, 1.0 / np.where(sq > 0, sq, 1.0), 0.0)
    sign = np.where(cx == cy, 1.0, -1.0)
    edge_x = (kx == 0) | (kx >= np.pi - 1e-9)
    edge_y = (ky == 0) | (ky >= np.pi - 1e-9)
    mxy = np.where(edge_x | edge_y, 0.0, sign * kx * ky * inv)
    mxx = 1.0 - kx * kx * inv
    myy = 1.0 - ky * ky * inv
    return mxx, myy, mxy


def project_spectral(u, v, mxx, myy, mxy):
    half_y, half_x = u.shape[0] // 2, u.shape[1] // 2

    def swap(a):
        a = jnp.concatenate([a[:, half_x:], a[:, :half_x]], axis=1)
        return jnp.concatenate([a[half_y:], a[:half_y]], axis=0)

    rows = lax.broadcasted_iota(jnp.int32, u.shape, 0)
    cols = lax.broadcasted_iota(jnp.int32, u.shape, 1)
    corner = jnp.where((rows == half_y) & (cols == half_x), -0.5, 0.0)
    return (
        mxx * u + mxy * swap(v) + corner * v,
        myy * v + mxy * swap(u) + corner * u,
    )


def halves(x):
    high = x.astype(bf16)
    return high, (x - high.astype(f32)).astype(bf16)


def product(a, b):
    def dot(x, y):
        return jnp.dot(x, y, preferred_element_type=f32)

    return dot(a[0], b[0]) + (dot(a[1], b[0]) + dot(a[0], b[1]))


def spectrum(h, field_ref, tx_ref, ty_ref):
    ny = field_ref.shape[0] * h if h % 8 == 0 else field_ref.shape[0] // 2
    if h % 8 == 0:
        fields = [field_ref[:, c].reshape(ny, KW) for c in range(2)]
        field = jnp.concatenate(fields, axis=0)
    else:
        field = field_ref[...]
    along = sum(
        jnp.dot(field, part, preferred_element_type=f32) for part in halves(tx_ref[...])[::-1]
    )
    table = halves(ty_ref[...])
    if h % 8 == 0:
        return [product(table, halves(along[c * ny : (c + 1) * ny])) for c in range(2)]
    out = product(table, halves(along))
    return out[:ny], out[ny:]


def project_back(trow, u, back_ref):
    back = halves(back_ref[...])
    return product(halves(product(trow, halves(u))), back)


def gelu(z):
    t = jnp.tanh(z * (A0 + A1 * (z * z)))
    return z * (0.5 * t + 0.5)


def gelu_slope(z):
    z2 = z * z
    t = jnp.tanh(z * (A0 + A1 * z2))
    return (0.5 * t + 0.5) + (z * (0.5 * A0 + 1.5 * A1 * z2)) * (1.0 - t * t)


def lroll(x, s):
    return pltpu.roll(x, s % x.shape[1], 1)


def shifts(x):
    return jnp.concatenate([lroll(x, 1), x, lroll(x, -1)], axis=0)


def unshifts(x):
    return jnp.concatenate([lroll(x, -1), x, lroll(x, 1)], axis=0)


def spread(ref, first, values):
    for k in range(ref.shape[0]):
        ref[k, pl.ds(first, values.shape[0], stride=8), :] = values[:, k * 128 : k * 128 + 128]


def collect(ref, first, count):
    planes = [ref[k, pl.ds(first, count, stride=8), :] for k in range(ref.shape[0])]
    return jnp.concatenate(planes, axis=1)


def rows_of(ref, first, count):
    at = pl.ds(first if isinstance(first, int) else pl.multiple_of(first, 8), count)
    return jnp.concatenate([ref[k, at, :] for k in range(ref.shape[0])], axis=1)


def put_rows(ref, first, values):
    at = pl.ds(
        first if isinstance(first, int) else pl.multiple_of(first, 8), values.shape[0]
    )
    for k in range(ref.shape[0]):
        ref[k, at, :] = values[:, k * 128 : k * 128 + 128]


def group4(s):
    i = lax.broadcasted_iota(jnp.int32, s.shape, 0)
    s = s + jnp.where(i % 2 == 0, pltpu.roll(s, 7, 0), pltpu.roll(s, 1, 0))
    return s + jnp.where((i // 2) % 2 == 0, pltpu.roll(s, 6, 0), pltpu.roll(s, 2, 0))


def point_order(offs):
    row = lax.broadcasted_iota(jnp.int32, (32, 16), 0)
    point = (row // 8) * 4 + row % 4
    comp = (row // 4) % 2
    parts = [
        jnp.where((comp == c) & (offs[c : c + 1, :] == point), 1.0, 0.0).astype(f32)
        for c in range(2)
    ]
    return jnp.concatenate(parts, axis=1)


def blocks(n, most=27):
    count = -(-n // most)
    return count, -(-n // count)


def step_kernel(
    h, vel_ref, up_ref, down_ref, w0, w1, w2, w3, perm_ref,
    cot_ref, *rest,
):
    held = rest[:7]
    (
    prov_ref, vel_grad_ref, keep_ref, send_ref,
    tx_ref, ty_ref, back_ref, trow_ref, mxx_ref, myy_ref, mxy_ref,
    vp_ref, vs_ref, face_ref, mix_ref, xb, zb, wk_ref, w7_ref, wf_ref, w7k,
    gz7, gz6, gz5, gz4, gz3, gz2, gz1, f8, adv_ref, acc_ref, gp_ref, near8, sems,
    ) = rest[7:]
    loads = [
        pltpu.make_async_copy(table.at[lax.axis_index("space")] if k == 3 else table, place, sems.at[k])
        for k, (table, place) in enumerate(
            zip(held, (tx_ref, ty_ref, back_ref, trow_ref, mxx_ref, myy_ref, mxy_ref))
        )
    ]
    for load in loads:
        load.start()
    rows = h + 2 * HALO
    me = lax.axis_index("chan")
    for k, piece in enumerate((w0, w1, w2, w3)):
        slot = jnp.bitwise_xor(me, k)
        at16 = pl.ds(pl.multiple_of(slot * 16, 16), 16)
        at8 = pl.ds(pl.multiple_of(slot * 8, 8), 8)
        for n in range(NL * 3):
            wk_ref[n, at16, :] = piece[n * 16 : n * 16 + 16]
        for j in range(3):
            block = piece[MIDROWS + j * 16 : MIDROWS + j * 16 + 16].astype(f32)
            w7k[j, at8, :] = block[0:8]
        wf_ref[at16, :] = piece[MIDROWS + 48 : MIDROWS + 64]
    perm = perm_ref[...]
    perm_low = perm.astype(bf16)
    for i in range(3):
        w7_ref[i] = jnp.dot(perm_low, w7k[i].astype(bf16), preferred_element_type=f32).astype(bf16)

    vp_ref[:, 0:HALO] = up_ref[...]
    vp_ref[:, HALO : HALO + h] = vel_ref[...]
    vp_ref[:, HALO + h :] = down_ref[...]
    for c in range(2):
        plane = vp_ref[c]
        for d in range(4):
            spread(vs_ref, c * 4 + d, lroll(plane, 1 - d))

    def vs_rows(y, n):
        return rows_of(vs_ref, (y + HALO) * 8, 8 * n)

    ones = jnp.ones((16, KW), bf16)

    wfirst = wf_ref[:, 0:32]
    n = h + 2 * (DEEP - 1)
    count, size = blocks(n, 60)

    def first_block(k, _):
        top = k * size - (DEEP - 1)
        for r in range(size):
            y = top + r
            x = jnp.concatenate([vs_rows(y - 1, 3), jnp.ones((8, KW), f32)], axis=0)
            z = jnp.dot(wfirst, x.astype(bf16), preferred_element_type=f32)
            zb[0, y + DEEP] = z
            xb[0, y + DEEP] = gelu(z).astype(bf16)
        return 0

    lax.fori_loop(0, count, first_block, 0)

    def rows_through(source, weight, width, first, n, most, done):
        count, size = blocks(n, most)

        def taps(row):
            x = jnp.concatenate([shifts(source(row)), ones], axis=0)
            o = jnp.dot(weight, x, preferred_element_type=f32)
            return [o[i * width : (i + 1) * width] for i in range(3)]

        def block(k, carry):
            p0, p1 = carry
            for r in range(size):
                row = first + k * size + r
                o = taps(row + 1)
                done(row, p1 + o[2])
                p0, p1 = o[0], p0 + o[1]
            return p0, p1

        before, here = taps(first - 1), taps(first)
        lax.fori_loop(0, count, block, (here[0], before[0] + here[1]))

    for l in range(1, NL + 1):

        def done(row, z, l=l):
            zb[l, row] = z
            xb[l, row] = gelu(z).astype(bf16)

        rows_through(
            lambda row, l=l: xb[l - 1, row],
            wk_ref[3 * (l - 1) : 3 * l].reshape(192, KW)[:, 0:208],
            C, 1 + l, h + 2 * (DEEP - 1 - l), 60, done,
        )

    row = lax.broadcasted_iota(jnp.int32, (32, KW), 0)
    point = (row // 8) * 4 + row % 4
    second = jnp.where((row // 4) % 2 == 0, 6, 9)
    base = jnp.where((point == 5) | (point == second), 0.5, 0.0).astype(f32)

    def mixed(row, s):
        y = row - DEEP
        mean = group4(s[0:8] + s[8:16] + s[16:24] + s[24:32]) * (1.0 / 16.0)
        mix = s - jnp.concatenate([mean] * 4, axis=0) + base
        mix_ref[pl.ds(pl.multiple_of((y + 2) * 32, 32), 32), :] = mix
        m = mix * vs_rows(y - 1, 4)
        m = group4(m[0:8] + m[8:16] + m[16:24] + m[24:32])
        put_rows(f8, (y + 2) * 8, m)

    rows_through(
        lambda row: xb[NL, row], w7_ref[...].reshape(96, KW)[:, 0:208], 32, DEEP - 2, h + 4, 18, mixed
    )
    for c in range(2):
        face_ref[c] = collect(f8, c * 4, h + 4)
    ue = face_ref[0, 2 : 2 + h]
    vn = face_ref[1, 2 : 2 + h]
    vn_south = face_ref[1, 1 : 1 + h]
    total = [jnp.sum(ue * ue) + jnp.sum(vn * vn)]
    own = update = 0.0
    for c in range(2):
        q = vp_ref[c, HALO : HALO + h]
        north = vp_ref[c, HALO + 1 : HALO + 1 + h]
        south = vp_ref[c, HALO - 1 : HALO - 1 + h]
        east, west = lroll(q, -1), lroll(q, 1)
        lap = east + west + north + south - 4.0 * q
        fx = ue * (q + east) * 0.5
        adv = fx - lroll(fx, 1) + vn * (q + north) * 0.5 - vn_south * (south + q) * 0.5
        new = q + time_step * (viscosity * lap - adv)
        for k in range(prov_ref.shape[0]):
            prov_ref[k, c] = new.astype(prov_ref.dtype)
        own = own + jnp.sum(q * q)
        update = update + jnp.sum((new - q) * (new - q))
    lane = lax.broadcasted_iota(jnp.int32, (8, KW), 1)
    squares = jnp.where(
        lane == 0, own, jnp.where(lane == 1, total[0], jnp.where(lane == 2, update, 0.0))
    )

    for load in loads:
        load.wait()

    n = h + 2 * GPH
    u, v = spectrum(h, cot_ref, tx_ref, ty_ref)
    u, v = project_spectral(u, v, mxx_ref[...], myy_ref[...], mxy_ref[...])
    trow = halves(trow_ref[...])
    gp_ref[0] = project_back(trow, u, back_ref)
    gp_ref[1] = project_back(trow, v, back_ref)

    m = n - 1
    fields = []
    gue = gvn = 0.0
    for c in range(2):
        g = -time_step * gp_ref[c, 0:m]
        g_north = -time_step * gp_ref[c, 1 : m + 1]
        q = vp_ref[c, HALO - GPH : HALO - GPH + m]
        q_north = vp_ref[c, HALO - GPH + 1 : HALO - GPH + 1 + m]
        gfx = g - lroll(g, -1)
        gfy = g - g_north
        gue = gue + gfx * (q + lroll(q, -1)) * 0.5
        gvn = gvn + gfy * (q + q_north) * 0.5
        adv_ref[c, 0:m] = gfy
        fields.append(gfx[GPH : GPH + h])
    for d in range(4):
        spread(f8, d, gue)
        spread(f8, 4 + d, gvn)
    ue = face_ref[0, 2 : 2 + h]
    vn = face_ref[1, 2 : 2 + h]
    vn_south = face_ref[1, 1 : 1 + h]
    for c in range(2):
        g = gp_ref[c, GPH : GPH + h]
        lap = (
            lroll(g, -1) + lroll(g, 1) + gp_ref[c, GPH + 1 : GPH + 1 + h]
            + gp_ref[c, GPH - 1 : GPH - 1 + h] - 4.0 * g
        )
        ex = fields[c] * ue
        ny = adv_ref[c, GPH : GPH + h] * vn
        sy = adv_ref[c, GPH - 1 : GPH - 1 + h] * vn_south
        vel_grad_ref[c] = g + time_step * viscosity * lap + 0.5 * (ex + lroll(ex, 1) + ny + sy)

    def f8_row(y):
        return rows_of(f8, (y + GPH) * 8, 8)

    def stencil_row(k, _):
        for r in range(2):
            y = 2 * k + r - 7
            face = f8_row(y)
            near = vs_rows(y - 1, 4)
            s = near[0:8] + near[8:16] + near[16:24] + near[24:32]
            mean = group4(s) * (1.0 / 16.0)
            gm = (near - jnp.concatenate([mean] * 4, axis=0)) * jnp.concatenate([face] * 4, axis=0)
            gz7[y + 7] = gm.astype(bf16)
        return 0

    lax.fori_loop(0, (h + 14) // 2, stencil_row, 0, unroll=4 if h >= 16 else 1)

    def wgrad(columns, inputs):
        return lax.dot_general(
            jnp.concatenate(columns, axis=1),
            jnp.concatenate(inputs, axis=1),
            (((1,), (1,)), ((), ())),
            preferred_element_type=f32,
        )

    gzs = {7: gz7, 6: gz6, 5: gz5, 4: gz4, 3: gz3, 2: gz2, 1: gz1}
    for l in range(7, 1, -1):
        source, target = gzs[l], gzs[l - 1]
        if l == 7:
            parts = [w7_ref[i][:, 0:192].astype(f32) for i in range(3)]
            width = 32
        else:
            parts = [wk_ref[3 * (l - 2) + i][:, 0:192].astype(f32) for i in range(3)]
            width = C
        weight = jnp.concatenate(
            [
                jnp.concatenate([p[:, j * C : (j + 1) * C].T for j in range(3)], axis=1)
                for p in parts
            ],
            axis=0,
        ).astype(bf16)
        p0 = p1 = None
        acc = None
        for ys in (range(-l, h // 2), range(h // 2, h + l)):
            columns = {y: unshifts(source[y + l]) for y in ys}
            for y in ys:
                o = jnp.dot(weight, columns[y], preferred_element_type=f32)
                if y >= 2 - l:
                    ga = p1 + o[0:64]
                    slope = gelu_slope(zb[l - 2, y - 1 + DEEP])
                    target[y - 1 + l - 1] = (ga * slope).astype(bf16)
                p1 = o[64:128] if p0 is None else p0 + o[64:128]
                p0 = o[128:192]
            own = [y for y in ys if 0 <= y < h]
            part = wgrad(
                [columns[y] for y in own],
                [
                    jnp.concatenate(
                        [xb[l - 2, y + DEEP - 1 : y + DEEP + 2].reshape(192, KW), ones], axis=0
                    )
                    for y in own
                ],
            )
            acc = part if acc is None else acc + part
        if l == 7:
            back = perm
            acc = jnp.concatenate(
                [
                    lax.dot_general(
                        back, acc[j * 32 : j * 32 + 32], (((0,), (0,)), ((), ())),
                        preferred_element_type=f32, precision=highest,
                    )
                    for j in range(3)
                ],
                axis=0,
            )
        acc_ref[l - 1, 0 : 3 * width, 0:208] = acc

    wfirst = wf_ref[:, 0:32].astype(f32).T.astype(bf16)
    source = gz1
    outs = {}
    for y in range(-1, h + 1):
        outs[y] = jnp.dot(wfirst[0:24], source[y + 1], preferred_element_type=f32)
    acc_ref[0, 0:64, 0:40] = wgrad(
        [source[y + 1] for y in range(h)],
        [
            jnp.concatenate(
                [vs_rows(y - 1, 3), jnp.ones((16, KW), f32)], axis=0
            ).astype(bf16)
            for y in range(h)
        ],
    )
    for y in range(h):
        total = outs[y + 1][0:8] + outs[y][8:16] + outs[y - 1][16:24]
        for k in range(4):
            at = y + 1 - k
            total = total + f8_row(at) * mix_ref[pl.ds((at + 2) * 32 + k * 8, 8), :]
        put_rows(near8, y * 8, total)
    for c in range(2):
        total = vel_grad_ref[c]
        for d in range(4):
            total = total + lroll(collect(near8, c * 4 + d, h), d - 1)
        vel_grad_ref[c] = total

    lane = lax.broadcasted_iota(jnp.int32, (16, 64), 1)
    for k, other in enumerate((0, 2, 1, 3)):
        slot = jnp.bitwise_xor(me, other)
        pack_ref = (keep_ref, send_ref)[k // 2]
        k = k % 2
        tails = []
        bias = jnp.zeros((16, 64), f32)
        for l in range(NL):
            for j in range(3):
                piece = acc_ref[l + 1, pl.ds(pl.multiple_of(j * 64 + slot * 16, 16), 16), :]
                at = (3 * l + j) * 16
                pack_ref[k, at : at + 16, :] = piece[:, 0:128].astype(bf16)
                tails.append(piece[:, 128:192])
                if j == 0:
                    bias = jnp.where(lane == l, jnp.broadcast_to(piece[:, 192:193], (16, 64)), bias)
        tails.append(bias)
        for n in range(8):
            at = TAILS + 16 * n
            pack_ref[k, at : at + 16, :] = jnp.concatenate(tails[2 * n : 2 * n + 2], axis=1).astype(bf16)
        last = [
            acc_ref[6, pl.ds(pl.multiple_of(j * 32 + slot * 8, 8), 8), :] for j in range(3)
        ]
        tails = [p[:, 128:192] for p in last]
        tails.append(jnp.broadcast_to(last[0][:, 192:193], (8, 64)))
        groups = [p[:, 0:128] for p in last]
        groups += [jnp.concatenate(tails[0:2], axis=1), jnp.concatenate(tails[2:4], axis=1)]
        groups.append(squares[:, 0:128])
        pack_ref[k, LAST:FIRST, :] = jnp.concatenate(groups, axis=0).astype(bf16)
        pack_ref[k, FIRST:SUMROWS, :] = acc_ref[
            0, pl.ds(pl.multiple_of(slot * 16, 16), 16), 0:128
        ].astype(bf16)


def project_kernel(h, prov_ref, tx_ref, ty_ref, back_ref, trow_ref, mxx_ref, myy_ref, mxy_ref, out_ref):
    trow = halves(trow_ref[GPH : GPH + h])
    u, v = spectrum(h, prov_ref, tx_ref, ty_ref)
    u, v = project_spectral(u, v, mxx_ref[...], myy_ref[...], mxy_ref[...])
    out_ref[0:h] = project_back(trow, u, back_ref)
    out_ref[h : 2 * h] = project_back(trow, v, back_ref)
    out_ref[2 * h :] = jnp.full((8, KW), jnp.sum(u * u) + jnp.sum(v * v), f32)


def prepare_kernel(h, vel_ref, wm_ref, wl_ref, wf_ref, bm_ref, bf_ref, bl_ref, offs_ref, pack_ref, own_ref, top_ref, bottom_ref, perm_ref, tall, wide):
    me = lax.axis_index("chan")
    own = vel_ref[:, me]
    own_ref[...] = own
    if h >= HALO:
        top_ref[...] = own[:, :HALO]
        bottom_ref[...] = own[:, h - HALO :]
    perm_ref[...] = point_order(offs_ref[...])
    wide[...] = jnp.zeros_like(wide)
    wide[0:NL, 0:16] = bm_ref[...].astype(f32)
    wide[NL : NL + 1, 0:16] = bf_ref[...].astype(f32)
    wide[NL + 1 : NL + 2, 0:8] = bl_ref[...].astype(f32)
    columns = wide[...].T

    def column(k, count, i):
        lane = lax.broadcasted_iota(jnp.int32, (count, 64), 1)
        here = jnp.broadcast_to(columns[0:count, k : k + 1], (count, 64))
        return jnp.where((lane == 0) & (i == 1), here, 0.0)

    for l in range(NL):
        for i in range(3):
            parts = [wm_ref[l, i, j] for j in range(3)] + [column(l, 16, i).astype(bf16)]
            at = (3 * l + i) * 16
            pack_ref[at : at + 16, :] = jnp.concatenate(parts, axis=1)
    for i in range(3):
        parts = [wl_ref[i, j].astype(f32) for j in range(3)] + [column(NL + 1, 8, i)]
        block = jnp.concatenate(parts, axis=1)
        at = MIDROWS + i * 16
        pack_ref[at : at + 16, :] = jnp.concatenate([block, jnp.zeros_like(block)], axis=0).astype(bf16)
    tall[...] = jnp.zeros_like(tall)
    for i in range(3):
        for j in range(3):
            taps = wf_ref[i, j].astype(f32)
            for c in range(2):
                at = i * 8 + c * 4 + j
                tall[at : at + 1, 0:16] = taps[c : c + 1]
    tall[24:25, 0:16] = bf_ref[...].astype(f32)
    first = tall[...].T[0:16]
    pack_ref[MIDROWS + 48 :, :] = jnp.concatenate([first, jnp.zeros_like(first)], axis=1).astype(bf16)


def finish_kernel(h, cells, low_ref, other_ref, n0, n1, n2, n3, new_ref, wf_ref, bf_ref, wm_ref, bm_ref, wl_ref, bl_ref, rms_ref, parts):
    me = lax.axis_index("chan")
    for k, piece in enumerate((n0, n1, n2, n3)):
        slot = jnp.bitwise_xor(me, k)
        new_ref[0, slot] = piece[0:h]
        new_ref[1, slot] = piece[h : 2 * h]
        parts[slot] = piece[2 * h :]

    def total(at, count):
        return low_ref[at : at + count, :].astype(f32) + other_ref[at : at + count, :].astype(f32)

    def turned(block):
        return jnp.concatenate([block, jnp.zeros((128 - block.shape[0], 128), f32)], axis=0).T

    for l in range(NL):
        for j in range(3):
            n = 3 * l + j
            block = total(n * 16, 16)
            tail = total(TAILS + (n // 2) * 16, 16)
            wm_ref[l, 0, j] = block[:, 0:64]
            wm_ref[l, 1, j] = block[:, 64:128]
            wm_ref[l, 2, j] = tail[:, 64 * (n % 2) : 64 * (n % 2) + 64]
    bm_ref[...] = turned(total(TAILS + 112, 16))[64 : 64 + NL, 0:16]
    tail = total(LAST, 48)
    for j in range(3):
        wl_ref[0, j] = tail[j * 8 : j * 8 + 8, 0:64]
        wl_ref[1, j] = tail[j * 8 : j * 8 + 8, 64:128]
    wl_ref[2, 0] = tail[24:32, 0:64]
    wl_ref[2, 1] = tail[24:32, 64:128]
    wl_ref[2, 2] = tail[32:40, 0:64]
    bl_ref[...] = turned(tail[32:40])[64:65, 0:8]
    first = turned(total(FIRST, 16))
    for i in range(3):
        for j in range(3):
            for c in range(2):
                at = i * 8 + c * 4 + j
                wf_ref[i, j, c : c + 1, :] = first[at : at + 1, 0:16]
    bf_ref[...] = first[24:25, 0:16]
    news = (parts[0] + parts[1]) + (parts[2] + parts[3])
    lane = lax.broadcasted_iota(jnp.int32, (8, 128), 1)
    sums = jnp.where(lane == 3, news[:, 0:128], tail[40:48])
    rms_ref[...] = jnp.sqrt(sums * (1.0 / cells))[0:1, 0:4]


def moved(x, axis, step):
    n = lax.axis_size(axis)
    return lax.ppermute(x, axis, [(i, (i + step) % n) for i in range(n)])


def swapped(x, axis, bit):
    n = lax.axis_size(axis)
    return lax.ppermute(x, axis, [(i, i ^ bit) for i in range(n)])


def halos(own, top, bottom, width):
    height = own.shape[1]
    if height >= width:
        return moved(bottom, "space", 1), moved(top, "space", -1)
    hops = -(-width // height)
    up = jnp.concatenate([moved(own, "space", k) for k in range(hops, 0, -1)], axis=1)
    down = jnp.concatenate([moved(own, "space", -k) for k in range(1, hops + 1)], axis=1)
    return up[:, up.shape[1] - width :], down[:, :width]


def tables(h, space, nx):
    ny = h * space
    ty, tx = basis(ny), basis(nx)

    def held(table):
        return jnp.asarray(np.ascontiguousarray(table).astype(np.float32))

    back_y = ty.T
    if h % 8:
        wide = np.zeros((2, ny, space, 2, h))
        for c in range(2):
            wide[c, :, :, c, :] = ty.T.reshape(ny, space, h)
        back_y = wide.reshape(2 * ny, 2 * ny)
    ring = (np.arange(space)[:, None] * h + np.arange(h + 2 * GPH)[None, :] - GPH) % ny
    spectral = [jnp.asarray(m.astype(np.float32)) for m in multipliers(ny, nx)]
    return [held(tx), held(back_y), held(tx.T), held(ty[ring])] + spectral


def vmem(count):
    return [pl.BlockSpec(memory_space=pltpu.VMEM)] * count


def per_device(velocity, w_first, b_first, w_mid, b_mid, w_last, b_last, offsets, cotangent):
    traj, h, nx = velocity.shape[1:]
    space = lax.axis_size("space")
    ny = h * space
    me_chan = lax.axis_index("chan")
    rows = h + 2 * HALO
    shape = jax.ShapeDtypeStruct
    inside = pltpu.VMEM

    def limit(mebibytes):
        return pltpu.CompilerParams(vmem_limit_bytes=mebibytes * 2**20)

    def outside(x):
        return pltpu.with_memory_space_constraint(x, pltpu.HBM)

    own_cot = lax.dynamic_index_in_dim(cotangent, me_chan, 1, keepdims=False).astype(bf16)
    cot_all = jnp.broadcast_to(own_cot[None], (space,) + own_cot.shape)
    packed, own, top, bottom, perm = pl.pallas_call(
        functools.partial(prepare_kernel, h),
        out_shape=[
            inside((MIDROWS + 64, KW), bf16),
            inside((2, h, nx), f32),
            inside((2, min(h, HALO), nx), f32),
            inside((2, min(h, HALO), nx), f32),
            inside((32, 32), f32),
        ],
        in_specs=vmem(8),
        out_specs=vmem(5),
        scratch_shapes=[pltpu.VMEM((128, 128), f32), pltpu.VMEM((8, 128), f32)],
        compiler_params=limit(16),
        name="prepare",
    )(
        *[
            outside(x)
            for x in (
                velocity, jnp.swapaxes(w_mid, 3, 4), jnp.swapaxes(w_last, 2, 3),
                w_first, b_mid, b_first[None], b_last[None], offsets,
            )
        ],
    )
    across = swapped(packed, "chan", 2)
    up, down = halos(own, top, bottom, HALO)
    across, up, down = lax.optimization_barrier((across, up, down))
    beside = swapped(packed, "chan", 1)
    diagonal = swapped(across, "chan", 1)
    cot_full = lax.all_to_all(cot_all, "space", 0, 0, tiled=True)
    if h % 8:
        cot_full = cot_full.reshape(space * 2 * h, nx)

    deep = h + 2 * DEEP
    constants = [outside(x) for x in tables(h, space, nx)]
    places = [inside(x.shape[1:] if k == 3 else x.shape, f32) for k, x in enumerate(constants)]
    prov, vel_grad, keep, send, *constants = pl.pallas_call(
        functools.partial(step_kernel, h),
        out_shape=[inside((space, 2, h, nx), bf16), inside((2, h, nx), f32)]
        + [inside((2, SUMROWS, 128), bf16)] * 2
        + places,
        in_specs=vmem(9) + [pl.BlockSpec(memory_space=pl.ANY)] * 7,
        out_specs=vmem(11),
        scratch_shapes=[
            inside((2, rows, nx), f32),
            inside((nx // 128, rows * 8, 128), f32),
            inside((2, h + 4, nx), f32),
            inside(((h + 4) * 32, nx), f32),
            inside((NL + 1, deep, C, nx), bf16),
            inside((NL + 1, deep, C, nx), f32),
            inside((NL * 3, C, KW), bf16),
            inside((3, 32, KW), bf16),
            inside((C, KW), bf16),
            inside((3, 32, KW), f32),
            inside((h + 14, 32, nx), bf16),
        ]
        + [inside((h + 2 * l, C, nx), bf16) for l in range(6, 0, -1)]
        + [
            inside((nx // 128, (h + 2 * GPH) * 8, 128), f32),
            inside((2, h + 2 * GPH, nx), f32),
            inside((7, 192, KW), f32),
            inside((2, h + 2 * GPH, nx), f32),
            inside((nx // 128, h * 8, 128), f32),
        ]
        + [pltpu.SemaphoreType.DMA((7,))],
        compiler_params=limit(50),
        cost_estimate=pl.CostEstimate(
            flops=6 * 7 * deep * nx * 9 * C * C, bytes_accessed=2**25, transcendentals=6 * deep * nx * C
        ),
        name="step",
    )(own, up, down, packed, beside, across, diagonal, perm, cot_full, *constants)
    everywhere = lax.all_to_all(prov, "space", 0, 0, tiled=True)
    if h % 8:
        everywhere = everywhere.reshape(space * 2 * h, nx)

    new_own = pl.pallas_call(
        functools.partial(project_kernel, h),
        out_shape=inside((2 * h + 8, nx), f32),
        in_specs=vmem(8),
        out_specs=vmem(1)[0],
        compiler_params=limit(16),
        cost_estimate=pl.CostEstimate(flops=2**31, bytes_accessed=2**22, transcendentals=0),
        name="project",
    )(everywhere, *constants)

    pair = (keep.astype(f32) + swapped(send, "chan", 1).astype(f32)).astype(bf16)
    low = (pair[0].astype(f32) + swapped(pair[1], "chan", 2).astype(f32)).astype(bf16)
    bit = 1
    while 2 * bit < space:
        low = (low.astype(f32) + swapped(low, "space", bit).astype(f32)).astype(bf16)
        bit *= 2
    low, _ = lax.optimization_barrier((low, new_own))
    new_across = swapped(new_own, "chan", 2)
    other = swapped(low, "space", bit)
    news = [new_own, swapped(new_own, "chan", 1), new_across, swapped(new_across, "chan", 1)]

    new_velocity, w_first_grad, b_first_grad, w_mid_grad, b_mid_grad, w_last_grad, b_last_grad, rms_stats = pl.pallas_call(
        functools.partial(finish_kernel, h, 2 * traj * ny * nx),
        out_shape=[
            shape((2, traj, h, nx), f32),
            shape((3, 3, 2, 16), f32),
            shape((1, 16), f32),
            shape((NL, 3, 3, 16, C), f32),
            shape((NL, 16), f32),
            shape((3, 3, 8, C), f32),
            shape((1, 8), f32),
            shape((1, 4), f32),
        ],
        in_specs=vmem(6),
        out_specs=vmem(8),
        scratch_shapes=[pltpu.VMEM((4, 8, KW), f32)],
        compiler_params=limit(16),
        name="finish",
    )(low, other, *news)
    return (
        new_velocity,
        vel_grad[:, None],
        w_first_grad,
        b_first_grad[0],
        jnp.swapaxes(w_mid_grad, 3, 4),
        b_mid_grad,
        jnp.swapaxes(w_last_grad, 2, 3),
        b_last_grad[0],
        rms_stats[0],
    )


def solution(mesh):
    return jax.shard_map(
        per_device,
        mesh=mesh,
        in_specs=(
            P(None, None, "space", None),
            P(None, None, None, "chan"),
            P("chan"),
            P(None, None, None, None, "chan"),
            P(None, "chan"),
            P(None, None, None, "chan"),
            P("chan"),
            P(),
            P(None, None, "space", None),
        ),
        out_specs=(
            P(None, None, "space", None),
            P(None, "chan", "space", None),
            P(None, None, None, "chan"),
            P("chan"),
            P(None, None, None, None, "chan"),
            P(None, "chan"),
            P(None, None, None, "chan"),
            P("chan"),
            P(),
        ),
        check_vma=False,
    )
```

```python
import functools

import jax
import jax.numpy as jnp
import numpy as np
from jax import lax
from jax.experimental import pallas as pl
from jax.experimental.pallas import tpu as pltpu
from jax.sharding import PartitionSpec as P

f32 = jnp.float32
bf16 = jnp.bfloat16
highest = lax.Precision.HIGHEST
time_step = 0.2
viscosity = 0.256
HALO = 16
DEEP = 12
GPH = 8
C = 64
NL = 5
KW = 256
MIDROWS = NL * 3 * 16
TAILS = MIDROWS
LAST = TAILS + 128
FIRST = LAST + 48
SUMROWS = FIRST + 16
A0 = 0.7978845608028654
A1 = 0.044715 * A0


def basis(length):
    half = length // 2
    pos = np.arange(length)[:, None]
    table = np.zeros((length, length))
    m = np.arange(half + 1)[None, :]
    table[:, : half + 1] = np.cos(2 * np.pi * ((pos * m) % length) / length) * np.sqrt(2.0 / length)
    table[:, 0] = np.sqrt(1.0 / length)
    table[:, half] = np.cos(np.pi * pos[:, 0]) * np.sqrt(1.0 / length)
    m = np.arange(1, half)[None, :]
    table[:, half + 1 :] = np.sin(2 * np.pi * ((pos * m) % length) / length) * np.sqrt(2.0 / length)
    return table


def multipliers(ny, nx):
    def modes(n):
        half = n // 2
        index = np.arange(n)
        wave = np.where(index <= half, index, index - half) * (2 * np.pi / n)
        return wave, index <= half

    ky, cy = modes(ny)
    kx, cx = modes(nx)
    ky, cy = ky[:, None], cy[:, None]
    kx, cx = kx[None, :], cx[None, :]
    sq = kx * kx + ky * ky
    inv = np.where(sq > 0, 1.0 / np.where(sq > 0, sq, 1.0), 0.0)
    sign = np.where(cx == cy, 1.0, -1.0)
    edge_x = (kx == 0) | (kx >= np.pi - 1e-9)
    edge_y = (ky == 0) | (ky >= np.pi - 1e-9)
    mxy = np.where(edge_x | edge_y, 0.0, sign * kx * ky * inv)
    mxx = 1.0 - kx * kx * inv
    myy = 1.0 - ky * ky * inv
    return mxx, myy, mxy


def project_spectral(u, v, mxx, myy, mxy):
    half_y, half_x = u.shape[0] // 2, u.shape[1] // 2

    def swap(a):
        a = jnp.concatenate([a[:, half_x:], a[:, :half_x]], axis=1)
        return jnp.concatenate([a[half_y:], a[:half_y]], axis=0)

    rows = lax.broadcasted_iota(jnp.int32, u.shape, 0)
    cols = lax.broadcasted_iota(jnp.int32, u.shape, 1)
    corner = jnp.where((rows == half_y) & (cols == half_x), -0.5, 0.0)
    return (
        mxx * u + mxy * swap(v) + corner * v,
        myy * v + mxy * swap(u) + corner * u,
    )


def halves(x):
    high = x.astype(bf16)
    return high, (x - high.astype(f32)).astype(bf16)


def product(a, b):
    def dot(x, y):
        return jnp.dot(x, y, preferred_element_type=f32)

    return dot(a[0], b[0]) + (dot(a[1], b[0]) + dot(a[0], b[1]))


def spectrum(h, field_ref, tx_ref, ty_ref):
    ny = field_ref.shape[0] * h if h % 8 == 0 else field_ref.shape[0] // 2
    if h % 8 == 0:
        fields = [field_ref[:, c].reshape(ny, KW) for c in range(2)]
        field = jnp.concatenate(fields, axis=0)
    else:
        field = field_ref[...]
    along = sum(
        jnp.dot(field, part, preferred_element_type=f32) for part in halves(tx_ref[...])[::-1]
    )
    table = halves(ty_ref[...])
    if h % 8 == 0:
        return [product(table, halves(along[c * ny : (c + 1) * ny])) for c in range(2)]
    out = product(table, halves(along))
    return out[:ny], out[ny:]


def project_back(trow, u, back_ref):
    back = halves(back_ref[...])
    return product(halves(product(trow, halves(u))), back)


def gelu(z):
    t = jnp.tanh(z * (A0 + A1 * (z * z)))
    return z * (0.5 * t + 0.5)


def gelu_slope(z):
    z2 = z * z
    t = jnp.tanh(z * (A0 + A1 * z2))
    return (0.5 * t + 0.5) + (z * (0.5 * A0 + 1.5 * A1 * z2)) * (1.0 - t * t)


def lroll(x, s):
    return pltpu.roll(x, s % x.shape[1], 1)


def shifts(x):
    return jnp.concatenate([lroll(x, 1), x, lroll(x, -1)], axis=0)


def unshifts(x):
    return jnp.concatenate([lroll(x, -1), x, lroll(x, 1)], axis=0)


def spread(ref, first, values):
    for k in range(ref.shape[0]):
        ref[k, pl.ds(first, values.shape[0], stride=8), :] = values[:, k * 128 : k * 128 + 128]


def collect(ref, first, count):
    planes = [ref[k, pl.ds(first, count, stride=8), :] for k in range(ref.shape[0])]
    return jnp.concatenate(planes, axis=1)


def rows_of(ref, first, count):
    at = pl.ds(first if isinstance(first, int) else pl.multiple_of(first, 8), count)
    return jnp.concatenate([ref[k, at, :] for k in range(ref.shape[0])], axis=1)


def put_rows(ref, first, values):
    at = pl.ds(
        first if isinstance(first, int) else pl.multiple_of(first, 8), values.shape[0]
    )
    for k in range(ref.shape[0]):
        ref[k, at, :] = values[:, k * 128 : k * 128 + 128]


def group4(s):
    i = lax.broadcasted_iota(jnp.int32, s.shape, 0)
    s = s + jnp.where(i % 2 == 0, pltpu.roll(s, 7, 0), pltpu.roll(s, 1, 0))
    return s + jnp.where((i // 2) % 2 == 0, pltpu.roll(s, 6, 0), pltpu.roll(s, 2, 0))


def point_order(offs):
    row = lax.broadcasted_iota(jnp.int32, (32, 16), 0)
    point = (row // 8) * 4 + row % 4
    comp = (row // 4) % 2
    parts = [
        jnp.where((comp == c) & (offs[c : c + 1, :] == point), 1.0, 0.0).astype(f32)
        for c in range(2)
    ]
    return jnp.concatenate(parts, axis=1)


def blocks(n, most=27):
    count = -(-n // most)
    return count, -(-n // count)


def step_kernel(
    h, vel_ref, up_ref, down_ref, w0, w1, w2, w3, perm_ref,
    cot_ref, *rest,
):
    held = rest[:7]
    (
    prov_ref, vel_grad_ref, keep_ref, send_ref,
    tx_ref, ty_ref, back_ref, trow_ref, mxx_ref, myy_ref, mxy_ref,
    vp_ref, vs_ref, face_ref, mix_ref, xb, zb, wk_ref, w7_ref, wf_ref, w7k,
    gz7, gz6, gz5, gz4, gz3, gz2, gz1, f8, adv_ref, acc_ref, gp_ref, near8, sems,
    ) = rest[7:]
    loads = [
        pltpu.make_async_copy(table.at[lax.axis_index("space")] if k == 3 else table, place, sems.at[k])
        for k, (table, place) in enumerate(
            zip(held, (tx_ref, ty_ref, back_ref, trow_ref, mxx_ref, myy_ref, mxy_ref))
        )
    ]
    for load in loads:
        load.start()
    rows = h + 2 * HALO
    me = lax.axis_index("chan")
    for k, piece in enumerate((w0, w1, w2, w3)):
        slot = jnp.bitwise_xor(me, k)
        at16 = pl.ds(pl.multiple_of(slot * 16, 16), 16)
        at8 = pl.ds(pl.multiple_of(slot * 8, 8), 8)
        for n in range(NL * 3):
            wk_ref[n, at16, :] = piece[n * 16 : n * 16 + 16]
        for j in range(3):
            block = piece[MIDROWS + j * 16 : MIDROWS + j * 16 + 16].astype(f32)
            w7k[j, at8, :] = block[0:8]
        wf_ref[at16, :] = piece[MIDROWS + 48 : MIDROWS + 64]
    perm = perm_ref[...]
    perm_low = perm.astype(bf16)
    for i in range(3):
        w7_ref[i] = jnp.dot(perm_low, w7k[i].astype(bf16), preferred_element_type=f32).astype(bf16)

    vp_ref[:, 0:HALO] = up_ref[...]
    vp_ref[:, HALO : HALO + h] = vel_ref[...]
    vp_ref[:, HALO + h :] = down_ref[...]
    for c in range(2):
        plane = vp_ref[c]
        for d in range(4):
            spread(vs_ref, c * 4 + d, lroll(plane, 1 - d))

    def vs_rows(y, n):
        return rows_of(vs_ref, (y + HALO) * 8, 8 * n)

    ones = jnp.ones((16, KW), bf16)

    wfirst = wf_ref[:, 0:32]
    n = h + 2 * (DEEP - 1)
    count, size = blocks(n, 60)

    def first_block(k, _):
        top = k * size - (DEEP - 1)
        for r in range(size):
            y = top + r
            x = jnp.concatenate([vs_rows(y - 1, 3), jnp.ones((8, KW), f32)], axis=0)
            z = jnp.dot(wfirst, x.astype(bf16), preferred_element_type=f32)
            zb[0, y + DEEP] = z
            xb[0, y + DEEP] = gelu(z).astype(bf16)
        return 0

    lax.fori_loop(0, count, first_block, 0)

    def rows_through(source, weight, width, first, n, most, done):
        count, size = blocks(n, most)

        def taps(row):
            x = jnp.concatenate([shifts(source(row)), ones], axis=0)
            o = jnp.dot(weight, x, preferred_element_type=f32)
            return [o[i * width : (i + 1) * width] for i in range(3)]

        def block(k, carry):
            p0, p1 = carry
            for r in range(size):
                row = first + k * size + r
                o = taps(row + 1)
                done(row, p1 + o[2])
                p0, p1 = o[0], p0 + o[1]
            return p0, p1

        before, here = taps(first - 1), taps(first)
        lax.fori_loop(0, count, block, (here[0], before[0] + here[1]))

    for l in range(1, NL + 1):

        def done(row, z, l=l):
            zb[l, row] = z
            xb[l, row] = gelu(z).astype(bf16)

        rows_through(
            lambda row, l=l: xb[l - 1, row],
            wk_ref[3 * (l - 1) : 3 * l].reshape(192, KW)[:, 0:208],
            C, 1 + l, h + 2 * (DEEP - 1 - l), 60, done,
        )

    row = lax.broadcasted_iota(jnp.int32, (32, KW), 0)
    point = (row // 8) * 4 + row % 4
    second = jnp.where((row // 4) % 2 == 0, 6, 9)
    base = jnp.where((point == 5) | (point == second), 0.5, 0.0).astype(f32)

    def mixed(row, s):
        y = row - DEEP
        mean = group4(s[0:8] + s[8:16] + s[16:24] + s[24:32]) * (1.0 / 16.0)
        mix = s - jnp.concatenate([mean] * 4, axis=0) + base
        mix_ref[pl.ds(pl.multiple_of((y + 2) * 32, 32), 32), :] = mix
        m = mix * vs_rows(y - 1, 4)
        m = group4(m[0:8] + m[8:16] + m[16:24] + m[24:32])
        put_rows(f8, (y + 2) * 8, m)

    rows_through(
        lambda row: xb[NL, row], w7_ref[...].reshape(96, KW)[:, 0:208], 32, DEEP - 2, h + 4, 18, mixed
    )
    for c in range(2):
        face_ref[c] = collect(f8, c * 4, h + 4)
    ue = face_ref[0, 2 : 2 + h]
    vn = face_ref[1, 2 : 2 + h]
    vn_south = face_ref[1, 1 : 1 + h]
    total = [jnp.sum(ue * ue) + jnp.sum(vn * vn)]
    own = update = 0.0
    for c in range(2):
        q = vp_ref[c, HALO : HALO + h]
        north = vp_ref[c, HALO + 1 : HALO + 1 + h]
        south = vp_ref[c, HALO - 1 : HALO - 1 + h]
        east, west = lroll(q, -1), lroll(q, 1)
        lap = east + west + north + south - 4.0 * q
        fx = ue * (q + east) * 0.5
        adv = fx - lroll(fx, 1) + vn * (q + north) * 0.5 - vn_south * (south + q) * 0.5
        new = q + time_step * (viscosity * lap - adv)
        for k in range(prov_ref.shape[0]):
            prov_ref[k, c] = new.astype(prov_ref.dtype)
        own = own + jnp.sum(q * q)
        update = update + jnp.sum((new - q) * (new - q))
    lane = lax.broadcasted_iota(jnp.int32, (8, KW), 1)
    squares = jnp.where(
        lane == 0, own, jnp.where(lane == 1, total[0], jnp.where(lane == 2, update, 0.0))
    )

    for load in loads:
        load.wait()

    n = h + 2 * GPH
    u, v = spectrum(h, cot_ref, tx_ref, ty_ref)
    u, v = project_spectral(u, v, mxx_ref[...], myy_ref[...], mxy_ref[...])
    trow = halves(trow_ref[...])
    gp_ref[0] = project_back(trow, u, back_ref)
    gp_ref[1] = project_back(trow, v, back_ref)

    m = n - 1
    fields = []
    gue = gvn = 0.0
    for c in range(2):
        g = -time_step * gp_ref[c, 0:m]
        g_north = -time_step * gp_ref[c, 1 : m + 1]
        q = vp_ref[c, HALO - GPH : HALO - GPH + m]
        q_north = vp_ref[c, HALO - GPH + 1 : HALO - GPH + 1 + m]
        gfx = g - lroll(g, -1)
        gfy = g - g_north
        gue = gue + gfx * (q + lroll(q, -1)) * 0.5
        gvn = gvn + gfy * (q + q_north) * 0.5
        adv_ref[c, 0:m] = gfy
        fields.append(gfx[GPH : GPH + h])
    for d in range(4):
        spread(f8, d, gue)
        spread(f8, 4 + d, gvn)
    ue = face_ref[0, 2 : 2 + h]
    vn = face_ref[1, 2 : 2 + h]
    vn_south = face_ref[1, 1 : 1 + h]
    for c in range(2):
        g = gp_ref[c, GPH : GPH + h]
        lap = (
            lroll(g, -1) + lroll(g, 1) + gp_ref[c, GPH + 1 : GPH + 1 + h]
            + gp_ref[c, GPH - 1 : GPH - 1 + h] - 4.0 * g
        )
        ex = fields[c] * ue
        ny = adv_ref[c, GPH : GPH + h] * vn
        sy = adv_ref[c, GPH - 1 : GPH - 1 + h] * vn_south
        vel_grad_ref[c] = g + time_step * viscosity * lap + 0.5 * (ex + lroll(ex, 1) + ny + sy)

    def f8_row(y):
        return rows_of(f8, (y + GPH) * 8, 8)

    def stencil_row(k, _):
        for r in range(2):
            y = 2 * k + r - 7
            face = f8_row(y)
            near = vs_rows(y - 1, 4)
            s = near[0:8] + near[8:16] + near[16:24] + near[24:32]
            mean = group4(s) * (1.0 / 16.0)
            gm = (near - jnp.concatenate([mean] * 4, axis=0)) * jnp.concatenate([face] * 4, axis=0)
            gz7[y + 7] = gm.astype(bf16)
        return 0

    lax.fori_loop(0, (h + 14) // 2, stencil_row, 0, unroll=4 if h >= 16 else 1)

    def wgrad(columns, inputs):
        return lax.dot_general(
            jnp.concatenate(columns, axis=1),
            jnp.concatenate(inputs, axis=1),
            (((1,), (1,)), ((), ())),
            preferred_element_type=f32,
        )

    gzs = {7: gz7, 6: gz6, 5: gz5, 4: gz4, 3: gz3, 2: gz2, 1: gz1}
    for l in range(7, 1, -1):
        source, target = gzs[l], gzs[l - 1]
        if l == 7:
            parts = [w7_ref[i][:, 0:192].astype(f32) for i in range(3)]
            width = 32
        else:
            parts = [wk_ref[3 * (l - 2) + i][:, 0:192].astype(f32) for i in range(3)]
            width = C
        weight = jnp.concatenate(
            [
                jnp.concatenate([p[:, j * C : (j + 1) * C].T for j in range(3)], axis=1)
                for p in parts
            ],
            axis=0,
        ).astype(bf16)
        p0 = p1 = None
        acc = None
        for ys in (range(-l, h // 2), range(h // 2, h + l)):
            columns = {y: unshifts(source[y + l]) for y in ys}
            for y in ys:
                o = jnp.dot(weight, columns[y], preferred_element_type=f32)
                if y >= 2 - l:
                    ga = p1 + o[0:64]
                    slope = gelu_slope(zb[l - 2, y - 1 + DEEP])
                    target[y - 1 + l - 1] = (ga * slope).astype(bf16)
                p1 = o[64:128] if p0 is None else p0 + o[64:128]
                p0 = o[128:192]
            own = [y for y in ys if 0 <= y < h]
            part = wgrad(
                [columns[y] for y in own],
                [
                    jnp.concatenate(
                        [xb[l - 2, y + DEEP - 1 : y + DEEP + 2].reshape(192, KW), ones], axis=0
                    )
                    for y in own
                ],
            )
            acc = part if acc is None else acc + part
        if l == 7:
            back = perm
            acc = jnp.concatenate(
                [
                    lax.dot_general(
                        back, acc[j * 32 : j * 32 + 32], (((0,), (0,)), ((), ())),
                        preferred_element_type=f32, precision=highest,
                    )
                    for j in range(3)
                ],
                axis=0,
            )
        acc_ref[l - 1, 0 : 3 * width, 0:208] = acc

    wfirst = wf_ref[:, 0:32].astype(f32).T.astype(bf16)
    source = gz1
    outs = {}
    for y in range(-1, h + 1):
        outs[y] = jnp.dot(wfirst[0:24], source[y + 1], preferred_element_type=f32)
    acc_ref[0, 0:64, 0:40] = wgrad(
        [source[y + 1] for y in range(h)],
        [
            jnp.concatenate(
                [vs_rows(y - 1, 3), jnp.ones((16, KW), f32)], axis=0
            ).astype(bf16)
            for y in range(h)
        ],
    )
    for y in range(h):
        total = outs[y + 1][0:8] + outs[y][8:16] + outs[y - 1][16:24]
        for k in range(4):
            at = y + 1 - k
            total = total + f8_row(at) * mix_ref[pl.ds((at + 2) * 32 + k * 8, 8), :]
        put_rows(near8, y * 8, total)
    for c in range(2):
        total = vel_grad_ref[c]
        for d in range(4):
            total = total + lroll(collect(near8, c * 4 + d, h), d - 1)
        vel_grad_ref[c] = total

    lane = lax.broadcasted_iota(jnp.int32, (16, 64), 1)
    for k, other in enumerate((0, 2, 1, 3)):
        slot = jnp.bitwise_xor(me, other)
        pack_ref = (keep_ref, send_ref)[k // 2]
        k = k % 2
        tails = []
        bias = jnp.zeros((16, 64), f32)
        for l in range(NL):
            for j in range(3):
                piece = acc_ref[l + 1, pl.ds(pl.multiple_of(j * 64 + slot * 16, 16), 16), :]
                at = (3 * l + j) * 16
                pack_ref[k, at : at + 16, :] = piece[:, 0:128].astype(bf16)
                tails.append(piece[:, 128:192])
                if j == 0:
                    bias = jnp.where(lane == l, jnp.broadcast_to(piece[:, 192:193], (16, 64)), bias)
        tails.append(bias)
        for n in range(8):
            at = TAILS + 16 * n
            pack_ref[k, at : at + 16, :] = jnp.concatenate(tails[2 * n : 2 * n + 2], axis=1).astype(bf16)
        last = [
            acc_ref[6, pl.ds(pl.multiple_of(j * 32 + slot * 8, 8), 8), :] for j in range(3)
        ]
        tails = [p[:, 128:192] for p in last]
        tails.append(jnp.broadcast_to(last[0][:, 192:193], (8, 64)))
        groups = [p[:, 0:128] for p in last]
        groups += [jnp.concatenate(tails[0:2], axis=1), jnp.concatenate(tails[2:4], axis=1)]
        groups.append(squares[:, 0:128])
        pack_ref[k, LAST:FIRST, :] = jnp.concatenate(groups, axis=0).astype(bf16)
        pack_ref[k, FIRST:SUMROWS, :] = acc_ref[
            0, pl.ds(pl.multiple_of(slot * 16, 16), 16), 0:128
        ].astype(bf16)


def project_kernel(h, prov_ref, tx_ref, ty_ref, back_ref, trow_ref, mxx_ref, myy_ref, mxy_ref, out_ref):
    trow = halves(trow_ref[GPH : GPH + h])
    u, v = spectrum(h, prov_ref, tx_ref, ty_ref)
    u, v = project_spectral(u, v, mxx_ref[...], myy_ref[...], mxy_ref[...])
    out_ref[0:h] = project_back(trow, u, back_ref)
    out_ref[h : 2 * h] = project_back(trow, v, back_ref)
    out_ref[2 * h :] = jnp.full((8, KW), jnp.sum(u * u) + jnp.sum(v * v), f32)


def prepare_kernel(h, vel_ref, wm_ref, wl_ref, wf_ref, bm_ref, bf_ref, bl_ref, offs_ref, pack_ref, own_ref, top_ref, bottom_ref, perm_ref, tall, wide):
    me = lax.axis_index("chan")
    own = vel_ref[:, me]
    own_ref[...] = own
    if h >= HALO:
        top_ref[...] = own[:, :HALO]
        bottom_ref[...] = own[:, h - HALO :]
    perm_ref[...] = point_order(offs_ref[...])
    wide[...] = jnp.zeros_like(wide)
    wide[0:NL, 0:16] = bm_ref[...].astype(f32)
    wide[NL : NL + 1, 0:16] = bf_ref[...].astype(f32)
    wide[NL + 1 : NL + 2, 0:8] = bl_ref[...].astype(f32)
    columns = wide[...].T

    def column(k, count, i):
        lane = lax.broadcasted_iota(jnp.int32, (count, 64), 1)
        here = jnp.broadcast_to(columns[0:count, k : k + 1], (count, 64))
        return jnp.where((lane == 0) & (i == 1), here, 0.0)

    for l in range(NL):
        for i in range(3):
            parts = [wm_ref[l, i, j] for j in range(3)] + [column(l, 16, i).astype(bf16)]
            at = (3 * l + i) * 16
            pack_ref[at : at + 16, :] = jnp.concatenate(parts, axis=1)
    for i in range(3):
        parts = [wl_ref[i, j].astype(f32) for j in range(3)] + [column(NL + 1, 8, i)]
        block = jnp.concatenate(parts, axis=1)
        at = MIDROWS + i * 16
        pack_ref[at : at + 16, :] = jnp.concatenate([block, jnp.zeros_like(block)], axis=0).astype(bf16)
    tall[...] = jnp.zeros_like(tall)
    for i in range(3):
        for j in range(3):
            taps = wf_ref[i, j].astype(f32)
            for c in range(2):
                at = i * 8 + c * 4 + j
                tall[at : at + 1, 0:16] = taps[c : c + 1]
    tall[24:25, 0:16] = bf_ref[...].astype(f32)
    first = tall[...].T[0:16]
    pack_ref[MIDROWS + 48 :, :] = jnp.concatenate([first, jnp.zeros_like(first)], axis=1).astype(bf16)


def finish_kernel(h, cells, low_ref, other_ref, n0, n1, n2, n3, new_ref, wf_ref, bf_ref, wm_ref, bm_ref, wl_ref, bl_ref, rms_ref, parts):
    me = lax.axis_index("chan")
    for k, piece in enumerate((n0, n1, n2, n3)):
        slot = jnp.bitwise_xor(me, k)
        new_ref[0, slot] = piece[0:h]
        new_ref[1, slot] = piece[h : 2 * h]
        parts[slot] = piece[2 * h :]

    def total(at, count):
        return low_ref[at : at + count, :].astype(f32) + other_ref[at : at + count, :].astype(f32)

    def turned(block):
        return jnp.concatenate([block, jnp.zeros((128 - block.shape[0], 128), f32)], axis=0).T

    for l in range(NL):
        for j in range(3):
            n = 3 * l + j
            block = total(n * 16, 16)
            tail = total(TAILS + (n // 2) * 16, 16)
            wm_ref[l, 0, j] = block[:, 0:64]
            wm_ref[l, 1, j] = block[:, 64:128]
            wm_ref[l, 2, j] = tail[:, 64 * (n % 2) : 64 * (n % 2) + 64]
    bm_ref[...] = turned(total(TAILS + 112, 16))[64 : 64 + NL, 0:16]
    tail = total(LAST, 48)
    for j in range(3):
        wl_ref[0, j] = tail[j * 8 : j * 8 + 8, 0:64]
        wl_ref[1, j] = tail[j * 8 : j * 8 + 8, 64:128]
    wl_ref[2, 0] = tail[24:32, 0:64]
    wl_ref[2, 1] = tail[24:32, 64:128]
    wl_ref[2, 2] = tail[32:40, 0:64]
    bl_ref[...] = turned(tail[32:40])[64:65, 0:8]
    first = turned(total(FIRST, 16))
    for i in range(3):
        for j in range(3):
            for c in range(2):
                at = i * 8 + c * 4 + j
                wf_ref[i, j, c : c + 1, :] = first[at : at + 1, 0:16]
    bf_ref[...] = first[24:25, 0:16]
    news = (parts[0] + parts[1]) + (parts[2] + parts[3])
    lane = lax.broadcasted_iota(jnp.int32, (8, 128), 1)
    sums = jnp.where(lane == 3, news[:, 0:128], tail[40:48])
    rms_ref[...] = jnp.sqrt(sums * (1.0 / cells))[0:1, 0:4]


def moved(x, axis, step):
    n = lax.axis_size(axis)
    return lax.ppermute(x, axis, [(i, (i + step) % n) for i in range(n)])


def swapped(x, axis, bit):
    n = lax.axis_size(axis)
    return lax.ppermute(x, axis, [(i, i ^ bit) for i in range(n)])


def halos(own, top, bottom, width):
    height = own.shape[1]
    if height >= width:
        return moved(bottom, "space", 1), moved(top, "space", -1)
    hops = -(-width // height)
    up = jnp.concatenate([moved(own, "space", k) for k in range(hops, 0, -1)], axis=1)
    down = jnp.concatenate([moved(own, "space", -k) for k in range(1, hops + 1)], axis=1)
    return up[:, up.shape[1] - width :], down[:, :width]


def tables(h, space, nx):
    ny = h * space
    ty, tx = basis(ny), basis(nx)

    def held(table):
        return jnp.asarray(np.ascontiguousarray(table).astype(np.float32))

    back_y = ty.T
    if h % 8:
        wide = np.zeros((2, ny, space, 2, h))
        for c in range(2):
            wide[c, :, :, c, :] = ty.T.reshape(ny, space, h)
        back_y = wide.reshape(2 * ny, 2 * ny)
    ring = (np.arange(space)[:, None] * h + np.arange(h + 2 * GPH)[None, :] - GPH) % ny
    spectral = [jnp.asarray(m.astype(np.float32)) for m in multipliers(ny, nx)]
    return [held(tx), held(back_y), held(tx.T), held(ty[ring])] + spectral


def vmem(count):
    return [pl.BlockSpec(memory_space=pltpu.VMEM)] * count


def per_device(velocity, w_first, b_first, w_mid, b_mid, w_last, b_last, offsets, cotangent):
    traj, h, nx = velocity.shape[1:]
    space = lax.axis_size("space")
    ny = h * space
    me_chan = lax.axis_index("chan")
    rows = h + 2 * HALO
    shape = jax.ShapeDtypeStruct
    inside = pltpu.VMEM

    def limit(mebibytes):
        return pltpu.CompilerParams(vmem_limit_bytes=mebibytes * 2**20)

    def outside(x):
        return pltpu.with_memory_space_constraint(x, pltpu.HBM)

    own_cot = lax.dynamic_index_in_dim(cotangent, me_chan, 1, keepdims=False).astype(bf16)
    cot_all = jnp.broadcast_to(own_cot[None], (space,) + own_cot.shape)
    packed, own, top, bottom, perm = pl.pallas_call(
        functools.partial(prepare_kernel, h),
        out_shape=[
            inside((MIDROWS + 64, KW), bf16),
            inside((2, h, nx), f32),
            inside((2, min(h, HALO), nx), f32),
            inside((2, min(h, HALO), nx), f32),
            inside((32, 32), f32),
        ],
        in_specs=vmem(8),
        out_specs=vmem(5),
        scratch_shapes=[pltpu.VMEM((128, 128), f32), pltpu.VMEM((8, 128), f32)],
        compiler_params=limit(16),
        name="prepare",
    )(
        *[
            outside(x)
            for x in (
                velocity, jnp.swapaxes(w_mid, 3, 4), jnp.swapaxes(w_last, 2, 3),
                w_first, b_mid, b_first[None], b_last[None], offsets,
            )
        ],
    )
    across = swapped(packed, "chan", 2)
    up, down = halos(own, top, bottom, HALO)
    beside = swapped(packed, "chan", 1)
    diagonal = swapped(packed, "chan", 3)
    cot_full = lax.all_to_all(cot_all, "space", 0, 0, tiled=True)
    if h % 8:
        cot_full = cot_full.reshape(space * 2 * h, nx)

    deep = h + 2 * DEEP
    constants = [outside(x) for x in tables(h, space, nx)]
    places = [inside(x.shape[1:] if k == 3 else x.shape, f32) for k, x in enumerate(constants)]
    prov, vel_grad, keep, send, *constants = pl.pallas_call(
        functools.partial(step_kernel, h),
        out_shape=[inside((space, 2, h, nx), bf16), inside((2, h, nx), f32)]
        + [inside((2, SUMROWS, 128), bf16)] * 2
        + places,
        in_specs=vmem(9) + [pl.BlockSpec(memory_space=pl.ANY)] * 7,
        out_specs=vmem(11),
        scratch_shapes=[
            inside((2, rows, nx), f32),
            inside((nx // 128, rows * 8, 128), f32),
            inside((2, h + 4, nx), f32),
            inside(((h + 4) * 32, nx), f32),
            inside((NL + 1, deep, C, nx), bf16),
            inside((NL + 1, deep, C, nx), f32),
            inside((NL * 3, C, KW), bf16),
            inside((3, 32, KW), bf16),
            inside((C, KW), bf16),
            inside((3, 32, KW), f32),
            inside((h + 14, 32, nx), bf16),
        ]
        + [inside((h + 2 * l, C, nx), bf16) for l in range(6, 0, -1)]
        + [
            inside((nx // 128, (h + 2 * GPH) * 8, 128), f32),
            inside((2, h + 2 * GPH, nx), f32),
            inside((7, 192, KW), f32),
            inside((2, h + 2 * GPH, nx), f32),
            inside((nx // 128, h * 8, 128), f32),
        ]
        + [pltpu.SemaphoreType.DMA((7,))],
        compiler_params=limit(50),
        cost_estimate=pl.CostEstimate(
            flops=6 * 7 * deep * nx * 9 * C * C, bytes_accessed=2**25, transcendentals=6 * deep * nx * C
        ),
        name="step",
    )(own, up, down, packed, beside, across, diagonal, perm, cot_full, *constants)
    everywhere = lax.all_to_all(prov, "space", 0, 0, tiled=True)
    if h % 8:
        everywhere = everywhere.reshape(space * 2 * h, nx)

    new_own = pl.pallas_call(
        functools.partial(project_kernel, h),
        out_shape=inside((2 * h + 8, nx), f32),
        in_specs=vmem(8),
        out_specs=vmem(1)[0],
        compiler_params=limit(16),
        cost_estimate=pl.CostEstimate(flops=2**31, bytes_accessed=2**22, transcendentals=0),
        name="project",
    )(everywhere, *constants)

    pair = (keep.astype(f32) + swapped(send, "chan", 1).astype(f32)).astype(bf16)
    low = (pair[0].astype(f32) + swapped(pair[1], "chan", 2).astype(f32)).astype(bf16)
    bit = 1
    while 2 * bit < space:
        low = (low.astype(f32) + swapped(low, "space", bit).astype(f32)).astype(bf16)
        bit *= 2
    low, _ = lax.optimization_barrier((low, new_own))
    new_across = swapped(new_own, "chan", 2)
    other = swapped(low, "space", bit)
    news = [new_own, swapped(new_own, "chan", 1), new_across, swapped(new_across, "chan", 1)]

    new_velocity, w_first_grad, b_first_grad, w_mid_grad, b_mid_grad, w_last_grad, b_last_grad, rms_stats = pl.pallas_call(
        functools.partial(finish_kernel, h, 2 * traj * ny * nx),
        out_shape=[
            shape((2, traj, h, nx), f32),
            shape((3, 3, 2, 16), f32),
            shape((1, 16), f32),
            shape((NL, 3, 3, 16, C), f32),
            shape((NL, 16), f32),
            shape((3, 3, 8, C), f32),
            shape((1, 8), f32),
            shape((1, 4), f32),
        ],
        in_specs=vmem(6),
        out_specs=vmem(8),
        scratch_shapes=[pltpu.VMEM((4, 8, KW), f32)],
        compiler_params=limit(16),
        name="finish",
    )(low, other, *news)
    return (
        new_velocity,
        vel_grad[:, None],
        w_first_grad,
        b_first_grad[0],
        jnp.swapaxes(w_mid_grad, 3, 4),
        b_mid_grad,
        jnp.swapaxes(w_last_grad, 2, 3),
        b_last_grad[0],
        rms_stats[0],
    )


def solution(mesh):
    return jax.shard_map(
        per_device,
        mesh=mesh,
        in_specs=(
            P(None, None, "space", None),
            P(None, None, None, "chan"),
            P("chan"),
            P(None, None, None, None, "chan"),
            P(None, "chan"),
            P(None, None, None, "chan"),
            P("chan"),
            P(),
            P(None, None, "space", None),
        ),
        out_specs=(
            P(None, None, "space", None),
            P(None, "chan", "space", None),
            P(None, None, None, "chan"),
            P("chan"),
            P(None, None, None, None, "chan"),
            P(None, "chan"),
            P(None, None, None, "chan"),
            P("chan"),
            P(),
        ),
        check_vma=False,
    )
```
